32 devices in a mesh: groups: 2 (over y), image: 16 (over z, x, core).
Axes of the slice: x: 2, y: 2, z: 4, core: 2. Of those that a mesh axis runs over, the one named last changes fastest.
Arguments:
- vision: bfloat16 [32, 256, 8192], P(('groups', 'image')), parts along dimension 0, may hold values from -6 to 6
- queries: bfloat16 [32, 4096], P(('groups', 'image')), parts along dimension 0, may hold values from -480 to 480
- text_request: int32 [32], P(('groups', 'image')), parts along dimension 0, may hold values from 0 to 7, never falling along the last dimension, each value on 1 to 4 neighbouring positions
- key_weight: bfloat16 [8192, 512], P('image'), may hold values from -0.0625 to 0.0625
- value_weight: bfloat16 [8192, 512], P('image'), may hold values from -0.0625 to 0.0625
- key_gain: float32 [128], replicated, may hold values from 0.25 to 1.75
- down_pages: bfloat16 [8192, 256], P('image'), may hold values from -0.0625 to 0.0625
- up_pages: bfloat16 [16, 16, 512], replicated, may hold values from -1.5 to 1.5
- image_request: int32 [32, 1], P(('groups', 'image')), parts along dimension 0, may hold values from 0 to 7
- image_tiles: int32 [32], P(('groups', 'image')), parts along dimension 0, may hold values from 1 to 4
- request_tenant: int32 [16], P('groups'), parts along dimension 0, may hold values from 0 to 15
- tenant_page: int32 [16], replicated, may hold values from 0 to 15, each once
Outputs:
- attended: bfloat16 [32, 4096], P(('groups', 'image')), parts along dimension 0
The draws below stay inside these ranges and needn't reach their ends.
There are 2 independent parts, one for each index of `groups`. The reference program is written for one: setup_inputs(seed, part) draws one part's arguments, and reference() takes and returns one part's arrays. A program takes and returns all parts, laid end to end along the dimension named above; an argument that names none is the same for every part. Nothing has to cross between parts.
Inputs may be any that keep to these rules, and one draw needn't show every extreme that they name: `text_request`: each request's text tokens are consecutive, 1 to 4 of them, requests in increasing order. `image_request`: every request owns at least one image. `tenant_page`: each page once.
All inputs are finite; a program needn't handle non-finite values.
Results may differ from the reference program's by a relative error of at most 0.012.
The reference program's roundings to bfloat16 on the way (of `lowrank`, `value_block`, `key_block` and `weights`) count: a program that leaves them out, or rounds other values in their place, can miss the bound.
Values may be sent and summed in bfloat16 or wider, within the bound.
No kernel may reach another device: no remote copies, remote signals or barrier semaphores. Data moves between devices by JAX's collectives and lax.ppermute only.
A program may use at most 128 MiB of HBM per device.

```python
import math
import jax
import jax.numpy as jnp
import numpy as np
from jax import lax

D = 8192
HEAD = 128
Q_HEADS = 32
KV_HEADS = 4
RANK = 16
TENANTS = 16
TILES = 4
V_DEV = 256
TXT_DEV = 1
IMAGES = 16
REQUESTS = 8
TEXT = 16
TILE_TOK = 64


def draw_queries(key, part):
    normal_part = 3.0 * jax.random.truncated_normal(key, -4.0, 4.0, (TEXT, Q_HEADS * HEAD), jnp.float32)
    return normal_part.astype(jnp.bfloat16)


def plant(entries, own_key, low, top_value):
    index_at = [jax.random.randint(jax.random.fold_in(own_key, axis), (), 0, length) for axis, length in enumerate(entries.shape)]
    widest = entries.shape.index(max(entries.shape))
    beside = index_at[:widest] + [(index_at[widest] + 1) % entries.shape[widest]] + index_at[widest + 1:]
    return entries.at[tuple(index_at)].set(low).at[tuple(beside)].set(top_value)


def steps_of(own_key, dims, pieces, smallest, top_value):
    level, own = 1.0, jax.random.fold_in(own_key, 6)
    for axis_at, blocks in pieces:
        draws = jnp.exp(jax.random.uniform(jax.random.fold_in(own, axis_at), (blocks,), jnp.float32, smallest / len(pieces), top_value / len(pieces)))
        level = level * jnp.repeat(draws, dims[axis_at] // blocks).reshape([-1 if axis == axis_at else 1 for axis in range(len(dims))])
    return level


def choose_distinct(own_key, rows, number_of, top, lift):
    order = jax.random.permutation(jax.random.fold_in(own_key, 1), number_of)
    favour = order
    for power in range(3):
        favour = favour * favour // number_of
    favour = favour * lift // number_of
    tickets = jax.random.randint(jax.random.fold_in(own_key, 2), (rows, number_of), 0, 4096) + favour
    holders = jax.random.permutation(jax.random.fold_in(own_key, 3), rows)[jnp.arange(number_of) % rows]
    tickets = jnp.where(jnp.arange(rows)[:, None] == holders[None, :], 1 << 14, tickets)
    priority = tickets * number_of + jnp.arange(number_of)
    return lax.top_k(priority.astype(jnp.int32), top)[1].astype(jnp.int32)


def length_profile(count, total, reach, lean):
    weights = [(1 << 20) // math.isqrt(grade ** lean) + 1 for grade in range(2, count + 1)]
    surplus, counts = total - reach - (count - 1), [1] * (count - 1)
    while surplus > 0:
        candidates = [i for i in range(count - 1) if counts[i] < reach]
        whole, budget = sum([weights[i] for i in candidates]), surplus
        for i in candidates:
            more = min(reach - counts[i], max(1, budget * weights[i] // whole), surplus)
            counts[i] = counts[i] + more
            surplus = surplus - more
    return np.array([reach] + counts)


def ragged(stream_key, count, total, limit, lean):
    if count == 2:
        one = jax.random.randint(stream_key, (), max(1, total - limit), min(limit, total - 1) + 1)
        return jnp.stack([one, total - one])
    sizes = jnp.asarray(length_profile(count, total, limit, lean), jnp.int32)
    pairs = (count - 1) // 2
    donor, taker = sizes[1:1 + 2 * pairs:2], sizes[2:2 + 2 * pairs:2]
    room = jnp.minimum(donor - 1, limit - taker)
    shifted = jax.random.randint(jax.random.fold_in(stream_key, 1), (pairs,), 0, 1 << 20) % (room + 1)
    sizes = sizes.at[1:1 + 2 * pairs:2].set(donor - shifted).at[2:2 + 2 * pairs:2].set(taker + shifted)
    return sizes[jax.random.permutation(jax.random.fold_in(stream_key, 2), count)]


def bell_draw(own_key, extent, width, bound, cuts=(), kind=jnp.bfloat16):
    values = jax.random.normal(own_key, extent, jnp.float32) * width
    if len(cuts) > 0:
        values = steps_of(own_key, extent, cuts, -0.22, 0.18) * values
    return jnp.clip(values, min=-bound, max=bound).astype(kind)


def setup_inputs(seed: int = 0, part: int = 0) -> dict:
    key_of = jax.random.split(jax.random.key(seed), 13)
    own_keys = jax.random.split(jax.random.fold_in(key_of[12], part), 13)
    vision = bell_draw(own_keys[0], (IMAGES, V_DEV, D), 1.0, 6.0, ((0, 16),))
    queries = draw_queries(jax.random.fold_in(jax.random.fold_in(key_of[12], part), 71), part)
    text_request = jnp.searchsorted(jnp.cumsum(ragged(own_keys[2], REQUESTS, TEXT, 4 * TXT_DEV, 2)), jnp.arange(TEXT), side="right").astype(jnp.int32)
    key_weight = bell_draw(key_of[3], (D, KV_HEADS * HEAD), D ** -0.5, 0.0625, ((0, 16),))
    value_weight = bell_draw(key_of[4], (D, KV_HEADS * HEAD), D ** -0.5, 0.0625, ((0, 16),))
    key_gain = jnp.clip(1.0 + 0.15 * jax.random.normal(key_of[5], (HEAD,), jnp.float32), 0.25, 1.75)
    down_pages = bell_draw(key_of[6], (D, TENANTS * RANK), D ** -0.5, 0.0625, ((0, 16),))
    up_pages = bell_draw(key_of[7], (TENANTS, RANK, KV_HEADS * HEAD), RANK ** -0.5, 1.5)
    image_request = choose_distinct(own_keys[8], IMAGES, REQUESTS, 1, 2048)
    image_tiles = plant(jax.random.randint(own_keys[9], (IMAGES,), 1, TILES + 1), jax.random.fold_in(own_keys[9], 1), 1, TILES).astype(jnp.int32)
    request_tenant = plant(jax.random.randint(own_keys[10], (REQUESTS,), 0, TENANTS), jax.random.fold_in(own_keys[10], 1), 0, TENANTS - 1).astype(jnp.int32)
    tenant_page = jax.random.permutation(key_of[11], TENANTS).astype(jnp.int32)
    return dict(vision=vision, queries=queries, text_request=text_request, key_weight=key_weight, value_weight=value_weight, key_gain=key_gain, down_pages=down_pages, up_pages=up_pages, image_request=image_request, image_tiles=image_tiles, request_tenant=request_tenant, tenant_page=tenant_page)


epsilon = 1e-05
masked_score = -1e+30

def project_image(image_tokens, key_weight, value_weight, down_factor, up_factor, key_gain):
    key_raw = jnp.dot(image_tokens, key_weight, preferred_element_type=jnp.float32)
    value_raw = jnp.dot(image_tokens, value_weight, preferred_element_type=jnp.float32)
    lowrank = jnp.dot(image_tokens, down_factor, preferred_element_type=jnp.float32).astype(jnp.bfloat16)
    value_block = (value_raw + jnp.dot(lowrank, up_factor, preferred_element_type=jnp.float32)).astype(jnp.bfloat16)
    key_heads = key_raw.reshape(V_DEV, KV_HEADS, HEAD)
    inverse_rms = lax.rsqrt(lax.optimization_barrier(jnp.mean(key_heads * key_heads, axis=-1, keepdims=True)) + epsilon)
    key_block = (key_heads * inverse_rms * key_gain).reshape(V_DEV, KV_HEADS * HEAD).astype(jnp.bfloat16)
    return (key_block, value_block)

def usable_mask(text_request, owner_id, tile_count):
    positions = jnp.arange(V_DEV, dtype=jnp.int32)
    return (text_request[:, None] == owner_id) & (positions[None, :] < tile_count * TILE_TOK)

def score_block(query_heads, key_block, usable):
    key_heads = key_block.astype(jnp.float32).reshape(V_DEV, KV_HEADS, HEAD)
    scores = jnp.einsum('tkgd,vkd->tkgv', query_heads, key_heads) * HEAD ** (-0.5)
    return jnp.where(usable[:, None, None, :], scores, masked_score)

def reference(vision, queries, text_request, key_weight, value_weight, key_gain, down_pages, up_pages, image_request, image_tiles, request_tenant, tenant_page):
    head_group = Q_HEADS // KV_HEADS
    query_heads = queries.astype(jnp.float32).reshape(TEXT, KV_HEADS, head_group, HEAD)

    def first_pass(image_item):
        image_tokens, owner_row, tile_count = image_item
        owner_id = owner_row[0]
        page_id = tenant_page[request_tenant[owner_id]].astype(jnp.int32)
        down_factor = lax.dynamic_slice_in_dim(down_pages, (page_id * RANK).astype(jnp.int32), RANK, 1)
        up_factor = lax.dynamic_index_in_dim(up_pages, page_id, 0, keepdims=False)
        key_block, value_block = project_image(image_tokens, key_weight, value_weight, down_factor, up_factor, key_gain)
        scores = score_block(query_heads, key_block, usable_mask(text_request, owner_id, tile_count))
        return (key_block, value_block, lax.optimization_barrier(jnp.max(scores, axis=-1)))
    key_all, value_all, maxima = lax.map(first_pass, (vision, image_request, image_tiles))
    top_score = lax.optimization_barrier(jnp.max(maxima, axis=0))

    def second_pass(running, image_item):
        key_block, value_block, owner_row, tile_count = image_item
        usable = usable_mask(text_request, owner_row[0], tile_count)
        scores = score_block(query_heads, key_block, usable)
        weights = jnp.where(usable[:, None, None, :], jnp.exp(scores - top_score[..., None]), 0.0).astype(jnp.bfloat16)
        weights = weights.astype(jnp.float32)
        value_heads = value_block.astype(jnp.float32).reshape(V_DEV, KV_HEADS, HEAD)
        numerator = running[0] + jnp.einsum('tkgv,vkd->tkgd', weights, value_heads)
        totals = running[1] + lax.optimization_barrier(jnp.sum(weights, axis=-1))
        return ((numerator, totals), None)
    start_state = (jnp.zeros((TEXT, KV_HEADS, head_group, HEAD), jnp.float32), jnp.zeros((TEXT, KV_HEADS, head_group), jnp.float32))
    final_state, ignored = lax.scan(second_pass, start_state, (key_all, value_all, image_request, image_tiles))
    numerator, totals = final_state
    return (numerator / totals[..., None]).reshape(TEXT, Q_HEADS * HEAD).astype(jnp.bfloat16)
```

```python
import functools

import jax
import jax.numpy as jnp
from jax import lax
from jax.experimental import pallas as pl
from jax.experimental.pallas import tpu as pltpu
from jax.sharding import PartitionSpec as P

HEAD = 128
KV_HEADS = 4
TILES = 4


epsilon = 1e-05
masked_score = -1e30


def select_entry(table, position):
    matches = jnp.arange(table.shape[0], dtype=jnp.int32) == position
    return jnp.sum(jnp.where(matches, table, 0))


def local_gathered(
    vision,
    queries,
    text_request,
    key_weight,
    value_weight,
    key_gain,
    down_pages,
    up_pages,
    image_request,
    image_tiles,
    request_tenant,
    tenant_page,
):
    image_tokens = vision[0]
    key_count = image_tokens.shape[0]
    kv_width = key_weight.shape[1]
    low_rank = up_pages.shape[1]
    owner_id = image_request[0, 0]
    tenant_id = select_entry(request_tenant, owner_id)
    page_id = select_entry(tenant_page, tenant_id)

    def token_columns():
        return image_tokens

    pieces = (
        lax.all_gather(key_weight, "image", axis=0, tiled=True),
        lax.all_gather(value_weight, "image", axis=0, tiled=True),
    )
    columns = token_columns()
    key_raw = jnp.dot(columns, pieces[0], preferred_element_type=jnp.float32)
    value_raw = jnp.dot(columns, pieces[1], preferred_element_type=jnp.float32)
    columns = token_columns()
    lowrank_sum = jnp.dot(
        columns,
        lax.dynamic_slice_in_dim(
            lax.all_gather(down_pages, "image", axis=0, tiled=True), page_id * low_rank, low_rank, 1
        ),
        preferred_element_type=jnp.float32,
    )
    lowrank = lowrank_sum.astype(jnp.bfloat16)
    up_factor = lax.dynamic_index_in_dim(up_pages, page_id, 0, keepdims=False)
    value_block = (
        value_raw + jnp.dot(lowrank, up_factor, preferred_element_type=jnp.float32)
    ).astype(jnp.bfloat16)
    key_heads = key_raw.reshape(key_count, KV_HEADS, HEAD)
    inverse_rms = lax.rsqrt(jnp.mean(key_heads * key_heads, axis=-1, keepdims=True) + epsilon)
    key_block = (
        (key_heads * inverse_rms * key_gain).reshape(key_count, kv_width).astype(jnp.bfloat16)
    )
    every_query, every_request = (
        lax.all_gather(queries, "image", axis=0, tiled=True),
        lax.all_gather(text_request, "image", axis=0, tiled=True),
    )
    text_total = every_query.shape[0]
    own_count = queries.shape[0]
    window = min(4 * own_count, text_total)
    head_group = every_query.shape[1] // kv_width
    q_count = KV_HEADS * head_group
    first_token = jnp.sum((every_request < owner_id).astype(jnp.int32))
    first_token = jnp.minimum(first_token, text_total - window)
    window_query = lax.dynamic_slice_in_dim(every_query, first_token, window, 0)
    window_request = lax.dynamic_slice_in_dim(every_request, first_token, window, 0)
    query_heads = window_query.reshape(window, KV_HEADS, head_group, HEAD)
    positions = jnp.arange(key_count, dtype=jnp.int32)
    usable = (window_request[:, None] == owner_id) & (
        positions[None, :] < image_tiles[0] * (key_count // TILES)
    )
    scores = jnp.einsum(
        "tkgd,vkd->tkgv",
        query_heads,
        key_block.reshape(key_count, KV_HEADS, HEAD),
        preferred_element_type=jnp.float32,
    ) * HEAD ** (-0.5)
    scores = jnp.where(usable[:, None, None, :], scores, masked_score)
    window_max = jnp.max(scores, axis=-1).reshape(window, q_count)
    every_max = lax.dynamic_update_slice_in_dim(
        jnp.full((text_total, q_count), masked_score, jnp.float32), window_max, first_token, 0
    )
    top_score = lax.pmax(every_max, "image")
    window_top = lax.dynamic_slice_in_dim(top_score, first_token, window, 0).reshape(
        window, KV_HEADS, head_group
    )
    weights = jnp.where(
        usable[:, None, None, :], jnp.exp(scores - window_top[..., None]), 0.0
    ).astype(jnp.bfloat16)
    totals = jnp.sum(weights, axis=-1, dtype=jnp.float32).reshape(window, q_count)
    numerator = jnp.einsum(
        "tkgv,vkd->tkgd",
        weights,
        value_block.reshape(key_count, KV_HEADS, HEAD),
        preferred_element_type=jnp.float32,
    ).reshape(window, q_count * HEAD)
    my_first = lax.axis_index("image") * own_count
    own_tokens = my_first + jnp.arange(own_count, dtype=jnp.int32)
    window_slots = jnp.arange(window, dtype=jnp.int32)
    start_value = first_token.astype(jnp.float32).reshape(1)
    pieces = (
        lax.all_gather(numerator, "image", axis=0, tiled=True),
        lax.all_gather(totals, "image", axis=0, tiled=True),
        lax.all_gather(start_value, "image", axis=0, tiled=True),
    )
    piece_count = pieces[2].shape[0]
    starts = pieces[2].astype(jnp.int32)
    offsets = own_tokens[None, :] - starts[:, None]
    chooser = (window_slots[None, None, :] == offsets[:, :, None]).astype(jnp.float32)
    numer_piece = pieces[0].reshape(piece_count, window, -1)
    totals_piece = pieces[1].reshape(piece_count, window, -1)
    numer_own = jnp.einsum("jrw,jwc->rc", chooser, numer_piece, precision=lax.Precision.HIGHEST)
    totals_own = jnp.einsum("jrw,jwc->rc", chooser, totals_piece, precision=lax.Precision.HIGHEST)
    attended = numer_own.reshape(own_count, -1, HEAD) / totals_own[..., None]
    return attended.reshape(own_count, -1).astype(jnp.bfloat16)


CORES = 2
COLUMNS = 2
PLANE = CORES * COLUMNS
EXTRA = 16
WINDOW = 4
MESSAGE = 40


def after(value, *others):
    return lax.optimization_barrier((value,) + others)[0]


def whole(count, space=pltpu.VMEM):
    return [pl.BlockSpec(memory_space=space)] * count


def call(kernel, out_shape, in_specs, scratch=(), vmem=16, flops=0, moved=0):
    outs = out_shape if isinstance(out_shape, (list, tuple)) else [out_shape]
    specs = [pl.BlockSpec(memory_space=pltpu.VMEM)] * len(outs)
    return pl.pallas_call(
        kernel,
        out_shape=out_shape,
        in_specs=in_specs,
        out_specs=specs if isinstance(out_shape, (list, tuple)) else specs[0],
        scratch_shapes=list(scratch),
        compiler_params=pltpu.CompilerParams(vmem_limit_bytes=vmem * 2**20),
        cost_estimate=pl.CostEstimate(flops=flops, bytes_accessed=moved, transcendentals=0),
    )


def split_kernel(place_ref, vision_ref, out_ref):
    out_ref[...] = vision_ref[...]


def split_vision(vision, core, rows):
    keys, depth = vision.shape
    shards = depth // rows // CORES
    return pl.pallas_call(
        split_kernel,
        out_shape=jax.ShapeDtypeStruct((keys, shards * rows), vision.dtype),
        grid_spec=pltpu.PrefetchScalarGridSpec(
            num_scalar_prefetch=1,
            grid=(shards,),
            in_specs=[pl.BlockSpec((keys, rows), lambda i, place: (0, CORES * i + 1 - place[0]))],
            out_specs=pl.BlockSpec((keys, rows), lambda i, place: (0, i)),
        ),
        cost_estimate=pl.CostEstimate(flops=0, bytes_accessed=keys * depth * 2, transcendentals=0),
    )(core.reshape(1), vision)


def prepare_kernel(half, place_ref, text_ref, image_ref, tenant_ref, page_ref, queries_ref, key_ref, out_ref):
    start = pl.multiple_of(place_ref[0] * half, half)
    out_ref[0:half, :] = key_ref[pl.ds(start, half), :]
    width = key_ref.shape[1]
    owner = image_ref[0, 0]
    page = page_ref[tenant_ref[owner]]
    row = lax.broadcasted_iota(jnp.int32, (EXTRA, width), 0)
    lane = lax.broadcasted_iota(jnp.int32, (EXTRA, width), 1)
    block = jnp.zeros((EXTRA, width), jnp.float32)
    for r in range(queries_ref.shape[1] // width):
        piece = queries_ref[0:1, r * width : (r + 1) * width].astype(jnp.float32)
        block = jnp.where(row == r, piece, block)
    for at, number in enumerate((text_ref[0], owner, page)):
        block = jnp.where((row == 8) & (lane == at), number.astype(jnp.float32), block)
    out_ref[half : half + EXTRA, :] = block.astype(out_ref.dtype)


def project_kernel(pieces, arrays, half, adds, *refs):
    cols_ref, vision_ref, other_ref = refs[:3]
    weight_refs = refs[3 : 3 + arrays]
    before = refs[3 + arrays : 3 + arrays + adds]
    own_ref, send_ref, slots, sems = refs[3 + arrays + adds :]
    keys = own_ref.shape[0]

    def copies(p):
        own_at = pl.multiple_of(cols_ref[0, p] * half, half)
        other_at = pl.multiple_of(cols_ref[1, p] * half, half)
        to = p * half
        return (
            pltpu.make_async_copy(
                vision_ref.at[:, pl.ds(own_at, half)], slots.at[0:keys, to : to + half], sems.at[0, p]
            ),
            pltpu.make_async_copy(
                other_ref.at[:, pl.ds(other_at, half)],
                slots.at[keys : 2 * keys, to : to + half],
                sems.at[1, p],
            ),
        )

    for p in range(len(pieces)):
        for one in copies(p):
            one.start()
    total = [None, None]
    for p, (which, row) in enumerate(pieces):
        for one in copies(p):
            one.wait()
        weight = weight_refs[which][row : row + half, :]
        for i in range(2):
            term = jnp.dot(
                slots[i * keys : (i + 1) * keys, p * half : (p + 1) * half],
                weight,
                preferred_element_type=jnp.float32,
            )
            if p == 0 and adds:
                total[i] = before[i][...] + term
            else:
                total[i] = term if total[i] is None else total[i] + term
    own_ref[...] = total[0]
    send_ref[...] = total[1]


def project(vision, other, arrays, pieces, cols, half, before=()):
    keys = vision.shape[0]
    width = arrays[0].shape[1]
    result = jax.ShapeDtypeStruct((keys, width), jnp.float32)
    count = len(pieces)
    return call(
        functools.partial(project_kernel, pieces, len(arrays), half, len(before)),
        [result, result],
        whole(1, pltpu.SMEM) + whole(2, pl.ANY) + whole(len(arrays) + len(before)),
        scratch=[
            pltpu.VMEM((2 * keys, count * half), vision.dtype),
            pltpu.SemaphoreType.DMA((2, count)),
        ],
        vmem=24,
        flops=4 * keys * half * width * count,
        moved=count * half * (2 * keys + width) * 2,
    )(cols, vision, other, *arrays, *before)


def slot_of(token, me, steps):
    z, x, core = token // PLANE, token // CORES % COLUMNS, token % CORES
    mz, mx, mcore = me // PLANE, me // CORES % COLUMNS, me % CORES
    d = lax.rem(z - mz + steps, steps)
    across = jnp.where(core == mcore, 0, 1) * COLUMNS + jnp.where(x == mx, 0, 1)
    return across * steps + d


def pick_kernel(total, steps, rank, place_ref, extras_ref, down_ref, out_ref, flat):
    me = place_ref[1]
    flat[...] = down_ref[...].T
    for dest in range(total):
        at = pl.multiple_of(slot_of(jnp.int32(dest), me, steps) * EXTRA, EXTRA)
        tile = extras_ref[pl.ds(at, EXTRA), 0:HEAD].astype(jnp.float32)
        page = tile[8, 2].astype(jnp.int32)
        out_ref[dest] = flat[pl.ds(pl.multiple_of(page * rank, rank), rank), :]


def lowrank_kernel(image_ref, tenant_ref, page_ref, vision_ref, down_ref, up_ref, out_ref):
    shards, rank, rows = down_ref.shape
    total = jnp.zeros((vision_ref.shape[0], rank), jnp.float32)
    for j in range(shards):
        total = total + lax.dot_general(
            vision_ref[:, j * rows : (j + 1) * rows],
            down_ref[j],
            (((1,), (1,)), ((), ())),
            preferred_element_type=jnp.float32,
        )
    page = page_ref[tenant_ref[image_ref[0, 0]]]
    out_ref[...] = jnp.dot(
        total.astype(jnp.bfloat16), up_ref[page], preferred_element_type=jnp.float32
    )


def window_start(extras_ref, owner, text_total):
    ids = extras_ref[:, 0:HEAD].astype(jnp.float32)
    row = lax.broadcasted_iota(jnp.int32, ids.shape, 0)
    lane = lax.broadcasted_iota(jnp.int32, ids.shape, 1)
    smaller = (row % EXTRA == 8) & (lane == 0) & (ids < owner.astype(jnp.float32))
    first = jnp.sum(jnp.where(smaller, 1.0, 0.0)).astype(jnp.int32)
    return jnp.minimum(first, text_total - WINDOW)


def select_rows(parts, rows):
    head = lax.broadcasted_iota(jnp.int32, parts[0].shape, 0) % 8 // 2
    result = parts[0]
    for k in range(1, KV_HEADS):
        result = jnp.where(head == k, parts[k], result)
    return result


def score_kernel(
    total, steps, place_ref, image_ref, tiles_ref, mine_ref, got_ref, gain_ref, extras_ref,
    weights_ref, stats_ref, state_ref,
):
    me, owner = place_ref[1], image_ref[0, 0]
    keys = mine_ref.shape[0]
    first = window_start(extras_ref, owner, total)
    tiles = []
    match = []
    for s in range(WINDOW):
        at = pl.multiple_of(slot_of(first + s, me, steps) * EXTRA, EXTRA)
        block = extras_ref[pl.ds(at, EXTRA), :].astype(jnp.float32)
        tiles += [block[0:8, k * HEAD : (k + 1) * HEAD] for k in range(KV_HEADS)]
        match.append(block[8, 0].astype(jnp.int32) == owner)
    query = jnp.concatenate(tiles, axis=0).astype(jnp.bfloat16)
    key_raw = mine_ref[...] + got_ref[...]
    gain = gain_ref[...]
    parts = []
    for k in range(KV_HEADS):
        head = key_raw[:, k * HEAD : (k + 1) * HEAD]
        scale = lax.rsqrt(jnp.mean(head * head, axis=1, keepdims=True) + epsilon)
        block = (head * scale * gain).astype(jnp.bfloat16)
        parts.append(
            lax.dot_general(query, block, (((1,), (1,)), ((), ())), preferred_element_type=jnp.float32)
        )
    scores = select_rows(parts, query.shape[0]) * HEAD ** (-0.5)
    row = lax.broadcasted_iota(jnp.int32, scores.shape, 0) // (8 * KV_HEADS)
    lane = lax.broadcasted_iota(jnp.int32, scores.shape, 1)
    limit = jnp.zeros(scores.shape, jnp.int32)
    slots = tiles_ref[0] * (keys // TILES)
    for s in range(WINDOW):
        limit = jnp.where(row == s, jnp.where(match[s], slots, 0), limit)
    usable = lane < limit
    scores = jnp.where(usable, scores, masked_score)
    top = jnp.max(scores, axis=1, keepdims=True)
    weights = jnp.where(usable, jnp.exp(scores - top), 0.0).astype(jnp.bfloat16)
    weights_ref[...] = weights
    sums = jnp.sum(weights.astype(jnp.float32), axis=1, keepdims=True)
    rows = 8 * KV_HEADS
    eye = lax.broadcasted_iota(jnp.int32, (rows, HEAD), 0) == lax.broadcasted_iota(jnp.int32, (rows, HEAD), 1)
    line = lax.broadcasted_iota(jnp.int32, (8, HEAD), 0)
    for s in range(WINDOW):
        own = slice(s * rows, (s + 1) * rows)
        top_row = jnp.sum(jnp.where(eye, top[own], 0.0), axis=0, keepdims=True)
        sum_row = jnp.sum(jnp.where(eye, sums[own], 0.0), axis=0, keepdims=True)
        stats_ref[s] = jnp.where(line == 0, top_row, jnp.where(line == 1, sum_row, 0.0))
        state_ref[1 + s] = match[s].astype(jnp.int32)
    state_ref[0] = first


def value_kernel(
    steps, place_ref, state_ref, mine_ref, got_ref, lowrank_ref, weights_ref, stats_ref, *refs
):
    out_refs, numerators = refs[:-1], refs[-1]
    me, first = place_ref[1], state_ref[0]
    value = (mine_ref[...] + got_ref[...] + lowrank_ref[...]).astype(jnp.bfloat16)
    weights = weights_ref[...]
    parts = [
        jnp.dot(weights, value[:, k * HEAD : (k + 1) * HEAD], preferred_element_type=jnp.float32)
        for k in range(KV_HEADS)
    ]
    result = select_rows(parts, weights.shape[0])
    rows = 8 * KV_HEADS
    for s in range(WINDOW):
        numerators[s, 0:rows, :] = result[s * rows : (s + 1) * rows]
        numerators[s, rows:MESSAGE, :] = stats_ref[s]
    line = lax.broadcasted_iota(jnp.int32, (MESSAGE, HEAD), 0)
    empty = jnp.where(line == rows, masked_score, 0.0)
    group = lax.rem(me, PLANE)
    for k, out_ref in enumerate(out_refs):
        core, x = lax.rem(group, CORES), group // CORES
        to = (x if k < CORES else 1 - x) * CORES + (core if k % CORES == 0 else 1 - core)
        for z in range(steps):
            s = z * PLANE + to - first
            inside = (s >= 0) & (s < WINDOW)
            s = jnp.clip(s, 0, WINDOW - 1)
            good = inside & (state_ref[1 + s] == 1)
            out_ref[z] = jnp.where(good, numerators[s], empty)


def merge(blocks):
    rows = 8 * KV_HEADS
    tops = [b[rows : rows + 1] for b in blocks]
    top = functools.reduce(jnp.maximum, tops)
    eye = lax.broadcasted_iota(jnp.int32, (rows, HEAD), 0) == lax.broadcasted_iota(jnp.int32, (rows, HEAD), 1)
    numerator, total = 0.0, 0.0
    for b, t in zip(blocks, tops):
        scale = jnp.exp(t - top)
        total = total + scale * b[rows + 1 : rows + 2]
        column = jnp.sum(jnp.where(eye, scale, 0.0), axis=1, keepdims=True)
        numerator = numerator + column * b[0:rows]
    return numerator, top, total, eye


def plane_kernel(steps, place_ref, *refs):
    in_refs, out_refs, merged = refs[:PLANE], refs[PLANE : PLANE + steps], refs[-1]
    rows = 8 * KV_HEADS
    line = lax.broadcasted_iota(jnp.int32, (8, HEAD), 0)
    for z in range(steps):
        numerator, top, total, _ = merge([ref[z] for ref in in_refs])
        merged[z, 0:rows, :] = numerator
        merged[z, rows:MESSAGE, :] = jnp.where(line == 0, top, jnp.where(line == 1, total, 0.0))
    for d, out_ref in enumerate(out_refs):
        out_ref[...] = merged[lax.rem(place_ref[1] // PLANE + d, steps)]


def final_kernel(*refs):
    out_ref = refs[-1]
    numerator, top, total, eye = merge([ref[...] for ref in refs[:-1]])
    column = jnp.sum(jnp.where(eye, total, 0.0), axis=1, keepdims=True)
    out = numerator / column
    for k in range(KV_HEADS):
        out_ref[:, k * HEAD : (k + 1) * HEAD] = out[8 * k : 8 * k + 8].astype(out_ref.dtype)


def local(
    devices,
    vision,
    queries,
    text_request,
    key_weight,
    value_weight,
    key_gain,
    down_pages,
    up_pages,
    image_request,
    image_tiles,
    request_tenant,
    tenant_page,
):
    steps = devices // PLANE
    me = lax.axis_index("image").astype(jnp.int32)
    y = lax.axis_index("groups").astype(jnp.int32)
    z, x, core = me // PLANE, me // CORES % COLUMNS, me % CORES
    tokens = vision[0]
    rows, width = key_weight.shape
    half = rows // 2
    rank = up_pages.shape[1]
    place = jnp.stack([y, me])
    everyone = range(devices)

    def across(value, bits):
        return lax.ppermute(value, "image", [(i, i ^ bits) for i in everyone])

    def along(value, d):
        return lax.ppermute(value, "image", [(i, (i - PLANE * d) % devices) for i in everyone])

    def swap(value):
        return lax.ppermute(value, "groups", [(0, 1), (1, 0)])

    def join(*arrays):
        return jnp.concatenate(arrays, axis=0)

    key_half = call(
        functools.partial(prepare_kernel, half),
        jax.ShapeDtypeStruct((half + EXTRA, width), key_weight.dtype),
        whole(5, pltpu.SMEM) + whole(2),
    )(place, text_request, image_request, request_tenant, tenant_page, queries, key_weight)
    value_half = lax.dynamic_slice_in_dim(value_weight, y * half, half, 0)
    extra = key_half[half:]

    k_own = across(key_weight, CORES)
    k1, k3 = along(key_half, 1), along(key_half, 3)
    k2 = along(after(key_half, k1, k3, k_own), 2)
    other = across(split_vision(tokens, core, rows), 1)
    kx = across(after(join(k1, k3, extra), k_own), CORES)
    ky = swap(after(join(k1[:half], k3[:half]), k_own))
    kx2 = across(k2, CORES)
    ky2 = swap(k2)
    v1, v3 = along(after(value_half, k2), 1), along(after(value_half, k2), 3)
    v_own = across(after(value_weight, kx, ky), CORES)
    kd = swap(after(join(kx[:half], kx[half + EXTRA : 2 * half + EXTRA]), ky))
    kd2 = swap(after(kx2, ky2))
    v2 = along(after(value_half, v1, v3, v_own, kd), 2)
    v_pair = join(v1, v3)
    vx = across(after(v_pair, kx2, v_own), CORES)
    vy = swap(after(v_pair, kd))
    vx2 = across(after(v2, v_own), CORES)
    vy2 = swap(after(v2, kd2))
    vd = swap(after(vx, vy))
    vd2 = across(after(vy2, vx), CORES)

    def columns(spots):
        own, other_at = [], []
        for d, mirrored, part in spots:
            pair = lax.rem(z + d, steps) * COLUMNS + (1 - x if mirrored else x)
            at = part if isinstance(part, int) else jnp.where(part == "near", y, 1 - y)
            at = {"near": y, "far": 1 - y}.get(part, part)
            own.append((pair * CORES + core) * 2 + at)
            other_at.append(pair * 2 + at)
        return jnp.stack([jnp.stack([jnp.int32(0) + v for v in own]), jnp.stack([jnp.int32(0) + v for v in other_at])])

    step = half + EXTRA
    spots = [
        (0, False, 0), (0, False, 1), (0, True, 0), (0, True, 1),
        (1, False, "near"), (3, False, "near"), (2, False, "near"),
        (1, True, "near"), (3, True, "near"), (2, True, "near"),
        (1, False, "far"), (3, False, "far"), (2, False, "far"),
        (1, True, "far"), (3, True, "far"), (2, True, "far"),
    ]
    cols = columns(spots)
    key_arrays = [key_weight, k_own, k1, k3, k2, kx, kx2, ky, ky2, kd, kd2]
    key_pieces = [
        (0, 0), (0, half), (1, 0), (1, half), (2, 0), (3, 0), (4, 0),
        (5, 0), (5, step), (6, 0), (7, 0), (7, half), (8, 0), (9, 0), (9, half), (10, 0),
    ]
    key_mine, key_send = project(tokens, other, key_arrays, tuple(key_pieces), cols, half)
    key_got = across(key_send, 1)

    near = join(extra, k1[half:], k2[half:], k3[half:], kx[2 * step :], kx[half:step], kx2[half:], kx[step + half : 2 * step])
    extras = join(near, across(near, 1))

    picked = call(
        functools.partial(pick_kernel, devices, steps, rank),
        jax.ShapeDtypeStruct((devices, rank, rows), down_pages.dtype),
        whole(1, pltpu.SMEM) + whole(2),
        scratch=[pltpu.VMEM(down_pages.shape[::-1], down_pages.dtype)],
    )(place, extras, down_pages)
    picked = lax.all_to_all(picked, "image", 0, 0, tiled=True)
    lowrank = call(
        lowrank_kernel,
        jax.ShapeDtypeStruct((tokens.shape[0], width), jnp.float32),
        whole(3, pltpu.SMEM) + whole(3),
        vmem=16,
        moved=tokens.size * 2,
    )(image_request, request_tenant, tenant_page, tokens, picked, up_pages)

    heads = WINDOW * 8 * KV_HEADS
    weights, stats, state = pl.pallas_call(
        functools.partial(score_kernel, devices, steps),
        out_shape=[
            jax.ShapeDtypeStruct((heads, tokens.shape[0]), jnp.bfloat16),
            jax.ShapeDtypeStruct((WINDOW, 8, HEAD), jnp.float32),
            jax.ShapeDtypeStruct((WINDOW + 1,), jnp.int32),
        ],
        in_specs=whole(3, pltpu.SMEM) + whole(4),
        out_specs=whole(2) + whole(1, pltpu.SMEM),
    )(place, image_request, image_tiles, key_mine, key_got, key_gain.reshape(1, HEAD), extras)

    value_arrays = [value_weight, v_own, v1, v3, v2, vx, vx2, vy]
    value_pieces = [
        (0, 0), (0, half), (1, 0), (1, half), (2, 0), (3, 0), (4, 0),
        (5, 0), (5, half), (6, 0), (7, 0), (7, half),
    ]
    early = project(tokens, other, value_arrays, tuple(value_pieces), cols[:, :12], half)
    value_mine, value_send = project(
        tokens, other, [vy2, vd, vd2], ((0, 0), (1, 0), (1, half), (2, 0)), cols[:, 12:], half, early
    )
    value_got = across(value_send, 1)

    message = jax.ShapeDtypeStruct((steps, MESSAGE, HEAD), jnp.float32)
    messages = call(
        functools.partial(value_kernel, steps),
        [message] * PLANE,
        whole(2, pltpu.SMEM) + whole(5),
        scratch=[pltpu.VMEM((WINDOW, MESSAGE, HEAD), jnp.float32)],
    )(place, state, value_mine, value_got, lowrank, weights, stats)
    arrived = [messages[0]] + [across(messages[k], k) for k in range(1, PLANE)]
    one = jax.ShapeDtypeStruct((MESSAGE, HEAD), jnp.float32)
    merged = call(
        functools.partial(plane_kernel, steps),
        [one] * steps,
        whole(1, pltpu.SMEM) + whole(PLANE),
        scratch=[pltpu.VMEM((steps, MESSAGE, HEAD), jnp.float32)],
    )(place, *arrived)
    arrived = [merged[0]] + [along(merged[d], steps - d) for d in range(1, steps)]
    out = call(
        final_kernel,
        jax.ShapeDtypeStruct((8, KV_HEADS * HEAD), jnp.bfloat16),
        whole(steps),
    )(*arrived)
    return out.reshape(queries.shape)


def fits(mesh, vision, queries, key_weight):
    devices = mesh.shape["image"]
    rows = key_weight.shape[0] // devices
    own = queries.shape[0] // (mesh.shape["groups"] * devices)
    one = vision.shape[0] == mesh.shape["groups"] * devices
    return rows % 256 == 0 and devices == 4 * PLANE and mesh.shape["groups"] == 2 and own == 1 and one


def solution(mesh):
    in_specs = (
        P(("groups", "image"), None, None),
        P(("groups", "image"), None),
        P(("groups", "image")),
        P("image", None),
        P("image", None),
        P(),
        P("image", None),
        P(),
        P(("groups", "image"), None),
        P(("groups", "image")),
        P("groups"),
        P(),
    )
    out_specs = P(("groups", "image"), None)

    def run(*args):
        if fits(mesh, args[0], args[1], args[3]):
            body = functools.partial(local, mesh.shape["image"])
        else:
            body = local_gathered
        return jax.shard_map(body, mesh=mesh, in_specs=in_specs, out_specs=out_specs, check_vma=False)(*args)

    return run
```

```python
import functools

import jax
import jax.numpy as jnp
from jax import lax
from jax.experimental import pallas as pl
from jax.experimental.pallas import tpu as pltpu
from jax.sharding import PartitionSpec as P

HEAD = 128
KV_HEADS = 4
TILES = 4


epsilon = 1e-05
masked_score = -1e30


def select_entry(table, position):
    matches = jnp.arange(table.shape[0], dtype=jnp.int32) == position
    return jnp.sum(jnp.where(matches, table, 0))


def local_gathered(
    vision,
    queries,
    text_request,
    key_weight,
    value_weight,
    key_gain,
    down_pages,
    up_pages,
    image_request,
    image_tiles,
    request_tenant,
    tenant_page,
):
    image_tokens = vision[0]
    key_count = image_tokens.shape[0]
    kv_width = key_weight.shape[1]
    low_rank = up_pages.shape[1]
    owner_id = image_request[0, 0]
    tenant_id = select_entry(request_tenant, owner_id)
    page_id = select_entry(tenant_page, tenant_id)

    def token_columns():
        return image_tokens

    pieces = (
        lax.all_gather(key_weight, "image", axis=0, tiled=True),
        lax.all_gather(value_weight, "image", axis=0, tiled=True),
    )
    columns = token_columns()
    key_raw = jnp.dot(columns, pieces[0], preferred_element_type=jnp.float32)
    value_raw = jnp.dot(columns, pieces[1], preferred_element_type=jnp.float32)
    columns = token_columns()
    lowrank_sum = jnp.dot(
        columns,
        lax.dynamic_slice_in_dim(
            lax.all_gather(down_pages, "image", axis=0, tiled=True), page_id * low_rank, low_rank, 1
        ),
        preferred_element_type=jnp.float32,
    )
    lowrank = lowrank_sum.astype(jnp.bfloat16)
    up_factor = lax.dynamic_index_in_dim(up_pages, page_id, 0, keepdims=False)
    value_block = (
        value_raw + jnp.dot(lowrank, up_factor, preferred_element_type=jnp.float32)
    ).astype(jnp.bfloat16)
    key_heads = key_raw.reshape(key_count, KV_HEADS, HEAD)
    inverse_rms = lax.rsqrt(jnp.mean(key_heads * key_heads, axis=-1, keepdims=True) + epsilon)
    key_block = (
        (key_heads * inverse_rms * key_gain).reshape(key_count, kv_width).astype(jnp.bfloat16)
    )
    every_query, every_request = (
        lax.all_gather(queries, "image", axis=0, tiled=True),
        lax.all_gather(text_request, "image", axis=0, tiled=True),
    )
    text_total = every_query.shape[0]
    own_count = queries.shape[0]
    window = min(4 * own_count, text_total)
    head_group = every_query.shape[1] // kv_width
    q_count = KV_HEADS * head_group
    first_token = jnp.sum((every_request < owner_id).astype(jnp.int32))
    first_token = jnp.minimum(first_token, text_total - window)
    window_query = lax.dynamic_slice_in_dim(every_query, first_token, window, 0)
    window_request = lax.dynamic_slice_in_dim(every_request, first_token, window, 0)
    query_heads = window_query.reshape(window, KV_HEADS, head_group, HEAD)
    positions = jnp.arange(key_count, dtype=jnp.int32)
    usable = (window_request[:, None] == owner_id) & (
        positions[None, :] < image_tiles[0] * (key_count // TILES)
    )
    scores = jnp.einsum(
        "tkgd,vkd->tkgv",
        query_heads,
        key_block.reshape(key_count, KV_HEADS, HEAD),
        preferred_element_type=jnp.float32,
    ) * HEAD ** (-0.5)
    scores = jnp.where(usable[:, None, None, :], scores, masked_score)
    window_max = jnp.max(scores, axis=-1).reshape(window, q_count)
    every_max = lax.dynamic_update_slice_in_dim(
        jnp.full((text_total, q_count), masked_score, jnp.float32), window_max, first_token, 0
    )
    top_score = lax.pmax(every_max, "image")
    window_top = lax.dynamic_slice_in_dim(top_score, first_token, window, 0).reshape(
        window, KV_HEADS, head_group
    )
    weights = jnp.where(
        usable[:, None, None, :], jnp.exp(scores - window_top[..., None]), 0.0
    ).astype(jnp.bfloat16)
    totals = jnp.sum(weights, axis=-1, dtype=jnp.float32).reshape(window, q_count)
    numerator = jnp.einsum(
        "tkgv,vkd->tkgd",
        weights,
        value_block.reshape(key_count, KV_HEADS, HEAD),
        preferred_element_type=jnp.float32,
    ).reshape(window, q_count * HEAD)
    my_first = lax.axis_index("image") * own_count
    own_tokens = my_first + jnp.arange(own_count, dtype=jnp.int32)
    window_slots = jnp.arange(window, dtype=jnp.int32)
    start_value = first_token.astype(jnp.float32).reshape(1)
    pieces = (
        lax.all_gather(numerator, "image", axis=0, tiled=True),
        lax.all_gather(totals, "image", axis=0, tiled=True),
        lax.all_gather(start_value, "image", axis=0, tiled=True),
    )
    piece_count = pieces[2].shape[0]
    starts = pieces[2].astype(jnp.int32)
    offsets = own_tokens[None, :] - starts[:, None]
    chooser = (window_slots[None, None, :] == offsets[:, :, None]).astype(jnp.float32)
    numer_piece = pieces[0].reshape(piece_count, window, -1)
    totals_piece = pieces[1].reshape(piece_count, window, -1)
    numer_own = jnp.einsum("jrw,jwc->rc", chooser, numer_piece, precision=lax.Precision.HIGHEST)
    totals_own = jnp.einsum("jrw,jwc->rc", chooser, totals_piece, precision=lax.Precision.HIGHEST)
    attended = numer_own.reshape(own_count, -1, HEAD) / totals_own[..., None]
    return attended.reshape(own_count, -1).astype(jnp.bfloat16)


CORES = 2
COLUMNS = 2
PLANE = CORES * COLUMNS
EXTRA = 16
WINDOW = 4
MESSAGE = 40
IMAGES = 4


def after(value, *others):
    return lax.optimization_barrier((value,) + others)[0]


def whole(count, space=pltpu.VMEM):
    return [pl.BlockSpec(memory_space=space)] * count


def call(kernel, out_shape, in_specs, scratch=(), vmem=16, flops=0, moved=0):
    outs = out_shape if isinstance(out_shape, (list, tuple)) else [out_shape]
    specs = [pl.BlockSpec(memory_space=pltpu.VMEM)] * len(outs)
    return pl.pallas_call(
        kernel,
        out_shape=out_shape,
        in_specs=in_specs,
        out_specs=specs if isinstance(out_shape, (list, tuple)) else specs[0],
        scratch_shapes=list(scratch),
        compiler_params=pltpu.CompilerParams(vmem_limit_bytes=vmem * 2**20),
        cost_estimate=pl.CostEstimate(flops=flops, bytes_accessed=moved, transcendentals=0),
    )


def send_kernel(half, targets, vision_ref, *refs):
    out_refs, sems = refs[:-1], refs[-1]
    y, core = lax.axis_index("groups"), lax.rem(lax.axis_index("image"), CORES)
    started = []
    for t, (core_flip, half_flip) in enumerate(targets):
        at_core = 1 - core if core_flip else core
        at_half = 1 - y if half_flip else y
        for p in range(out_refs[t].shape[1] // half):
            at = pl.multiple_of(((p * CORES + at_core) * 2 + at_half) * half, half)
            copy = pltpu.make_async_copy(
                vision_ref.at[:, pl.ds(at, half)],
                out_refs[t].at[:, p * half : (p + 1) * half],
                sems.at[t, p],
            )
            copy.start()
            started.append(copy)
    for copy in started:
        copy.wait()


def send_columns(vision, half, targets):
    keys, depth = vision.shape
    pairs = depth // half // (2 * CORES)
    one = jax.ShapeDtypeStruct((keys, pairs * half), vision.dtype)
    count = len(targets)
    return pl.pallas_call(
        functools.partial(send_kernel, half, targets),
        out_shape=[one] * count,
        in_specs=whole(1, pl.ANY),
        out_specs=whole(count, pl.ANY),
        scratch_shapes=[pltpu.SemaphoreType.DMA((count, pairs))],
        cost_estimate=pl.CostEstimate(flops=0, bytes_accessed=count * keys * depth, transcendentals=0),
    )(vision)


def prepare_kernel(
    half, text_ref, image_ref, tiles_ref, tenant_ref, page_ref, queries_ref, key_ref, value_ref,
    key_out, value_out, text, image, tiles, tenant, pages, line, sems,
):
    start = pl.multiple_of(lax.axis_index("groups") * half, half)
    copies = [
        pltpu.make_async_copy(*pair, sems.at[i])
        for i, pair in enumerate(
            (
                (text_ref, text), (image_ref, image), (tiles_ref, tiles), (tenant_ref, tenant),
                (page_ref, pages), (queries_ref, line),
                (key_ref.at[pl.ds(start, half), :], key_out.at[0:half, :]),
                (value_ref.at[pl.ds(start, half), :], value_out),
            )
        )
    ]
    for copy in copies:
        copy.start()
    for copy in copies:
        copy.wait()
    width = key_ref.shape[1]
    owner = image[0, 0]
    page = pages[tenant[owner]]
    row = lax.broadcasted_iota(jnp.int32, (EXTRA, width), 0)
    lane = lax.broadcasted_iota(jnp.int32, (EXTRA, width), 1)
    block = jnp.zeros((EXTRA, width), jnp.float32)
    for r in range(queries_ref.shape[1] // width):
        piece = line[0:1, r * width : (r + 1) * width].astype(jnp.float32)
        block = jnp.where(row == r, piece, block)
    for at, number in enumerate((text[0], owner, page, tiles[0])):
        block = jnp.where((row == 8) & (lane == at), number.astype(jnp.float32), block)
    key_out[half : half + EXTRA, :] = block.astype(key_out.dtype)


def project_kernel(pieces, arrays, half, *refs):
    cols_ref = refs[0]
    vision_refs = refs[1 : 1 + IMAGES]
    weight_refs = refs[1 + IMAGES : 1 + IMAGES + arrays]
    out_ref, slots, weights, sems = refs[1 + IMAGES + arrays :]
    keys = vision_refs[0].shape[0]
    count = len(pieces)
    weight_copies = []
    image_copies = [[] for _ in range(IMAGES)]
    for p, (which, row) in enumerate(pieces):
        weight_copies.append(
            pltpu.make_async_copy(
                weight_refs[which].at[row : row + half, :],
                weights.at[p * half : (p + 1) * half, :],
                sems.at[IMAGES, p],
            )
        )
    for i in range(IMAGES):
        for p in range(count):
            at = pl.multiple_of(cols_ref[0 if i == 0 else 1, p] * half, half)
            image_copies[i].append(
                pltpu.make_async_copy(
                    vision_refs[i].at[:, pl.ds(at, half)],
                    slots.at[i, :, p * half : (p + 1) * half],
                    sems.at[i, p],
                )
            )
    order = [weight_copies] + image_copies
    for group in order:
        for copy in group:
            copy.start()
    for copy in weight_copies:
        copy.wait()
    for i in range(IMAGES):
        for copy in image_copies[i]:
            copy.wait()
        out_ref[i] = jnp.dot(slots[i], weights[...], preferred_element_type=jnp.float32)


def project(images, arrays, pieces, cols, half):
    keys = images[0].shape[0]
    width = arrays[0].shape[1]
    count = len(pieces)
    return call(
        functools.partial(project_kernel, pieces, len(arrays), half),
        jax.ShapeDtypeStruct((IMAGES, keys, width), jnp.float32),
        whole(1, pltpu.SMEM) + whole(IMAGES + len(arrays), pl.ANY),
        scratch=[
            pltpu.VMEM((IMAGES, keys, count * half), images[0].dtype),
            pltpu.VMEM((count * half, width), arrays[0].dtype),
            pltpu.SemaphoreType.DMA((IMAGES + 1, count)),
        ],
        vmem=24,
        flops=2 * IMAGES * keys * half * width * count,
        moved=count * half * (IMAGES * keys + width) * 2,
    )(cols, *images, *arrays)


def slot_of(token, me, steps):
    z, x, core = token // PLANE, token // CORES % COLUMNS, token % CORES
    mz, mx, mcore = me // PLANE, me // CORES % COLUMNS, me % CORES
    d = lax.rem(z - mz + steps, steps)
    across = jnp.where(core == mcore, 0, 1) * COLUMNS + jnp.where(x == mx, 0, 1)
    return across * steps + d


def pick_kernel(total, steps, rank, extras_ref, down_ref, out_ref, flat):
    me = lax.axis_index("image")
    flat[...] = down_ref[...].T
    for dest in range(total):
        at = pl.multiple_of(slot_of(jnp.int32(dest), me, steps) * EXTRA, EXTRA)
        tile = extras_ref[pl.ds(at, EXTRA), 0:HEAD].astype(jnp.float32)
        page = tile[8, 2].astype(jnp.int32)
        out_ref[dest] = flat[pl.ds(pl.multiple_of(page * rank, rank), rank), :]


def own_fact(extras_ref, lane):
    return extras_ref[0:EXTRA, 0:HEAD].astype(jnp.float32)[8, lane].astype(jnp.int32)


def lowrank_kernel(extras_ref, vision_ref, down_ref, up_ref, out_ref):
    shards, rank, rows = down_ref.shape
    total = jnp.zeros((vision_ref.shape[0], rank), jnp.float32)
    for j in range(shards):
        total = total + lax.dot_general(
            vision_ref[:, j * rows : (j + 1) * rows],
            down_ref[j],
            (((1,), (1,)), ((), ())),
            preferred_element_type=jnp.float32,
        )
    page = own_fact(extras_ref, 2)
    out_ref[...] = jnp.dot(
        total.astype(jnp.bfloat16), up_ref[page], preferred_element_type=jnp.float32
    )


def window_start(extras_ref, owner, text_total):
    ids = extras_ref[:, 0:HEAD].astype(jnp.float32)
    row = lax.broadcasted_iota(jnp.int32, ids.shape, 0)
    lane = lax.broadcasted_iota(jnp.int32, ids.shape, 1)
    smaller = (row % EXTRA == 8) & (lane == 0) & (ids < owner.astype(jnp.float32))
    first = jnp.sum(jnp.where(smaller, 1.0, 0.0)).astype(jnp.int32)
    return jnp.minimum(first, text_total - WINDOW)


def select_rows(parts, rows):
    head = lax.broadcasted_iota(jnp.int32, parts[0].shape, 0) % 8 // 2
    result = parts[0]
    for k in range(1, KV_HEADS):
        result = jnp.where(head == k, parts[k], result)
    return result


def score_kernel(total, steps, mine_ref, core_ref, pair_ref, gain_ref, extras_ref, weights_ref, stats_ref):
    me, owner = lax.axis_index("image"), own_fact(extras_ref, 1)
    keys = mine_ref.shape[1]
    first = window_start(extras_ref, owner, total)
    tiles = []
    match = []
    for s in range(WINDOW):
        at = pl.multiple_of(slot_of(first + s, me, steps) * EXTRA, EXTRA)
        block = extras_ref[pl.ds(at, EXTRA), :].astype(jnp.float32)
        tiles += [block[0:8, k * HEAD : (k + 1) * HEAD] for k in range(KV_HEADS)]
        match.append(block[8, 0].astype(jnp.int32) == owner)
    query = jnp.concatenate(tiles, axis=0).astype(jnp.bfloat16)
    key_raw = mine_ref[0] + core_ref[0] + pair_ref[...]
    gain = gain_ref[...]
    parts = []
    for k in range(KV_HEADS):
        head = key_raw[:, k * HEAD : (k + 1) * HEAD]
        scale = lax.rsqrt(jnp.mean(head * head, axis=1, keepdims=True) + epsilon)
        block = (head * scale * gain).astype(jnp.bfloat16)
        parts.append(
            lax.dot_general(query, block, (((1,), (1,)), ((), ())), preferred_element_type=jnp.float32)
        )
    scores = select_rows(parts, query.shape[0]) * HEAD ** (-0.5)
    row = lax.broadcasted_iota(jnp.int32, scores.shape, 0) // (8 * KV_HEADS)
    lane = lax.broadcasted_iota(jnp.int32, scores.shape, 1)
    limit = jnp.zeros(scores.shape, jnp.int32)
    slots = own_fact(extras_ref, 3) * (keys // TILES)
    for s in range(WINDOW):
        limit = jnp.where(row == s, jnp.where(match[s], slots, 0), limit)
    usable = lane < limit
    scores = jnp.where(usable, scores, masked_score)
    top = jnp.max(scores, axis=1, keepdims=True)
    weights = jnp.where(usable, jnp.exp(scores - top), 0.0).astype(jnp.bfloat16)
    weights_ref[...] = weights
    sums = jnp.sum(weights.astype(jnp.float32), axis=1, keepdims=True)
    rows = 8 * KV_HEADS
    eye = lax.broadcasted_iota(jnp.int32, (rows, HEAD), 0) == lax.broadcasted_iota(jnp.int32, (rows, HEAD), 1)
    line = lax.broadcasted_iota(jnp.int32, (8, HEAD), 0)
    for s in range(WINDOW):
        own = slice(s * rows, (s + 1) * rows)
        top_row = jnp.sum(jnp.where(eye, top[own], 0.0), axis=0, keepdims=True)
        sum_row = jnp.sum(jnp.where(eye, sums[own], 0.0), axis=0, keepdims=True)
        block = jnp.where(line == 0, top_row, jnp.where(line == 1, sum_row, 0.0))
        block = jnp.where(line == 2, first.astype(jnp.float32), block)
        stats_ref[s] = jnp.where(line == 3, jnp.where(match[s], 1.0, 0.0), block)


def value_kernel(steps, mine_ref, core_ref, pair_ref, lowrank_ref, weights_ref, stats_ref, *refs):
    out_refs, numerators = refs[:-1], refs[-1]
    me, first = lax.axis_index("image"), stats_ref[0][2, 0].astype(jnp.int32)
    value = (mine_ref[0] + core_ref[0] + pair_ref[...] + lowrank_ref[...]).astype(jnp.bfloat16)
    weights = weights_ref[...]
    parts = [
        jnp.dot(weights, value[:, k * HEAD : (k + 1) * HEAD], preferred_element_type=jnp.float32)
        for k in range(KV_HEADS)
    ]
    result = select_rows(parts, weights.shape[0])
    rows = 8 * KV_HEADS
    for s in range(WINDOW):
        numerators[s, 0:rows, :] = result[s * rows : (s + 1) * rows]
        numerators[s, rows:MESSAGE, :] = stats_ref[s]
    match = [stats_ref[s][3, 0] for s in range(WINDOW)]
    line = lax.broadcasted_iota(jnp.int32, (MESSAGE, HEAD), 0)
    empty = jnp.where(line == rows, masked_score, 0.0)
    group = lax.rem(me, PLANE)
    for k, out_ref in enumerate(out_refs):
        core, x = lax.rem(group, CORES), group // CORES
        to = (x if k < CORES else 1 - x) * CORES + (core if k % CORES == 0 else 1 - core)
        for z in range(steps):
            s = z * PLANE + to - first
            inside = (s >= 0) & (s < WINDOW)
            s = jnp.clip(s, 0, WINDOW - 1)
            good = match[0] > 0.5
            for j in range(1, WINDOW):
                good = jnp.where(s == j, match[j], jnp.where(good, 1.0, 0.0)) > 0.5
            good = inside & good
            out_ref[z] = jnp.where(good, numerators[s], empty)


def merge(blocks):
    rows = 8 * KV_HEADS
    tops = [b[rows : rows + 1] for b in blocks]
    top = functools.reduce(jnp.maximum, tops)
    eye = lax.broadcasted_iota(jnp.int32, (rows, HEAD), 0) == lax.broadcasted_iota(jnp.int32, (rows, HEAD), 1)
    numerator, total = 0.0, 0.0
    for b, t in zip(blocks, tops):
        scale = jnp.exp(t - top)
        total = total + scale * b[rows + 1 : rows + 2]
        column = jnp.sum(jnp.where(eye, scale, 0.0), axis=1, keepdims=True)
        numerator = numerator + column * b[0:rows]
    return numerator, top, total, eye


def plane_kernel(steps, *refs):
    in_refs, out_refs, merged = refs[:PLANE], refs[PLANE : PLANE + steps], refs[-1]
    rows = 8 * KV_HEADS
    line = lax.broadcasted_iota(jnp.int32, (8, HEAD), 0)
    for z in range(steps):
        numerator, top, total, _ = merge([ref[z] for ref in in_refs])
        merged[z, 0:rows, :] = numerator
        merged[z, rows:MESSAGE, :] = jnp.where(line == 0, top, jnp.where(line == 1, total, 0.0))
    for d, out_ref in enumerate(out_refs):
        out_ref[...] = merged[lax.rem(lax.axis_index("image") // PLANE + d, steps)]


def final_kernel(*refs):
    out_ref = refs[-1]
    numerator, top, total, eye = merge([ref[...] for ref in refs[:-1]])
    column = jnp.sum(jnp.where(eye, total, 0.0), axis=1, keepdims=True)
    out = numerator / column
    for k in range(KV_HEADS):
        for r in range(8):
            at = (r * KV_HEADS + k) * HEAD
            out_ref[:, at : at + HEAD] = out[8 * k + r : 8 * k + r + 1].astype(out_ref.dtype)


def local(
    devices,
    vision,
    queries,
    text_request,
    key_weight,
    value_weight,
    key_gain,
    down_pages,
    up_pages,
    image_request,
    image_tiles,
    request_tenant,
    tenant_page,
):
    steps = devices // PLANE
    me = lax.axis_index("image").astype(jnp.int32)
    y = lax.axis_index("groups").astype(jnp.int32)
    z, x, core = me // PLANE, me // CORES % COLUMNS, me % CORES
    tokens = vision[0]
    rows, width = key_weight.shape
    half = rows // 2
    rank = up_pages.shape[1]
    everyone = range(devices)

    def across(value, bits):
        return lax.ppermute(value, "image", [(i, i ^ bits) for i in everyone])

    def along(value, d):
        return lax.ppermute(value, "image", [(i, (i - PLANE * d) % devices) for i in everyone])

    def swap(value, bits=0):
        pairs = [(g * devices + i, (1 - g) * devices + (i ^ bits)) for g in range(2) for i in everyone]
        return lax.ppermute(value, ("groups", "image"), pairs)

    def join(*arrays):
        return jnp.concatenate(arrays, axis=0)

    step = half + EXTRA
    key_half, value_half = pl.pallas_call(
        functools.partial(prepare_kernel, half),
        out_shape=[
            jax.ShapeDtypeStruct((step, width), key_weight.dtype),
            jax.ShapeDtypeStruct((half, width), value_weight.dtype),
        ],
        in_specs=whole(8, pl.ANY),
        out_specs=whole(2),
        scratch_shapes=[
            pltpu.SMEM(text_request.shape, jnp.int32),
            pltpu.SMEM(image_request.shape, jnp.int32),
            pltpu.SMEM(image_tiles.shape, jnp.int32),
            pltpu.SMEM(request_tenant.shape, jnp.int32),
            pltpu.SMEM(tenant_page.shape, jnp.int32),
            pltpu.VMEM(queries.shape, queries.dtype),
            pltpu.SemaphoreType.DMA((8,)),
        ],
    )(text_request, image_request, image_tiles, request_tenant, tenant_page, queries, key_weight, value_weight)

    to_pair, to_diagonal = send_columns(tokens, half, ((False, True), (True, True)))
    (to_core,) = send_columns(tokens, half, ((True, False),))
    from_pair = swap(to_pair)
    from_diagonal = swap(after(to_diagonal, from_pair), 1)
    from_core = across(to_core, 1)

    k1, k3 = along(key_half, 1), along(key_half, 3)
    k_own = across(key_half, CORES)
    k2 = along(after(key_half, k1, k3, k_own), 2)
    kx = across(after(join(k1, k3), k_own), CORES)
    v_own = across(after(value_half, k_own), CORES)
    v1, v3 = along(after(value_half, k2, kx), 1), along(after(value_half, k2, kx), 3)
    kx2 = across(after(k2, kx), CORES)
    v2 = along(after(value_half, v1, v3), 2)
    vx = across(after(join(v1, v3), kx2), CORES)
    vx2 = across(v2, CORES)

    spots = [(d, mirrored) for mirrored in (False, True) for d in (0, 1, 3, 2)]
    pairs = [lax.rem(z + d, steps) * COLUMNS + (1 - x if mirrored else x) for d, mirrored in spots]
    cols = jnp.stack([jnp.stack([(p * CORES + core) * 2 + y for p in pairs]), jnp.stack(pairs)])

    near = join(key_half[half:], k1[half:], k2[half:], k3[half:], k_own[half:], kx[half:step], kx2[half:], kx[step + half :])
    extras = join(near, across(near, 1))
    picked = call(
        functools.partial(pick_kernel, devices, steps, rank),
        jax.ShapeDtypeStruct((devices, rank, rows), down_pages.dtype),
        whole(2),
        scratch=[pltpu.VMEM(down_pages.shape[::-1], down_pages.dtype)],
    )(extras, down_pages)
    picked = lax.all_to_all(picked, "image", 0, 0, tiled=True)
    lowrank = call(
        lowrank_kernel,
        jax.ShapeDtypeStruct((tokens.shape[0], width), jnp.float32),
        whole(4),
        vmem=16,
        moved=tokens.size * 2,
    )(extras, tokens, picked, up_pages)

    images = [tokens, from_core, from_pair, from_diagonal]
    pieces = ((0, 0), (2, 0), (3, 0), (4, 0), (1, 0), (5, 0), (5, step), (6, 0))
    keys_part = project(images, [key_half, k_own, k1, k3, k2, kx, kx2], pieces, after(cols, lowrank), half)
    pieces = ((0, 0), (2, 0), (3, 0), (4, 0), (1, 0), (5, 0), (5, half), (6, 0))
    values_part = project(
        images, [value_half, v_own, v1, v3, v2, vx, vx2], pieces, after(cols, keys_part), half
    )

    keys_core = across(jnp.stack([keys_part[1], keys_part[3]]), 1)
    keys_pair = swap(keys_part[2] + keys_core[1])
    values_core = across(jnp.stack([values_part[1], values_part[3]]), 1)
    values_pair = swap(after(values_part[2] + values_core[1], keys_pair))

    heads = WINDOW * 8 * KV_HEADS
    weights, stats = call(
        functools.partial(score_kernel, devices, steps),
        [
            jax.ShapeDtypeStruct((heads, tokens.shape[0]), jnp.bfloat16),
            jax.ShapeDtypeStruct((WINDOW, 8, HEAD), jnp.float32),
        ],
        whole(5),
    )(keys_part, keys_core, keys_pair, key_gain.reshape(1, HEAD), extras)

    message = jax.ShapeDtypeStruct((steps, MESSAGE, HEAD), jnp.float32)
    messages = call(
        functools.partial(value_kernel, steps),
        [message] * PLANE,
        whole(6),
        scratch=[pltpu.VMEM((WINDOW, MESSAGE, HEAD), jnp.float32)],
    )(values_part, values_core, values_pair, lowrank, weights, stats)
    arrived = [messages[0]] + [across(messages[k], k) for k in range(1, PLANE)]
    one = jax.ShapeDtypeStruct((MESSAGE, HEAD), jnp.float32)
    merged = call(
        functools.partial(plane_kernel, steps),
        [one] * steps,
        whole(PLANE),
        scratch=[pltpu.VMEM((steps, MESSAGE, HEAD), jnp.float32)],
    )(*arrived)
    arrived = [merged[0]] + [along(merged[d], steps - d) for d in range(1, steps)]
    out = call(
        final_kernel,
        jax.ShapeDtypeStruct(queries.shape, jnp.bfloat16),
        whole(steps),
    )(*arrived)
    return out


def fits(mesh, vision, queries, key_weight):
    devices = mesh.shape["image"]
    rows = key_weight.shape[0] // devices
    own = queries.shape[0] // (mesh.shape["groups"] * devices)
    one = vision.shape[0] == mesh.shape["groups"] * devices
    return rows % 256 == 0 and devices == 4 * PLANE and mesh.shape["groups"] == 2 and own == 1 and one


def solution(mesh):
    in_specs = (
        P(("groups", "image"), None, None),
        P(("groups", "image"), None),
        P(("groups", "image")),
        P("image", None),
        P("image", None),
        P(),
        P("image", None),
        P(),
        P(("groups", "image"), None),
        P(("groups", "image")),
        P("groups"),
        P(),
    )
    out_specs = P(("groups", "image"), None)

    def run(*args):
        if fits(mesh, args[0], args[1], args[3]):
            body = functools.partial(local, mesh.shape["image"])
        else:
            body = local_gathered
        return jax.shard_map(body, mesh=mesh, in_specs=in_specs, out_specs=out_specs, check_vma=False)(*args)

    return run
```

```python
import functools

import jax
import jax.numpy as jnp
from jax import lax
from jax.experimental import pallas as pl
from jax.experimental.pallas import tpu as pltpu
from jax.sharding import PartitionSpec as P

HEAD = 128
KV_HEADS = 4
TILES = 4


epsilon = 1e-05
masked_score = -1e30


def select_entry(table, position):
    matches = jnp.arange(table.shape[0], dtype=jnp.int32) == position
    return jnp.sum(jnp.where(matches, table, 0))


def local_gathered(
    vision,
    queries,
    text_request,
    key_weight,
    value_weight,
    key_gain,
    down_pages,
    up_pages,
    image_request,
    image_tiles,
    request_tenant,
    tenant_page,
):
    image_tokens = vision[0]
    key_count = image_tokens.shape[0]
    kv_width = key_weight.shape[1]
    low_rank = up_pages.shape[1]
    owner_id = image_request[0, 0]
    tenant_id = select_entry(request_tenant, owner_id)
    page_id = select_entry(tenant_page, tenant_id)

    def token_columns():
        return image_tokens

    pieces = (
        lax.all_gather(key_weight, "image", axis=0, tiled=True),
        lax.all_gather(value_weight, "image", axis=0, tiled=True),
    )
    columns = token_columns()
    key_raw = jnp.dot(columns, pieces[0], preferred_element_type=jnp.float32)
    value_raw = jnp.dot(columns, pieces[1], preferred_element_type=jnp.float32)
    columns = token_columns()
    lowrank_sum = jnp.dot(
        columns,
        lax.dynamic_slice_in_dim(
            lax.all_gather(down_pages, "image", axis=0, tiled=True), page_id * low_rank, low_rank, 1
        ),
        preferred_element_type=jnp.float32,
    )
    lowrank = lowrank_sum.astype(jnp.bfloat16)
    up_factor = lax.dynamic_index_in_dim(up_pages, page_id, 0, keepdims=False)
    value_block = (
        value_raw + jnp.dot(lowrank, up_factor, preferred_element_type=jnp.float32)
    ).astype(jnp.bfloat16)
    key_heads = key_raw.reshape(key_count, KV_HEADS, HEAD)
    inverse_rms = lax.rsqrt(jnp.mean(key_heads * key_heads, axis=-1, keepdims=True) + epsilon)
    key_block = (
        (key_heads * inverse_rms * key_gain).reshape(key_count, kv_width).astype(jnp.bfloat16)
    )
    every_query, every_request = (
        lax.all_gather(queries, "image", axis=0, tiled=True),
        lax.all_gather(text_request, "image", axis=0, tiled=True),
    )
    text_total = every_query.shape[0]
    own_count = queries.shape[0]
    window = min(4 * own_count, text_total)
    head_group = every_query.shape[1] // kv_width
    q_count = KV_HEADS * head_group
    first_token = jnp.sum((every_request < owner_id).astype(jnp.int32))
    first_token = jnp.minimum(first_token, text_total - window)
    window_query = lax.dynamic_slice_in_dim(every_query, first_token, window, 0)
    window_request = lax.dynamic_slice_in_dim(every_request, first_token, window, 0)
    query_heads = window_query.reshape(window, KV_HEADS, head_group, HEAD)
    positions = jnp.arange(key_count, dtype=jnp.int32)
    usable = (window_request[:, None] == owner_id) & (
        positions[None, :] < image_tiles[0] * (key_count // TILES)
    )
    scores = jnp.einsum(
        "tkgd,vkd->tkgv",
        query_heads,
        key_block.reshape(key_count, KV_HEADS, HEAD),
        preferred_element_type=jnp.float32,
    ) * HEAD ** (-0.5)
    scores = jnp.where(usable[:, None, None, :], scores, masked_score)
    window_max = jnp.max(scores, axis=-1).reshape(window, q_count)
    every_max = lax.dynamic_update_slice_in_dim(
        jnp.full((text_total, q_count), masked_score, jnp.float32), window_max, first_token, 0
    )
    top_score = lax.pmax(every_max, "image")
    window_top = lax.dynamic_slice_in_dim(top_score, first_token, window, 0).reshape(
        window, KV_HEADS, head_group
    )
    weights = jnp.where(
        usable[:, None, None, :], jnp.exp(scores - window_top[..., None]), 0.0
    ).astype(jnp.bfloat16)
    totals = jnp.sum(weights, axis=-1, dtype=jnp.float32).reshape(window, q_count)
    numerator = jnp.einsum(
        "tkgv,vkd->tkgd",
        weights,
        value_block.reshape(key_count, KV_HEADS, HEAD),
        preferred_element_type=jnp.float32,
    ).reshape(window, q_count * HEAD)
    my_first = lax.axis_index("image") * own_count
    own_tokens = my_first + jnp.arange(own_count, dtype=jnp.int32)
    window_slots = jnp.arange(window, dtype=jnp.int32)
    start_value = first_token.astype(jnp.float32).reshape(1)
    pieces = (
        lax.all_gather(numerator, "image", axis=0, tiled=True),
        lax.all_gather(totals, "image", axis=0, tiled=True),
        lax.all_gather(start_value, "image", axis=0, tiled=True),
    )
    piece_count = pieces[2].shape[0]
    starts = pieces[2].astype(jnp.int32)
    offsets = own_tokens[None, :] - starts[:, None]
    chooser = (window_slots[None, None, :] == offsets[:, :, None]).astype(jnp.float32)
    numer_piece = pieces[0].reshape(piece_count, window, -1)
    totals_piece = pieces[1].reshape(piece_count, window, -1)
    numer_own = jnp.einsum("jrw,jwc->rc", chooser, numer_piece, precision=lax.Precision.HIGHEST)
    totals_own = jnp.einsum("jrw,jwc->rc", chooser, totals_piece, precision=lax.Precision.HIGHEST)
    attended = numer_own.reshape(own_count, -1, HEAD) / totals_own[..., None]
    return attended.reshape(own_count, -1).astype(jnp.bfloat16)


CORES = 2
COLUMNS = 2
PLANE = CORES * COLUMNS
EXTRA = 16
WINDOW = 4
MESSAGE = 40
IMAGES = 4


def after(value, *others):
    return lax.optimization_barrier((value,) + others)[0]


def whole(count, space=pltpu.VMEM):
    return [pl.BlockSpec(memory_space=space)] * count


def call(kernel, out_shape, in_specs, scratch=(), vmem=16, flops=0, moved=0):
    outs = out_shape if isinstance(out_shape, (list, tuple)) else [out_shape]
    specs = [pl.BlockSpec(memory_space=pltpu.VMEM)] * len(outs)
    return pl.pallas_call(
        kernel,
        out_shape=out_shape,
        in_specs=in_specs,
        out_specs=specs if isinstance(out_shape, (list, tuple)) else specs[0],
        scratch_shapes=list(scratch),
        compiler_params=pltpu.CompilerParams(vmem_limit_bytes=vmem * 2**20),
        cost_estimate=pl.CostEstimate(flops=flops, bytes_accessed=moved, transcendentals=0),
    )


def column_copies(half, targets, vision_ref, out_refs, sems):
    y, core = lax.axis_index("groups"), lax.rem(lax.axis_index("image"), CORES)
    copies = []
    for t, (core_flip, half_flip) in enumerate(targets):
        at_core = 1 - core if core_flip else core
        at_half = 1 - y if half_flip else y
        for p in range(out_refs[t].shape[1] // half):
            at = pl.multiple_of(((p * CORES + at_core) * 2 + at_half) * half, half)
            copies.append(
                pltpu.make_async_copy(
                    vision_ref.at[:, pl.ds(at, half)],
                    out_refs[t].at[:, p * half : (p + 1) * half],
                    sems.at[t, p],
                )
            )
    return copies


def send_kernel(half, targets, vision_ref, *refs):
    copies = column_copies(half, targets, vision_ref, refs[:-1], refs[-1])
    for copy in copies:
        copy.start()
    for copy in copies:
        copy.wait()


def send_columns(vision, half, targets):
    keys, depth = vision.shape
    pairs = depth // half // (2 * CORES)
    one = jax.ShapeDtypeStruct((keys, pairs * half), vision.dtype)
    count = len(targets)
    return pl.pallas_call(
        functools.partial(send_kernel, half, targets),
        out_shape=[one] * count,
        in_specs=whole(1, pl.ANY),
        out_specs=whole(count),
        scratch_shapes=[pltpu.SemaphoreType.DMA((count, pairs))],
        cost_estimate=pl.CostEstimate(flops=0, bytes_accessed=count * keys * depth, transcendentals=0),
    )(vision)


def prepare_kernel(
    half, text_ref, image_ref, tiles_ref, tenant_ref, page_ref, queries_ref, key_ref, value_ref, vision_ref,
    key_out, value_out, pair_out, diagonal_out, text, image, tiles, tenant, pages, line, sems, column_sems,
):
    start = pl.multiple_of(lax.axis_index("groups") * half, half)
    copies = [
        pltpu.make_async_copy(*pair, sems.at[i])
        for i, pair in enumerate(
            (
                (text_ref, text), (image_ref, image), (tiles_ref, tiles), (tenant_ref, tenant),
                (page_ref, pages), (queries_ref, line),
                (key_ref.at[pl.ds(start, half), :], key_out.at[0:half, :]),
                (value_ref.at[pl.ds(start, half), :], value_out),
            )
        )
    ]
    columns = column_copies(
        half, ((False, True), (True, True)), vision_ref, (pair_out, diagonal_out), column_sems
    )
    for copy in copies + columns:
        copy.start()
    for copy in copies:
        copy.wait()
    width = key_ref.shape[1]
    owner = image[0, 0]
    page = pages[tenant[owner]]
    row = lax.broadcasted_iota(jnp.int32, (EXTRA, width), 0)
    lane = lax.broadcasted_iota(jnp.int32, (EXTRA, width), 1)
    block = jnp.zeros((EXTRA, width), jnp.float32)
    for r in range(queries_ref.shape[1] // width):
        piece = line[0:1, r * width : (r + 1) * width].astype(jnp.float32)
        block = jnp.where(row == r, piece, block)
    for at, number in enumerate((text[0], owner, page, tiles[0])):
        block = jnp.where((row == 8) & (lane == at), number.astype(jnp.float32), block)
    key_out[half : half + EXTRA, :] = block.astype(key_out.dtype)
    for copy in columns:
        copy.wait()


def project_kernel(pieces, spots, images, own, arrays, adds, half, steps, *refs):
    vision_refs = refs[:images]
    weight_refs = refs[images : images + arrays]
    before = refs[images + arrays : images + arrays + adds]
    out_ref, slots, weights, sems = refs[images + arrays + adds :]
    me, y = lax.axis_index("image"), lax.axis_index("groups")
    z, x, core = me // PLANE, me // CORES % COLUMNS, me % CORES
    count = len(pieces)
    weight_copies = []
    image_copies = [[] for _ in range(images)]
    for p, (which, row) in enumerate(pieces):
        weight_copies.append(
            pltpu.make_async_copy(
                weight_refs[which].at[row : row + half, :],
                weights.at[p * half : (p + 1) * half, :],
                sems.at[images, p],
            )
        )
    for i in range(images):
        for p in range(count):
            d, mirrored = spots[p]
            pair = lax.rem(z + d, steps) * COLUMNS + (1 - x if mirrored else x)
            at = pl.multiple_of(((pair * CORES + core) * 2 + y if i == own else pair) * half, half)
            image_copies[i].append(
                pltpu.make_async_copy(
                    vision_refs[i].at[:, pl.ds(at, half)],
                    slots.at[i, :, p * half : (p + 1) * half],
                    sems.at[i, p],
                )
            )
    order = [weight_copies] + image_copies
    for group in order:
        for copy in group:
            copy.start()
    for copy in weight_copies:
        copy.wait()
    for i in range(images):
        for copy in image_copies[i]:
            copy.wait()
        product = jnp.dot(slots[i], weights[...], preferred_element_type=jnp.float32)
        out_ref[i] = before[0][i] + product if adds else product


def project(images, own, arrays, pieces, spots, half, steps, *before):
    keys = images[-1].shape[0]
    width = arrays[0].shape[1]
    count = len(pieces)
    number = len(images)
    return call(
        functools.partial(project_kernel, pieces, spots, number, own, len(arrays), len(before), half, steps),
        jax.ShapeDtypeStruct((number, keys, width), jnp.float32),
        whole(number + len(arrays), pl.ANY) + whole(len(before)),
        scratch=[
            pltpu.VMEM((number, keys, count * half), images[0].dtype),
            pltpu.VMEM((count * half, width), arrays[0].dtype),
            pltpu.SemaphoreType.DMA((number + 1, count)),
        ],
        vmem=16,
        flops=2 * number * keys * half * width * count,
        moved=count * half * (number * keys + width) * 2,
    )(*images, *arrays, *before)


def slot_of(token, me, steps):
    z, x, core = token // PLANE, token // CORES % COLUMNS, token % CORES
    mz, mx, mcore = me // PLANE, me // CORES % COLUMNS, me % CORES
    d = lax.rem(z - mz + steps, steps)
    across = jnp.where(core == mcore, 0, 1) * COLUMNS + jnp.where(x == mx, 0, 1)
    return across * steps + d


def pick_kernel(total, steps, rank, extras_ref, down_ref, out_ref, flat):
    me = lax.axis_index("image")
    flat[...] = down_ref[...].T
    for k in range(total):
        at = pl.multiple_of(slot_of(jnp.bitwise_xor(me, k), me, steps) * EXTRA, EXTRA)
        tile = extras_ref[pl.ds(at, EXTRA), 0:HEAD].astype(jnp.float32)
        page = tile[8, 2].astype(jnp.int32)
        out_ref[k] = flat[pl.ds(pl.multiple_of(page * rank, rank), rank), :]


def own_fact(extras_ref, lane):
    return extras_ref[0:EXTRA, 0:HEAD].astype(jnp.float32)[8, lane].astype(jnp.int32)


def lowrank_kernel(order, extras_ref, vision_ref, down_ref, up_ref, out_ref):
    shards, rank, rows = down_ref.shape
    total = jnp.zeros((vision_ref.shape[0], rank), jnp.float32)
    for j in range(shards):
        shard = jnp.bitwise_xor(lax.axis_index("image"), order[j])
        total = total + lax.dot_general(
            vision_ref[:, pl.ds(pl.multiple_of(shard * rows, rows), rows)],
            down_ref[j],
            (((1,), (1,)), ((), ())),
            preferred_element_type=jnp.float32,
        )
    page = own_fact(extras_ref, 2)
    out_ref[...] = jnp.dot(
        total.astype(jnp.bfloat16), up_ref[page], preferred_element_type=jnp.float32
    )


def window_start(extras_ref, owner, text_total):
    ids = extras_ref[:, 0:HEAD].astype(jnp.float32)
    row = lax.broadcasted_iota(jnp.int32, ids.shape, 0)
    lane = lax.broadcasted_iota(jnp.int32, ids.shape, 1)
    smaller = (row % EXTRA == 8) & (lane == 0) & (ids < owner.astype(jnp.float32))
    first = jnp.sum(jnp.where(smaller, 1.0, 0.0)).astype(jnp.int32)
    return jnp.minimum(first, text_total - WINDOW)


def select_rows(parts, rows):
    head = lax.broadcasted_iota(jnp.int32, parts[0].shape, 0) % 8 // 2
    result = parts[0]
    for k in range(1, KV_HEADS):
        result = jnp.where(head == k, parts[k], result)
    return result


def score_kernel(
    total, steps, mine_ref, core_ref, low_ref, high_ref, gain_ref, extras_ref, weights_ref, stats_ref
):
    me, owner = lax.axis_index("image"), own_fact(extras_ref, 1)
    keys = mine_ref.shape[1]
    first = window_start(extras_ref, owner, total)
    tiles = []
    match = []
    for s in range(WINDOW):
        at = pl.multiple_of(slot_of(first + s, me, steps) * EXTRA, EXTRA)
        block = extras_ref[pl.ds(at, EXTRA), :].astype(jnp.float32)
        tiles += [block[0:8, k * HEAD : (k + 1) * HEAD] for k in range(KV_HEADS)]
        match.append(block[8, 0].astype(jnp.int32) == owner)
    query = jnp.concatenate(tiles, axis=0).astype(jnp.bfloat16)
    key_raw = mine_ref[0] + core_ref[...] + jnp.concatenate([low_ref[...], high_ref[...]], axis=1)
    gain = gain_ref[...]
    parts = []
    for k in range(KV_HEADS):
        head = key_raw[:, k * HEAD : (k + 1) * HEAD]
        scale = lax.rsqrt(jnp.mean(head * head, axis=1, keepdims=True) + epsilon)
        block = (head * scale * gain).astype(jnp.bfloat16)
        parts.append(
            lax.dot_general(query, block, (((1,), (1,)), ((), ())), preferred_element_type=jnp.float32)
        )
    scores = select_rows(parts, query.shape[0]) * HEAD ** (-0.5)
    row = lax.broadcasted_iota(jnp.int32, scores.shape, 0) // (8 * KV_HEADS)
    lane = lax.broadcasted_iota(jnp.int32, scores.shape, 1)
    limit = jnp.zeros(scores.shape, jnp.int32)
    slots = own_fact(extras_ref, 3) * (keys // TILES)
    for s in range(WINDOW):
        limit = jnp.where(row == s, jnp.where(match[s], slots, 0), limit)
    usable = lane < limit
    scores = jnp.where(usable, scores, masked_score)
    top = jnp.max(scores, axis=1, keepdims=True)
    weights = jnp.where(usable, jnp.exp(scores - top), 0.0).astype(jnp.bfloat16)
    weights_ref[...] = weights
    sums = jnp.sum(weights.astype(jnp.float32), axis=1, keepdims=True)
    rows = 8 * KV_HEADS
    eye = lax.broadcasted_iota(jnp.int32, (rows, HEAD), 0) == lax.broadcasted_iota(jnp.int32, (rows, HEAD), 1)
    line = lax.broadcasted_iota(jnp.int32, (8, HEAD), 0)
    for s in range(WINDOW):
        own = slice(s * rows, (s + 1) * rows)
        top_row = jnp.sum(jnp.where(eye, top[own], 0.0), axis=0, keepdims=True)
        sum_row = jnp.sum(jnp.where(eye, sums[own], 0.0), axis=0, keepdims=True)
        block = jnp.where(line == 0, top_row, jnp.where(line == 1, sum_row, 0.0))
        block = jnp.where(line == 2, first.astype(jnp.float32), block)
        stats_ref[s] = jnp.where(line == 3, jnp.where(match[s], 1.0, 0.0), block)


def value_kernel(steps, mine_ref, core_ref, pair_ref, lowrank_ref, weights_ref, stats_ref, *refs):
    out_refs, numerators = refs[:-1], refs[-1]
    me, first = lax.axis_index("image"), stats_ref[0][2, 0].astype(jnp.int32)
    value = (mine_ref[0] + core_ref[0] + pair_ref[...] + lowrank_ref[...]).astype(jnp.bfloat16)
    weights = weights_ref[...]
    parts = [
        jnp.dot(weights, value[:, k * HEAD : (k + 1) * HEAD], preferred_element_type=jnp.float32)
        for k in range(KV_HEADS)
    ]
    result = select_rows(parts, weights.shape[0])
    rows = 8 * KV_HEADS
    for s in range(WINDOW):
        numerators[s, 0:rows, :] = result[s * rows : (s + 1) * rows]
        numerators[s, rows:MESSAGE, :] = stats_ref[s]
    match = [stats_ref[s][3, 0] for s in range(WINDOW)]
    line = lax.broadcasted_iota(jnp.int32, (MESSAGE, HEAD), 0)
    empty = jnp.where(line == rows, masked_score, 0.0)
    group = lax.rem(me, PLANE)
    for k, out_ref in enumerate(out_refs):
        core, x = lax.rem(group, CORES), group // CORES
        to = (x if k < CORES else 1 - x) * CORES + (core if k % CORES == 0 else 1 - core)
        for z in range(steps):
            s = z * PLANE + to - first
            inside = (s >= 0) & (s < WINDOW)
            s = jnp.clip(s, 0, WINDOW - 1)
            good = match[0] > 0.5
            for j in range(1, WINDOW):
                good = jnp.where(s == j, match[j], jnp.where(good, 1.0, 0.0)) > 0.5
            good = inside & good
            out_ref[z] = jnp.where(good, numerators[s], empty)


def merge(blocks):
    rows = 8 * KV_HEADS
    tops = [b[rows : rows + 1] for b in blocks]
    top = functools.reduce(jnp.maximum, tops)
    eye = lax.broadcasted_iota(jnp.int32, (rows, HEAD), 0) == lax.broadcasted_iota(jnp.int32, (rows, HEAD), 1)
    numerator, total = 0.0, 0.0
    for b, t in zip(blocks, tops):
        scale = jnp.exp(t - top)
        total = total + scale * b[rows + 1 : rows + 2]
        column = jnp.sum(jnp.where(eye, scale, 0.0), axis=1, keepdims=True)
        numerator = numerator + column * b[0:rows]
    return numerator, top, total, eye


def plane_kernel(steps, *refs):
    in_refs, out_refs, merged = refs[:PLANE], refs[PLANE : PLANE + steps], refs[-1]
    rows = 8 * KV_HEADS
    line = lax.broadcasted_iota(jnp.int32, (8, HEAD), 0)
    for z in range(steps):
        numerator, top, total, _ = merge([ref[z] for ref in in_refs])
        merged[z, 0:rows, :] = numerator
        merged[z, rows:MESSAGE, :] = jnp.where(line == 0, top, jnp.where(line == 1, total, 0.0))
    for d, out_ref in enumerate(out_refs):
        out_ref[...] = merged[lax.rem(lax.axis_index("image") // PLANE + d, steps)]


def final_kernel(*refs):
    out_ref = refs[-1]
    numerator, top, total, eye = merge([ref[...] for ref in refs[:-1]])
    column = jnp.sum(jnp.where(eye, total, 0.0), axis=1, keepdims=True)
    out = numerator / column
    for k in range(KV_HEADS):
        for r in range(8):
            at = (r * KV_HEADS + k) * HEAD
            out_ref[:, at : at + HEAD] = out[8 * k + r : 8 * k + r + 1].astype(out_ref.dtype)


def local(
    devices,
    vision,
    queries,
    text_request,
    key_weight,
    value_weight,
    key_gain,
    down_pages,
    up_pages,
    image_request,
    image_tiles,
    request_tenant,
    tenant_page,
):
    steps = devices // PLANE
    me = lax.axis_index("image").astype(jnp.int32)
    y = lax.axis_index("groups").astype(jnp.int32)
    z, x, core = me // PLANE, me // CORES % COLUMNS, me % CORES
    tokens = vision[0]
    rows, width = key_weight.shape
    half = rows // 2
    rank = up_pages.shape[1]
    everyone = range(devices)

    def across(value, bits):
        return lax.ppermute(value, "image", [(i, i ^ bits) for i in everyone])

    def along(value, d):
        return lax.ppermute(value, "image", [(i, (i - PLANE * d) % devices) for i in everyone])

    def swap(value, bits=0):
        pairs = [(g * devices + i, (1 - g) * devices + (i ^ bits)) for g in range(2) for i in everyone]
        return lax.ppermute(value, ("groups", "image"), pairs)

    def join(*arrays):
        return jnp.concatenate(arrays, axis=0)

    step = half + EXTRA
    sent = jax.ShapeDtypeStruct((tokens.shape[0], tokens.shape[1] // 4), tokens.dtype)
    key_half, value_half, to_pair, to_diagonal = pl.pallas_call(
        functools.partial(prepare_kernel, half),
        out_shape=[
            jax.ShapeDtypeStruct((step, width), key_weight.dtype),
            jax.ShapeDtypeStruct((half, width), value_weight.dtype),
            sent,
            sent,
        ],
        in_specs=whole(9, pl.ANY),
        out_specs=whole(4),
        scratch_shapes=[
            pltpu.SMEM(text_request.shape, jnp.int32),
            pltpu.SMEM(image_request.shape, jnp.int32),
            pltpu.SMEM(image_tiles.shape, jnp.int32),
            pltpu.SMEM(request_tenant.shape, jnp.int32),
            pltpu.SMEM(tenant_page.shape, jnp.int32),
            pltpu.VMEM(queries.shape, queries.dtype),
            pltpu.SemaphoreType.DMA((8,)),
            pltpu.SemaphoreType.DMA((2, sent.shape[1] // half)),
        ],
    )(
        text_request, image_request, image_tiles, request_tenant, tenant_page, queries, key_weight,
        value_weight, tokens,
    )

    (to_core,) = send_columns(tokens, half, ((True, False),))
    from_pair = swap(to_pair)
    from_diagonal = swap(after(to_diagonal, from_pair), 1)
    from_core = across(to_core, 1)

    k1, k3 = along(key_half, 1), along(key_half, 3)
    k_own = across(key_half, CORES)
    k2 = along(after(key_half, k1, k3, k_own), 2)
    kx = across(after(join(k1, k3), k_own), CORES)
    v_own = across(after(value_half, k_own), CORES)
    v1, v3 = along(after(value_half, k2, kx), 1), along(after(value_half, k2, kx), 3)
    kx2 = across(after(k2, kx), CORES)
    v2 = along(after(value_half, v1, v3), 2)
    vx = across(after(join(v1, v3), kx2), CORES)
    vx2 = across(v2, CORES)

    spots = [(d, mirrored) for mirrored in (False, True) for d in (0, 1, 3, 2)]
    near = join(key_half[half:], k1[half:], k2[half:], k3[half:], k_own[half:], kx[half:step], kx2[half:], kx[step + half :])
    extras = join(near, across(near, 1))
    images = [tokens, from_core, from_pair]
    arrays = [key_half, k_own, k1, k3, k2, kx, kx2]
    pieces = ((0, 0), (2, 0), (3, 0), (4, 0), (1, 0), (5, 0), (5, step), (6, 0))
    keys_part = project(images, 0, arrays, pieces, spots, half, steps)
    keys_core = across(keys_part[1], 1)
    late = project([from_diagonal], -1, [after(key_half, keys_part)] + arrays[1:], pieces, spots, half, steps)
    keys_sum = keys_part[2] + across(late[0], 1)
    middle = width // KV_HEADS
    keys_pair = [swap(keys_sum[:, :middle]), swap(keys_sum[:, middle:])]
    picked = call(
        functools.partial(pick_kernel, devices, steps, rank),
        jax.ShapeDtypeStruct((devices, rank, rows), down_pages.dtype),
        whole(2),
        scratch=[pltpu.VMEM(down_pages.shape[::-1], down_pages.dtype)],
    )(after(extras, keys_sum), down_pages)
    picked = picked.reshape(devices, 1, rank, rows)
    order = [0]
    while picked.shape[0] > 1:
        bit = picked.shape[0] // 2
        picked = jnp.concatenate([picked[:bit], across(picked[bit:], bit)], axis=1)
        order = order + [k ^ bit for k in order]
    picked = picked.reshape(devices, rank, rows)
    lowrank = call(
        functools.partial(lowrank_kernel, tuple(order)),
        jax.ShapeDtypeStruct((tokens.shape[0], width), jnp.float32),
        whole(4),
        vmem=16,
        moved=tokens.size * 2,
    )(extras, tokens, picked, up_pages)

    pieces = ((0, 0), (2, 0), (3, 0), (4, 0), (1, 0), (5, 0), (5, half), (6, 0))
    near_values = after(value_half, keys_pair[0])
    images = images + [from_diagonal]
    values_part = project(images, 0, [near_values, v_own, v1, v3, v2, vx], pieces[:-1], spots, half, steps)
    values_part = project(images, 0, [after(vx2, keys_pair[1])], ((0, 0),), spots[-1:], half, steps, values_part)
    values_core = across(jnp.stack([values_part[1], values_part[3]]), 1)
    values_sum = (values_part[2] + values_core[1]).astype(jnp.bfloat16)
    values_pair = swap(values_sum)

    heads = WINDOW * 8 * KV_HEADS
    weights, stats = call(
        functools.partial(score_kernel, devices, steps),
        [
            jax.ShapeDtypeStruct((heads, tokens.shape[0]), jnp.bfloat16),
            jax.ShapeDtypeStruct((WINDOW, 8, HEAD), jnp.float32),
        ],
        whole(6),
    )(keys_part, keys_core, *keys_pair, key_gain.reshape(1, HEAD), extras)

    message = jax.ShapeDtypeStruct((steps, MESSAGE, HEAD), jnp.float32)
    messages = call(
        functools.partial(value_kernel, steps),
        [message] * PLANE,
        whole(6),
        scratch=[pltpu.VMEM((WINDOW, MESSAGE, HEAD), jnp.float32)],
    )(values_part, values_core, values_pair, lowrank, weights, stats)
    arrived = [messages[0]] + [across(messages[k], k) for k in range(1, PLANE)]
    one = jax.ShapeDtypeStruct((MESSAGE, HEAD), jnp.float32)
    merged = call(
        functools.partial(plane_kernel, steps),
        [one] * steps,
        whole(PLANE),
        scratch=[pltpu.VMEM((steps, MESSAGE, HEAD), jnp.float32)],
    )(*arrived)
    arrived = [merged[0]] + [along(merged[d], steps - d) for d in range(1, steps)]
    out = call(
        final_kernel,
        jax.ShapeDtypeStruct(queries.shape, jnp.bfloat16),
        whole(steps),
    )(*arrived)
    return out


def fits(mesh, vision, queries, key_weight):
    devices = mesh.shape["image"]
    rows = key_weight.shape[0] // devices
    own = queries.shape[0] // (mesh.shape["groups"] * devices)
    one = vision.shape[0] == mesh.shape["groups"] * devices
    return rows % 256 == 0 and devices == 4 * PLANE and mesh.shape["groups"] == 2 and own == 1 and one


def solution(mesh):
    in_specs = (
        P(("groups", "image"), None, None),
        P(("groups", "image"), None),
        P(("groups", "image")),
        P("image", None),
        P("image", None),
        P(),
        P("image", None),
        P(),
        P(("groups", "image"), None),
        P(("groups", "image")),
        P("groups"),
        P(),
    )
    out_specs = P(("groups", "image"), None)

    def run(*args):
        if fits(mesh, args[0], args[1], args[3]):
            body = functools.partial(local, mesh.shape["image"])
        else:
            body = local_gathered
        return jax.shard_map(body, mesh=mesh, in_specs=in_specs, out_specs=out_specs, check_vma=False)(*args)

    return run
```

```python
import functools

import jax
import jax.numpy as jnp
from jax import lax
from jax.experimental import pallas as pl
from jax.experimental.pallas import tpu as pltpu
from jax.sharding import PartitionSpec as P

HEAD = 128
KV_HEADS = 4
TILES = 4


epsilon = 1e-05
masked_score = -1e30


def select_entry(table, position):
    matches = jnp.arange(table.shape[0], dtype=jnp.int32) == position
    return jnp.sum(jnp.where(matches, table, 0))


def local_gathered(
    vision,
    queries,
    text_request,
    key_weight,
    value_weight,
    key_gain,
    down_pages,
    up_pages,
    image_request,
    image_tiles,
    request_tenant,
    tenant_page,
):
    image_tokens = vision[0]
    key_count = image_tokens.shape[0]
    kv_width = key_weight.shape[1]
    low_rank = up_pages.shape[1]
    owner_id = image_request[0, 0]
    tenant_id = select_entry(request_tenant, owner_id)
    page_id = select_entry(tenant_page, tenant_id)

    def token_columns():
        return image_tokens

    pieces = (
        lax.all_gather(key_weight, "image", axis=0, tiled=True),
        lax.all_gather(value_weight, "image", axis=0, tiled=True),
    )
    columns = token_columns()
    key_raw = jnp.dot(columns, pieces[0], preferred_element_type=jnp.float32)
    value_raw = jnp.dot(columns, pieces[1], preferred_element_type=jnp.float32)
    columns = token_columns()
    lowrank_sum = jnp.dot(
        columns,
        lax.dynamic_slice_in_dim(
            lax.all_gather(down_pages, "image", axis=0, tiled=True), page_id * low_rank, low_rank, 1
        ),
        preferred_element_type=jnp.float32,
    )
    lowrank = lowrank_sum.astype(jnp.bfloat16)
    up_factor = lax.dynamic_index_in_dim(up_pages, page_id, 0, keepdims=False)
    value_block = (
        value_raw + jnp.dot(lowrank, up_factor, preferred_element_type=jnp.float32)
    ).astype(jnp.bfloat16)
    key_heads = key_raw.reshape(key_count, KV_HEADS, HEAD)
    inverse_rms = lax.rsqrt(jnp.mean(key_heads * key_heads, axis=-1, keepdims=True) + epsilon)
    key_block = (
        (key_heads * inverse_rms * key_gain).reshape(key_count, kv_width).astype(jnp.bfloat16)
    )
    every_query, every_request = (
        lax.all_gather(queries, "image", axis=0, tiled=True),
        lax.all_gather(text_request, "image", axis=0, tiled=True),
    )
    text_total = every_query.shape[0]
    own_count = queries.shape[0]
    window = min(4 * own_count, text_total)
    head_group = every_query.shape[1] // kv_width
    q_count = KV_HEADS * head_group
    first_token = jnp.sum((every_request < owner_id).astype(jnp.int32))
    first_token = jnp.minimum(first_token, text_total - window)
    window_query = lax.dynamic_slice_in_dim(every_query, first_token, window, 0)
    window_request = lax.dynamic_slice_in_dim(every_request, first_token, window, 0)
    query_heads = window_query.reshape(window, KV_HEADS, head_group, HEAD)
    positions = jnp.arange(key_count, dtype=jnp.int32)
    usable = (window_request[:, None] == owner_id) & (
        positions[None, :] < image_tiles[0] * (key_count // TILES)
    )
    scores = jnp.einsum(
        "tkgd,vkd->tkgv",
        query_heads,
        key_block.reshape(key_count, KV_HEADS, HEAD),
        preferred_element_type=jnp.float32,
    ) * HEAD ** (-0.5)
    scores = jnp.where(usable[:, None, None, :], scores, masked_score)
    window_max = jnp.max(scores, axis=-1).reshape(window, q_count)
    every_max = lax.dynamic_update_slice_in_dim(
        jnp.full((text_total, q_count), masked_score, jnp.float32), window_max, first_token, 0
    )
    top_score = lax.pmax(every_max, "image")
    window_top = lax.dynamic_slice_in_dim(top_score, first_token, window, 0).reshape(
        window, KV_HEADS, head_group
    )
    weights = jnp.where(
        usable[:, None, None, :], jnp.exp(scores - window_top[..., None]), 0.0
    ).astype(jnp.bfloat16)
    totals = jnp.sum(weights, axis=-1, dtype=jnp.float32).reshape(window, q_count)
    numerator = jnp.einsum(
        "tkgv,vkd->tkgd",
        weights,
        value_block.reshape(key_count, KV_HEADS, HEAD),
        preferred_element_type=jnp.float32,
    ).reshape(window, q_count * HEAD)
    my_first = lax.axis_index("image") * own_count
    own_tokens = my_first + jnp.arange(own_count, dtype=jnp.int32)
    window_slots = jnp.arange(window, dtype=jnp.int32)
    start_value = first_token.astype(jnp.float32).reshape(1)
    pieces = (
        lax.all_gather(numerator, "image", axis=0, tiled=True),
        lax.all_gather(totals, "image", axis=0, tiled=True),
        lax.all_gather(start_value, "image", axis=0, tiled=True),
    )
    piece_count = pieces[2].shape[0]
    starts = pieces[2].astype(jnp.int32)
    offsets = own_tokens[None, :] - starts[:, None]
    chooser = (window_slots[None, None, :] == offsets[:, :, None]).astype(jnp.float32)
    numer_piece = pieces[0].reshape(piece_count, window, -1)
    totals_piece = pieces[1].reshape(piece_count, window, -1)
    numer_own = jnp.einsum("jrw,jwc->rc", chooser, numer_piece, precision=lax.Precision.HIGHEST)
    totals_own = jnp.einsum("jrw,jwc->rc", chooser, totals_piece, precision=lax.Precision.HIGHEST)
    attended = numer_own.reshape(own_count, -1, HEAD) / totals_own[..., None]
    return attended.reshape(own_count, -1).astype(jnp.bfloat16)


CORES = 2
COLUMNS = 2
PLANE = CORES * COLUMNS
EXTRA = 16
WINDOW = 4
MESSAGE = 40
IMAGES = 4


def after(value, *others):
    return lax.optimization_barrier((value,) + others)[0]


def whole(count, space=pltpu.VMEM):
    return [pl.BlockSpec(memory_space=space)] * count


def call(kernel, out_shape, in_specs, scratch=(), vmem=16, flops=0, moved=0):
    outs = out_shape if isinstance(out_shape, (list, tuple)) else [out_shape]
    specs = [pl.BlockSpec(memory_space=pltpu.VMEM)] * len(outs)
    return pl.pallas_call(
        kernel,
        out_shape=out_shape,
        in_specs=in_specs,
        out_specs=specs if isinstance(out_shape, (list, tuple)) else specs[0],
        scratch_shapes=list(scratch),
        compiler_params=pltpu.CompilerParams(vmem_limit_bytes=vmem * 2**20),
        cost_estimate=pl.CostEstimate(flops=flops, bytes_accessed=moved, transcendentals=0),
    )


def column_copies(half, targets, vision_ref, out_refs, sems):
    y, core = lax.axis_index("groups"), lax.rem(lax.axis_index("image"), CORES)
    copies = []
    for t, (core_flip, half_flip) in enumerate(targets):
        at_core = 1 - core if core_flip else core
        at_half = 1 - y if half_flip else y
        for p in range(out_refs[t].shape[1] // half):
            at = pl.multiple_of(((p * CORES + at_core) * 2 + at_half) * half, half)
            copies.append(
                pltpu.make_async_copy(
                    vision_ref.at[:, pl.ds(at, half)],
                    out_refs[t].at[:, p * half : (p + 1) * half],
                    sems.at[t, p],
                )
            )
    return copies


def send_kernel(half, targets, vision_ref, *refs):
    copies = column_copies(half, targets, vision_ref, refs[:-1], refs[-1])
    for copy in copies:
        copy.start()
    for copy in copies:
        copy.wait()


def send_columns(vision, half, targets):
    keys, depth = vision.shape
    pairs = depth // half // (2 * CORES)
    one = jax.ShapeDtypeStruct((keys, pairs * half), vision.dtype)
    count = len(targets)
    return pl.pallas_call(
        functools.partial(send_kernel, half, targets),
        out_shape=[one] * count,
        in_specs=whole(1, pl.ANY),
        out_specs=whole(count),
        scratch_shapes=[pltpu.SemaphoreType.DMA((count, pairs))],
        cost_estimate=pl.CostEstimate(flops=0, bytes_accessed=count * keys * depth, transcendentals=0),
    )(vision)


def prepare_kernel(
    half, text_ref, image_ref, tiles_ref, tenant_ref, page_ref, queries_ref, key_ref, value_ref, vision_ref,
    key_out, value_out, pair_out, diagonal_out, text, image, tiles, tenant, pages, line, sems, column_sems,
):
    start = pl.multiple_of(lax.axis_index("groups") * half, half)
    copies = [
        pltpu.make_async_copy(*pair, sems.at[i])
        for i, pair in enumerate(
            (
                (text_ref, text), (image_ref, image), (tiles_ref, tiles), (tenant_ref, tenant),
                (page_ref, pages), (queries_ref, line),
                (key_ref.at[pl.ds(start, half), :], key_out.at[0:half, :]),
                (value_ref.at[pl.ds(start, half), :], value_out),
            )
        )
    ]
    columns = column_copies(
        half, ((False, True), (True, True)), vision_ref, (pair_out, diagonal_out), column_sems
    )
    for copy in copies + columns:
        copy.start()
    for copy in copies:
        copy.wait()
    width = key_ref.shape[1]
    owner = image[0, 0]
    page = pages[tenant[owner]]
    row = lax.broadcasted_iota(jnp.int32, (EXTRA, width), 0)
    lane = lax.broadcasted_iota(jnp.int32, (EXTRA, width), 1)
    block = jnp.zeros((EXTRA, width), jnp.float32)
    for r in range(queries_ref.shape[1] // width):
        piece = line[0:1, r * width : (r + 1) * width].astype(jnp.float32)
        block = jnp.where(row == r, piece, block)
    for at, number in enumerate((text[0], owner, page, tiles[0])):
        block = jnp.where((row == 8) & (lane == at), number.astype(jnp.float32), block)
    key_out[half : half + EXTRA, :] = block.astype(key_out.dtype)
    for copy in columns:
        copy.wait()


def project_kernel(pieces, spots, images, own, arrays, adds, half, steps, *refs):
    vision_refs = refs[:images]
    weight_refs = refs[images : images + arrays]
    before = refs[images + arrays : images + arrays + adds]
    out_ref, slots, weights, sems = refs[images + arrays + adds :]
    me, y = lax.axis_index("image"), lax.axis_index("groups")
    z, x, core = me // PLANE, me // CORES % COLUMNS, me % CORES
    count = len(pieces)
    weight_copies = []
    image_copies = [[] for _ in range(images)]
    for p, (which, row) in enumerate(pieces):
        weight_copies.append(
            pltpu.make_async_copy(
                weight_refs[which].at[row : row + half, :],
                weights.at[p * half : (p + 1) * half, :],
                sems.at[images, p],
            )
        )
    for i in range(images):
        for p in range(count):
            d, mirrored = spots[p]
            pair = lax.rem(z + d, steps) * COLUMNS + (1 - x if mirrored else x)
            at = pl.multiple_of(((pair * CORES + core) * 2 + y if i == own else pair) * half, half)
            image_copies[i].append(
                pltpu.make_async_copy(
                    vision_refs[i].at[:, pl.ds(at, half)],
                    slots.at[i, :, p * half : (p + 1) * half],
                    sems.at[i, p],
                )
            )
    order = [weight_copies] + image_copies
    for group in order:
        for copy in group:
            copy.start()
    for copy in weight_copies:
        copy.wait()
    for i in range(images):
        for copy in image_copies[i]:
            copy.wait()
        product = jnp.dot(slots[i], weights[...], preferred_element_type=jnp.float32)
        out_ref[i] = before[0][i] + product if adds else product


def project(images, own, arrays, pieces, spots, half, steps, *before):
    keys = images[-1].shape[0]
    width = arrays[0].shape[1]
    count = len(pieces)
    number = len(images)
    return call(
        functools.partial(project_kernel, pieces, spots, number, own, len(arrays), len(before), half, steps),
        jax.ShapeDtypeStruct((number, keys, width), jnp.float32),
        whole(number + len(arrays), pl.ANY) + whole(len(before)),
        scratch=[
            pltpu.VMEM((number, keys, count * half), images[0].dtype),
            pltpu.VMEM((count * half, width), arrays[0].dtype),
            pltpu.SemaphoreType.DMA((number + 1, count)),
        ],
        vmem=16,
        flops=2 * number * keys * half * width * count,
        moved=count * half * (number * keys + width) * 2,
    )(*images, *arrays, *before)


def slot_of(token, me, steps):
    z, x, core = token // PLANE, token // CORES % COLUMNS, token % CORES
    mz, mx, mcore = me // PLANE, me // CORES % COLUMNS, me % CORES
    d = lax.rem(z - mz + steps, steps)
    across = jnp.where(core == mcore, 0, 1) * COLUMNS + jnp.where(x == mx, 0, 1)
    return across * steps + d


def pick_kernel(total, steps, rank, extras_ref, down_ref, out_ref, flat):
    me = lax.axis_index("image")
    flat[...] = down_ref[...].T
    for k in range(total):
        at = pl.multiple_of(slot_of(jnp.bitwise_xor(me, k), me, steps) * EXTRA, EXTRA)
        tile = extras_ref[pl.ds(at, EXTRA), 0:HEAD].astype(jnp.float32)
        page = tile[8, 2].astype(jnp.int32)
        out_ref[k] = flat[pl.ds(pl.multiple_of(page * rank, rank), rank), :]


def own_fact(extras_ref, lane):
    return extras_ref[0:EXTRA, 0:HEAD].astype(jnp.float32)[8, lane].astype(jnp.int32)


def lowrank_kernel(order, extras_ref, vision_ref, down_ref, up_ref, out_ref):
    shards, rank, rows = down_ref.shape
    total = jnp.zeros((vision_ref.shape[0], rank), jnp.float32)
    for j in range(shards):
        shard = jnp.bitwise_xor(lax.axis_index("image"), order[j])
        total = total + lax.dot_general(
            vision_ref[:, pl.ds(pl.multiple_of(shard * rows, rows), rows)],
            down_ref[j],
            (((1,), (1,)), ((), ())),
            preferred_element_type=jnp.float32,
        )
    page = own_fact(extras_ref, 2)
    out_ref[...] = jnp.dot(
        total.astype(jnp.bfloat16), up_ref[page], preferred_element_type=jnp.float32
    )


def window_start(extras_ref, owner, text_total):
    ids = extras_ref[:, 0:HEAD].astype(jnp.float32)
    row = lax.broadcasted_iota(jnp.int32, ids.shape, 0)
    lane = lax.broadcasted_iota(jnp.int32, ids.shape, 1)
    smaller = (row % EXTRA == 8) & (lane == 0) & (ids < owner.astype(jnp.float32))
    first = jnp.sum(jnp.where(smaller, 1.0, 0.0)).astype(jnp.int32)
    return jnp.minimum(first, text_total - WINDOW)


def select_rows(parts, rows):
    head = lax.broadcasted_iota(jnp.int32, parts[0].shape, 0) % 8 // 2
    result = parts[0]
    for k in range(1, KV_HEADS):
        result = jnp.where(head == k, parts[k], result)
    return result


def score_kernel(
    total, steps, mine_ref, core_ref, pair_ref, gain_ref, extras_ref, weights_ref, stats_ref
):
    me, owner = lax.axis_index("image"), own_fact(extras_ref, 1)
    keys = mine_ref.shape[1]
    first = window_start(extras_ref, owner, total)
    tiles = []
    match = []
    for s in range(WINDOW):
        at = pl.multiple_of(slot_of(first + s, me, steps) * EXTRA, EXTRA)
        block = extras_ref[pl.ds(at, EXTRA), :].astype(jnp.float32)
        tiles += [block[0:8, k * HEAD : (k + 1) * HEAD] for k in range(KV_HEADS)]
        match.append(block[8, 0].astype(jnp.int32) == owner)
    query = jnp.concatenate(tiles, axis=0).astype(jnp.bfloat16)
    key_raw = mine_ref[0] + core_ref[...] + pair_ref[...]
    gain = gain_ref[...]
    parts = []
    for k in range(KV_HEADS):
        head = key_raw[:, k * HEAD : (k + 1) * HEAD]
        scale = lax.rsqrt(jnp.mean(head * head, axis=1, keepdims=True) + epsilon)
        block = (head * scale * gain).astype(jnp.bfloat16)
        parts.append(
            lax.dot_general(query, block, (((1,), (1,)), ((), ())), preferred_element_type=jnp.float32)
        )
    scores = select_rows(parts, query.shape[0]) * HEAD ** (-0.5)
    row = lax.broadcasted_iota(jnp.int32, scores.shape, 0) // (8 * KV_HEADS)
    lane = lax.broadcasted_iota(jnp.int32, scores.shape, 1)
    limit = jnp.zeros(scores.shape, jnp.int32)
    slots = own_fact(extras_ref, 3) * (keys // TILES)
    for s in range(WINDOW):
        limit = jnp.where(row == s, jnp.where(match[s], slots, 0), limit)
    usable = lane < limit
    scores = jnp.where(usable, scores, masked_score)
    top = jnp.max(scores, axis=1, keepdims=True)
    weights = jnp.where(usable, jnp.exp(scores - top), 0.0).astype(jnp.bfloat16)
    weights_ref[...] = weights
    sums = jnp.sum(weights.astype(jnp.float32), axis=1, keepdims=True)
    rows = 8 * KV_HEADS
    eye = lax.broadcasted_iota(jnp.int32, (rows, HEAD), 0) == lax.broadcasted_iota(jnp.int32, (rows, HEAD), 1)
    line = lax.broadcasted_iota(jnp.int32, (8, HEAD), 0)
    for s in range(WINDOW):
        own = slice(s * rows, (s + 1) * rows)
        top_row = jnp.sum(jnp.where(eye, top[own], 0.0), axis=0, keepdims=True)
        sum_row = jnp.sum(jnp.where(eye, sums[own], 0.0), axis=0, keepdims=True)
        block = jnp.where(line == 0, top_row, jnp.where(line == 1, sum_row, 0.0))
        block = jnp.where(line == 2, first.astype(jnp.float32), block)
        stats_ref[s] = jnp.where(line == 3, jnp.where(match[s], 1.0, 0.0), block)


def value_kernel(steps, mine_ref, core_ref, pair_ref, lowrank_ref, weights_ref, stats_ref, *refs):
    out_refs, numerators = refs[:-1], refs[-1]
    me, first = lax.axis_index("image"), stats_ref[0][2, 0].astype(jnp.int32)
    value = (mine_ref[0] + core_ref[0] + pair_ref[...] + lowrank_ref[...]).astype(jnp.bfloat16)
    weights = weights_ref[...]
    parts = [
        jnp.dot(weights, value[:, k * HEAD : (k + 1) * HEAD], preferred_element_type=jnp.float32)
        for k in range(KV_HEADS)
    ]
    result = select_rows(parts, weights.shape[0])
    rows = 8 * KV_HEADS
    for s in range(WINDOW):
        numerators[s, 0:rows, :] = result[s * rows : (s + 1) * rows]
        numerators[s, rows:MESSAGE, :] = stats_ref[s]
    match = [stats_ref[s][3, 0] for s in range(WINDOW)]
    line = lax.broadcasted_iota(jnp.int32, (MESSAGE, HEAD), 0)
    empty = jnp.where(line == rows, masked_score, 0.0)
    group = lax.rem(me, PLANE)
    for k, out_ref in enumerate(out_refs):
        core, x = lax.rem(group, CORES), group // CORES
        to = (x if k < CORES else 1 - x) * CORES + (core if k % CORES == 0 else 1 - core)
        for z in range(steps):
            s = z * PLANE + to - first
            inside = (s >= 0) & (s < WINDOW)
            s = jnp.clip(s, 0, WINDOW - 1)
            good = match[0] > 0.5
            for j in range(1, WINDOW):
                good = jnp.where(s == j, match[j], jnp.where(good, 1.0, 0.0)) > 0.5
            good = inside & good
            out_ref[z] = jnp.where(good, numerators[s], empty)


def merge(blocks):
    rows = 8 * KV_HEADS
    tops = [b[rows : rows + 1] for b in blocks]
    top = functools.reduce(jnp.maximum, tops)
    eye = lax.broadcasted_iota(jnp.int32, (rows, HEAD), 0) == lax.broadcasted_iota(jnp.int32, (rows, HEAD), 1)
    numerator, total = 0.0, 0.0
    for b, t in zip(blocks, tops):
        scale = jnp.exp(t - top)
        total = total + scale * b[rows + 1 : rows + 2]
        column = jnp.sum(jnp.where(eye, scale, 0.0), axis=1, keepdims=True)
        numerator = numerator + column * b[0:rows]
    return numerator, top, total, eye


def plane_kernel(steps, *refs):
    in_refs, out_refs, merged = refs[:PLANE], refs[PLANE : PLANE + steps], refs[-1]
    rows = 8 * KV_HEADS
    line = lax.broadcasted_iota(jnp.int32, (8, HEAD), 0)
    for z in range(steps):
        numerator, top, total, _ = merge([ref[z] for ref in in_refs])
        merged[z, 0:rows, :] = numerator
        merged[z, rows:MESSAGE, :] = jnp.where(line == 0, top, jnp.where(line == 1, total, 0.0))
    for d, out_ref in enumerate(out_refs):
        out_ref[...] = merged[lax.rem(lax.axis_index("image") // PLANE + d, steps)]


def final_kernel(*refs):
    out_ref = refs[-1]
    numerator, top, total, eye = merge([ref[...] for ref in refs[:-1]])
    column = jnp.sum(jnp.where(eye, total, 0.0), axis=1, keepdims=True)
    out = numerator / column
    for k in range(KV_HEADS):
        for r in range(8):
            at = (r * KV_HEADS + k) * HEAD
            out_ref[:, at : at + HEAD] = out[8 * k + r : 8 * k + r + 1].astype(out_ref.dtype)


def local(
    devices,
    vision,
    queries,
    text_request,
    key_weight,
    value_weight,
    key_gain,
    down_pages,
    up_pages,
    image_request,
    image_tiles,
    request_tenant,
    tenant_page,
):
    steps = devices // PLANE
    me = lax.axis_index("image").astype(jnp.int32)
    y = lax.axis_index("groups").astype(jnp.int32)
    z, x, core = me // PLANE, me // CORES % COLUMNS, me % CORES
    tokens = vision[0]
    rows, width = key_weight.shape
    half = rows // 2
    rank = up_pages.shape[1]
    everyone = range(devices)

    def across(value, bits):
        return lax.ppermute(value, "image", [(i, i ^ bits) for i in everyone])

    def along(value, d):
        return lax.ppermute(value, "image", [(i, (i - PLANE * d) % devices) for i in everyone])

    def swap(value, bits=0):
        pairs = [(g * devices + i, (1 - g) * devices + (i ^ bits)) for g in range(2) for i in everyone]
        return lax.ppermute(value, ("groups", "image"), pairs)

    def join(*arrays):
        return jnp.concatenate(arrays, axis=0)

    step = half + EXTRA
    sent = jax.ShapeDtypeStruct((tokens.shape[0], tokens.shape[1] // 4), tokens.dtype)
    key_half, value_half, to_pair, to_diagonal = pl.pallas_call(
        functools.partial(prepare_kernel, half),
        out_shape=[
            jax.ShapeDtypeStruct((step, width), key_weight.dtype),
            jax.ShapeDtypeStruct((half, width), value_weight.dtype),
            sent,
            sent,
        ],
        in_specs=whole(9, pl.ANY),
        out_specs=whole(4),
        scratch_shapes=[
            pltpu.SMEM(text_request.shape, jnp.int32),
            pltpu.SMEM(image_request.shape, jnp.int32),
            pltpu.SMEM(image_tiles.shape, jnp.int32),
            pltpu.SMEM(request_tenant.shape, jnp.int32),
            pltpu.SMEM(tenant_page.shape, jnp.int32),
            pltpu.VMEM(queries.shape, queries.dtype),
            pltpu.SemaphoreType.DMA((8,)),
            pltpu.SemaphoreType.DMA((2, sent.shape[1] // half)),
        ],
    )(
        text_request, image_request, image_tiles, request_tenant, tenant_page, queries, key_weight,
        value_weight, tokens,
    )

    (to_core,) = send_columns(tokens, half, ((True, False),))
    from_pair = swap(to_pair)
    from_diagonal = swap(to_diagonal, 1)
    from_core = across(to_core, 1)

    k1, k3 = along(key_half, 1), along(key_half, 3)
    k_own = across(key_half, CORES)
    k2 = along(after(key_half, k1, k3, k_own), 2)
    kx = across(after(join(k1, k3), k_own), CORES)
    v_own = across(after(value_half, k_own), CORES)
    v1, v3 = along(after(value_half, k2, kx), 1), along(after(value_half, k2, kx), 3)
    kx2 = across(after(k2, kx), CORES)
    v2 = along(after(value_half, v1, v3), 2)
    vx = across(after(join(v1, v3), kx2), CORES)

    spots = [(d, mirrored) for mirrored in (False, True) for d in (0, 1, 3, 2)]
    near = join(key_half[half:], k1[half:], k2[half:], k3[half:], k_own[half:], kx[half:step], kx2[half:], kx[step + half :])
    extras = join(near, across(near, 1))
    images = [tokens, from_core, from_pair]
    arrays = [key_half, k_own, k1, k3, k2, kx, kx2]
    pieces = ((0, 0), (2, 0), (3, 0), (4, 0), (1, 0), (5, 0), (5, step), (6, 0))
    keys_part = project(images, 0, arrays, pieces, spots, half, steps)
    keys_core = across(keys_part[1], 1)
    late = project([from_diagonal], -1, [after(key_half, keys_part)] + arrays[1:], pieces, spots, half, steps)
    keys_sum = keys_part[2] + across(late[0], 1)
    vx2 = across(after(v2, keys_sum), CORES)
    keys_pair = [swap(keys_sum)]
    picked = call(
        functools.partial(pick_kernel, devices, steps, rank),
        jax.ShapeDtypeStruct((devices, rank, rows), down_pages.dtype),
        whole(2),
        scratch=[pltpu.VMEM(down_pages.shape[::-1], down_pages.dtype)],
    )(after(extras, keys_sum), down_pages)
    picked = picked.reshape(devices, 1, rank, rows)
    order = [0]
    pages = []
    while picked.shape[0] > 1:
        bit = picked.shape[0] // 2
        pages.append(across(picked[bit:], bit))
        picked = jnp.concatenate([picked[:bit], pages[-1]], axis=1)
        order = order + [k ^ bit for k in order]
    picked = picked.reshape(devices, rank, rows)
    lowrank = call(
        functools.partial(lowrank_kernel, tuple(order)),
        jax.ShapeDtypeStruct((tokens.shape[0], width), jnp.float32),
        whole(4),
        vmem=16,
        moved=tokens.size * 2,
    )(extras, tokens, picked, up_pages)

    pieces = ((0, 0), (2, 0), (3, 0), (4, 0), (1, 0), (5, 0), (5, half), (6, 0))
    near_values = after(value_half, keys_sum, pages[0])
    images = images + [from_diagonal]
    values_part = project(images, 0, [near_values, v_own, v1, v3, v2, vx], pieces[:-1], spots, half, steps)
    values_part = project(images, 0, [after(vx2, keys_pair[0], pages[1])], ((0, 0),), spots[-1:], half, steps, values_part)
    values_core = across(jnp.stack([values_part[1], values_part[3]]), 1)
    values_sum = (values_part[2] + values_core[1]).astype(jnp.bfloat16)
    values_pair = swap(values_sum)

    heads = WINDOW * 8 * KV_HEADS
    weights, stats = call(
        functools.partial(score_kernel, devices, steps),
        [
            jax.ShapeDtypeStruct((heads, tokens.shape[0]), jnp.bfloat16),
            jax.ShapeDtypeStruct((WINDOW, 8, HEAD), jnp.float32),
        ],
        whole(5),
    )(keys_part, keys_core, *keys_pair, key_gain.reshape(1, HEAD), extras)

    message = jax.ShapeDtypeStruct((steps, MESSAGE, HEAD), jnp.float32)
    messages = call(
        functools.partial(value_kernel, steps),
        [message] * PLANE,
        whole(6),
        scratch=[pltpu.VMEM((WINDOW, MESSAGE, HEAD), jnp.float32)],
    )(values_part, values_core, values_pair, lowrank, weights, stats)
    arrived = [messages[0]] + [across(messages[k], k) for k in range(1, PLANE)]
    one = jax.ShapeDtypeStruct((MESSAGE, HEAD), jnp.float32)
    merged = call(
        functools.partial(plane_kernel, steps),
        [one] * steps,
        whole(PLANE),
        scratch=[pltpu.VMEM((steps, MESSAGE, HEAD), jnp.float32)],
    )(*arrived)
    arrived = [merged[0]] + [along(merged[d], steps - d) for d in range(1, steps)]
    out = call(
        final_kernel,
        jax.ShapeDtypeStruct(queries.shape, jnp.bfloat16),
        whole(steps),
    )(*arrived)
    return out


def fits(mesh, vision, queries, key_weight):
    devices = mesh.shape["image"]
    rows = key_weight.shape[0] // devices
    own = queries.shape[0] // (mesh.shape["groups"] * devices)
    one = vision.shape[0] == mesh.shape["groups"] * devices
    return rows % 256 == 0 and devices == 4 * PLANE and mesh.shape["groups"] == 2 and own == 1 and one


def solution(mesh):
    in_specs = (
        P(("groups", "image"), None, None),
        P(("groups", "image"), None),
        P(("groups", "image")),
        P("image", None),
        P("image", None),
        P(),
        P("image", None),
        P(),
        P(("groups", "image"), None),
        P(("groups", "image")),
        P("groups"),
        P(),
    )
    out_specs = P(("groups", "image"), None)

    def run(*args):
        if fits(mesh, args[0], args[1], args[3]):
            body = functools.partial(local, mesh.shape["image"])
        else:
            body = local_gathered
        return jax.shard_map(body, mesh=mesh, in_specs=in_specs, out_specs=out_specs, check_vma=False)(*args)

    return run
```

```python
import functools

import jax
import jax.numpy as jnp
from jax import lax
from jax.experimental import pallas as pl
from jax.experimental.pallas import tpu as pltpu
from jax.sharding import PartitionSpec as P

HEAD = 128
KV_HEADS = 4
TILES = 4


epsilon = 1e-05
masked_score = -1e30


def select_entry(table, position):
    matches = jnp.arange(table.shape[0], dtype=jnp.int32) == position
    return jnp.sum(jnp.where(matches, table, 0))


def local_gathered(
    vision,
    queries,
    text_request,
    key_weight,
    value_weight,
    key_gain,
    down_pages,
    up_pages,
    image_request,
    image_tiles,
    request_tenant,
    tenant_page,
):
    image_tokens = vision[0]
    key_count = image_tokens.shape[0]
    kv_width = key_weight.shape[1]
    low_rank = up_pages.shape[1]
    owner_id = image_request[0, 0]
    tenant_id = select_entry(request_tenant, owner_id)
    page_id = select_entry(tenant_page, tenant_id)

    def token_columns():
        return image_tokens

    pieces = (
        lax.all_gather(key_weight, "image", axis=0, tiled=True),
        lax.all_gather(value_weight, "image", axis=0, tiled=True),
    )
    columns = token_columns()
    key_raw = jnp.dot(columns, pieces[0], preferred_element_type=jnp.float32)
    value_raw = jnp.dot(columns, pieces[1], preferred_element_type=jnp.float32)
    columns = token_columns()
    lowrank_sum = jnp.dot(
        columns,
        lax.dynamic_slice_in_dim(
            lax.all_gather(down_pages, "image", axis=0, tiled=True), page_id * low_rank, low_rank, 1
        ),
        preferred_element_type=jnp.float32,
    )
    lowrank = lowrank_sum.astype(jnp.bfloat16)
    up_factor = lax.dynamic_index_in_dim(up_pages, page_id, 0, keepdims=False)
    value_block = (
        value_raw + jnp.dot(lowrank, up_factor, preferred_element_type=jnp.float32)
    ).astype(jnp.bfloat16)
    key_heads = key_raw.reshape(key_count, KV_HEADS, HEAD)
    inverse_rms = lax.rsqrt(jnp.mean(key_heads * key_heads, axis=-1, keepdims=True) + epsilon)
    key_block = (
        (key_heads * inverse_rms * key_gain).reshape(key_count, kv_width).astype(jnp.bfloat16)
    )
    every_query, every_request = (
        lax.all_gather(queries, "image", axis=0, tiled=True),
        lax.all_gather(text_request, "image", axis=0, tiled=True),
    )
    text_total = every_query.shape[0]
    own_count = queries.shape[0]
    window = min(4 * own_count, text_total)
    head_group = every_query.shape[1] // kv_width
    q_count = KV_HEADS * head_group
    first_token = jnp.sum((every_request < owner_id).astype(jnp.int32))
    first_token = jnp.minimum(first_token, text_total - window)
    window_query = lax.dynamic_slice_in_dim(every_query, first_token, window, 0)
    window_request = lax.dynamic_slice_in_dim(every_request, first_token, window, 0)
    query_heads = window_query.reshape(window, KV_HEADS, head_group, HEAD)
    positions = jnp.arange(key_count, dtype=jnp.int32)
    usable = (window_request[:, None] == owner_id) & (
        positions[None, :] < image_tiles[0] * (key_count // TILES)
    )
    scores = jnp.einsum(
        "tkgd,vkd->tkgv",
        query_heads,
        key_block.reshape(key_count, KV_HEADS, HEAD),
        preferred_element_type=jnp.float32,
    ) * HEAD ** (-0.5)
    scores = jnp.where(usable[:, None, None, :], scores, masked_score)
    window_max = jnp.max(scores, axis=-1).reshape(window, q_count)
    every_max = lax.dynamic_update_slice_in_dim(
        jnp.full((text_total, q_count), masked_score, jnp.float32), window_max, first_token, 0
    )
    top_score = lax.pmax(every_max, "image")
    window_top = lax.dynamic_slice_in_dim(top_score, first_token, window, 0).reshape(
        window, KV_HEADS, head_group
    )
    weights = jnp.where(
        usable[:, None, None, :], jnp.exp(scores - window_top[..., None]), 0.0
    ).astype(jnp.bfloat16)
    totals = jnp.sum(weights, axis=-1, dtype=jnp.float32).reshape(window, q_count)
    numerator = jnp.einsum(
        "tkgv,vkd->tkgd",
        weights,
        value_block.reshape(key_count, KV_HEADS, HEAD),
        preferred_element_type=jnp.float32,
    ).reshape(window, q_count * HEAD)
    my_first = lax.axis_index("image") * own_count
    own_tokens = my_first + jnp.arange(own_count, dtype=jnp.int32)
    window_slots = jnp.arange(window, dtype=jnp.int32)
    start_value = first_token.astype(jnp.float32).reshape(1)
    pieces = (
        lax.all_gather(numerator, "image", axis=0, tiled=True),
        lax.all_gather(totals, "image", axis=0, tiled=True),
        lax.all_gather(start_value, "image", axis=0, tiled=True),
    )
    piece_count = pieces[2].shape[0]
    starts = pieces[2].astype(jnp.int32)
    offsets = own_tokens[None, :] - starts[:, None]
    chooser = (window_slots[None, None, :] == offsets[:, :, None]).astype(jnp.float32)
    numer_piece = pieces[0].reshape(piece_count, window, -1)
    totals_piece = pieces[1].reshape(piece_count, window, -1)
    numer_own = jnp.einsum("jrw,jwc->rc", chooser, numer_piece, precision=lax.Precision.HIGHEST)
    totals_own = jnp.einsum("jrw,jwc->rc", chooser, totals_piece, precision=lax.Precision.HIGHEST)
    attended = numer_own.reshape(own_count, -1, HEAD) / totals_own[..., None]
    return attended.reshape(own_count, -1).astype(jnp.bfloat16)


CORES = 2
COLUMNS = 2
PLANE = CORES * COLUMNS
EXTRA = 16
WINDOW = 4
MESSAGE = 40
IMAGES = 4


def after(value, *others):
    return lax.optimization_barrier((value,) + others)[0]


def whole(count, space=pltpu.VMEM):
    return [pl.BlockSpec(memory_space=space)] * count


def call(kernel, out_shape, in_specs, scratch=(), vmem=16, flops=0, moved=0):
    outs = out_shape if isinstance(out_shape, (list, tuple)) else [out_shape]
    specs = [pl.BlockSpec(memory_space=pltpu.VMEM)] * len(outs)
    return pl.pallas_call(
        kernel,
        out_shape=out_shape,
        in_specs=in_specs,
        out_specs=specs if isinstance(out_shape, (list, tuple)) else specs[0],
        scratch_shapes=list(scratch),
        compiler_params=pltpu.CompilerParams(vmem_limit_bytes=vmem * 2**20),
        cost_estimate=pl.CostEstimate(flops=flops, bytes_accessed=moved, transcendentals=0),
    )


def column_copies(half, targets, vision_ref, out_refs, sems):
    y, core = lax.axis_index("groups"), lax.rem(lax.axis_index("image"), CORES)
    copies = []
    for t, (core_flip, half_flip) in enumerate(targets):
        at_core = 1 - core if core_flip else core
        at_half = 1 - y if half_flip else y
        for p in range(out_refs[t].shape[1] // half):
            at = pl.multiple_of(((p * CORES + at_core) * 2 + at_half) * half, half)
            copies.append(
                pltpu.make_async_copy(
                    vision_ref.at[:, pl.ds(at, half)],
                    out_refs[t].at[:, p * half : (p + 1) * half],
                    sems.at[t, p],
                )
            )
    return copies


def send_kernel(half, targets, vision_ref, *refs):
    copies = column_copies(half, targets, vision_ref, refs[:-1], refs[-1])
    for copy in copies:
        copy.start()
    for copy in copies:
        copy.wait()


def send_columns(vision, half, targets):
    keys, depth = vision.shape
    pairs = depth // half // (2 * CORES)
    one = jax.ShapeDtypeStruct((keys, pairs * half), vision.dtype)
    count = len(targets)
    return pl.pallas_call(
        functools.partial(send_kernel, half, targets),
        out_shape=[one] * count,
        in_specs=whole(1, pl.ANY),
        out_specs=whole(count),
        scratch_shapes=[pltpu.SemaphoreType.DMA((count, pairs))],
        cost_estimate=pl.CostEstimate(flops=0, bytes_accessed=count * keys * depth, transcendentals=0),
    )(vision)


def prepare_kernel(
    half, text_ref, image_ref, tiles_ref, tenant_ref, page_ref, queries_ref, key_ref, value_ref, vision_ref,
    key_out, value_out, pair_out, diagonal_out, text, image, tiles, tenant, pages, line, sems, column_sems,
):
    start = pl.multiple_of(lax.axis_index("groups") * half, half)
    copies = [
        pltpu.make_async_copy(*pair, sems.at[i])
        for i, pair in enumerate(
            (
                (text_ref, text), (image_ref, image), (tiles_ref, tiles), (tenant_ref, tenant),
                (page_ref, pages), (queries_ref, line),
                (key_ref.at[pl.ds(start, half), :], key_out.at[0:half, :]),
                (value_ref.at[pl.ds(start, half), :], value_out),
            )
        )
    ]
    columns = column_copies(
        half, ((False, True), (True, True)), vision_ref, (pair_out, diagonal_out), column_sems
    )
    for copy in copies + columns:
        copy.start()
    for copy in copies:
        copy.wait()
    width = key_ref.shape[1]
    owner = image[0, 0]
    page = pages[tenant[owner]]
    row = lax.broadcasted_iota(jnp.int32, (EXTRA, width), 0)
    lane = lax.broadcasted_iota(jnp.int32, (EXTRA, width), 1)
    block = jnp.zeros((EXTRA, width), jnp.float32)
    for r in range(queries_ref.shape[1] // width):
        piece = line[0:1, r * width : (r + 1) * width].astype(jnp.float32)
        block = jnp.where(row == r, piece, block)
    for at, number in enumerate((text[0], owner, page, tiles[0])):
        block = jnp.where((row == 8) & (lane == at), number.astype(jnp.float32), block)
    key_out[half : half + EXTRA, :] = block.astype(key_out.dtype)
    for copy in columns:
        copy.wait()


def project_kernel(pieces, spots, images, own, arrays, adds, half, steps, *refs):
    vision_refs = refs[:images]
    weight_refs = refs[images : images + arrays]
    before = refs[images + arrays : images + arrays + adds]
    out_ref, slots, weights, sems = refs[images + arrays + adds :]
    me, y = lax.axis_index("image"), lax.axis_index("groups")
    z, x, core = me // PLANE, me // CORES % COLUMNS, me % CORES
    count = len(pieces)
    weight_copies = []
    image_copies = [[] for _ in range(images)]
    for p, (which, row) in enumerate(pieces):
        weight_copies.append(
            pltpu.make_async_copy(
                weight_refs[which].at[row : row + half, :],
                weights.at[p * half : (p + 1) * half, :],
                sems.at[images, p],
            )
        )
    for i in range(images):
        for p in range(count):
            d, mirrored = spots[p]
            pair = lax.rem(z + d, steps) * COLUMNS + (1 - x if mirrored else x)
            at = pl.multiple_of(((pair * CORES + core) * 2 + y if i == own else pair) * half, half)
            image_copies[i].append(
                pltpu.make_async_copy(
                    vision_refs[i].at[:, pl.ds(at, half)],
                    slots.at[i, :, p * half : (p + 1) * half],
                    sems.at[i, p],
                )
            )
    order = [weight_copies] + image_copies
    for group in order:
        for copy in group:
            copy.start()
    for copy in weight_copies:
        copy.wait()
    for i in range(images):
        for copy in image_copies[i]:
            copy.wait()
        product = jnp.dot(slots[i], weights[...], preferred_element_type=jnp.float32)
        out_ref[i] = before[0][i] + product if adds else product


def project(images, own, arrays, pieces, spots, half, steps, *before):
    keys = images[-1].shape[0]
    width = arrays[0].shape[1]
    count = len(pieces)
    number = len(images)
    return call(
        functools.partial(project_kernel, pieces, spots, number, own, len(arrays), len(before), half, steps),
        jax.ShapeDtypeStruct((number, keys, width), jnp.float32),
        whole(number + len(arrays), pl.ANY) + whole(len(before)),
        scratch=[
            pltpu.VMEM((number, keys, count * half), images[0].dtype),
            pltpu.VMEM((count * half, width), arrays[0].dtype),
            pltpu.SemaphoreType.DMA((number + 1, count)),
        ],
        vmem=16,
        flops=2 * number * keys * half * width * count,
        moved=count * half * (number * keys + width) * 2,
    )(*images, *arrays, *before)


def slot_of(token, me, steps):
    z, x, core = token // PLANE, token // CORES % COLUMNS, token % CORES
    mz, mx, mcore = me // PLANE, me // CORES % COLUMNS, me % CORES
    d = lax.rem(z - mz + steps, steps)
    across = jnp.where(core == mcore, 0, 1) * COLUMNS + jnp.where(x == mx, 0, 1)
    return across * steps + d


def pick_kernel(total, steps, rank, extras_ref, down_ref, out_ref, flat):
    me = lax.axis_index("image")
    flat[...] = down_ref[...].T
    for k in range(total):
        at = pl.multiple_of(slot_of(jnp.bitwise_xor(me, k), me, steps) * EXTRA, EXTRA)
        tile = extras_ref[pl.ds(at, EXTRA), 0:HEAD].astype(jnp.float32)
        page = tile[8, 2].astype(jnp.int32)
        out_ref[k] = flat[pl.ds(pl.multiple_of(page * rank, rank), rank), :]


def own_fact(extras_ref, lane):
    return extras_ref[0:EXTRA, 0:HEAD].astype(jnp.float32)[8, lane].astype(jnp.int32)


def lowrank_kernel(order, extras_ref, vision_ref, down_ref, up_ref, out_ref):
    shards, rank, rows = down_ref.shape
    total = jnp.zeros((vision_ref.shape[0], rank), jnp.float32)
    for j in range(shards):
        shard = jnp.bitwise_xor(lax.axis_index("image"), order[j])
        total = total + lax.dot_general(
            vision_ref[:, pl.ds(pl.multiple_of(shard * rows, rows), rows)],
            down_ref[j],
            (((1,), (1,)), ((), ())),
            preferred_element_type=jnp.float32,
        )
    page = own_fact(extras_ref, 2)
    out_ref[...] = jnp.dot(
        total.astype(jnp.bfloat16), up_ref[page], preferred_element_type=jnp.float32
    )


def window_start(extras_ref, owner, text_total):
    ids = extras_ref[:, 0:HEAD].astype(jnp.float32)
    row = lax.broadcasted_iota(jnp.int32, ids.shape, 0)
    lane = lax.broadcasted_iota(jnp.int32, ids.shape, 1)
    smaller = (row % EXTRA == 8) & (lane == 0) & (ids < owner.astype(jnp.float32))
    first = jnp.sum(jnp.where(smaller, 1.0, 0.0)).astype(jnp.int32)
    return jnp.minimum(first, text_total - WINDOW)


def select_rows(parts, rows):
    head = lax.broadcasted_iota(jnp.int32, parts[0].shape, 0) % 8 // 2
    result = parts[0]
    for k in range(1, KV_HEADS):
        result = jnp.where(head == k, parts[k], result)
    return result


def score_kernel(
    total, steps, mine_ref, core_ref, pair_ref, gain_ref, extras_ref, weights_ref, stats_ref
):
    me, owner = lax.axis_index("image"), own_fact(extras_ref, 1)
    keys = mine_ref.shape[1]
    first = window_start(extras_ref, owner, total)
    tiles = []
    match = []
    for s in range(WINDOW):
        at = pl.multiple_of(slot_of(first + s, me, steps) * EXTRA, EXTRA)
        block = extras_ref[pl.ds(at, EXTRA), :].astype(jnp.float32)
        tiles += [block[0:8, k * HEAD : (k + 1) * HEAD] for k in range(KV_HEADS)]
        match.append(block[8, 0].astype(jnp.int32) == owner)
    query = jnp.concatenate(tiles, axis=0).astype(jnp.bfloat16)
    key_raw = mine_ref[0] + core_ref[...] + pair_ref[...]
    gain = gain_ref[...]
    parts = []
    for k in range(KV_HEADS):
        head = key_raw[:, k * HEAD : (k + 1) * HEAD]
        scale = lax.rsqrt(jnp.mean(head * head, axis=1, keepdims=True) + epsilon)
        block = (head * scale * gain).astype(jnp.bfloat16)
        parts.append(
            lax.dot_general(query, block, (((1,), (1,)), ((), ())), preferred_element_type=jnp.float32)
        )
    scores = select_rows(parts, query.shape[0]) * HEAD ** (-0.5)
    row = lax.broadcasted_iota(jnp.int32, scores.shape, 0) // (8 * KV_HEADS)
    lane = lax.broadcasted_iota(jnp.int32, scores.shape, 1)
    limit = jnp.zeros(scores.shape, jnp.int32)
    slots = own_fact(extras_ref, 3) * (keys // TILES)
    for s in range(WINDOW):
        limit = jnp.where(row == s, jnp.where(match[s], slots, 0), limit)
    usable = lane < limit
    scores = jnp.where(usable, scores, masked_score)
    top = jnp.max(scores, axis=1, keepdims=True)
    weights = jnp.where(usable, jnp.exp(scores - top), 0.0).astype(jnp.bfloat16)
    weights_ref[...] = weights
    sums = jnp.sum(weights.astype(jnp.float32), axis=1, keepdims=True)
    rows = 8 * KV_HEADS
    eye = lax.broadcasted_iota(jnp.int32, (rows, HEAD), 0) == lax.broadcasted_iota(jnp.int32, (rows, HEAD), 1)
    line = lax.broadcasted_iota(jnp.int32, (8, HEAD), 0)
    for s in range(WINDOW):
        own = slice(s * rows, (s + 1) * rows)
        top_row = jnp.sum(jnp.where(eye, top[own], 0.0), axis=0, keepdims=True)
        sum_row = jnp.sum(jnp.where(eye, sums[own], 0.0), axis=0, keepdims=True)
        block = jnp.where(line == 0, top_row, jnp.where(line == 1, sum_row, 0.0))
        block = jnp.where(line == 2, first.astype(jnp.float32), block)
        stats_ref[s] = jnp.where(line == 3, jnp.where(match[s], 1.0, 0.0), block)


def value_kernel(steps, mine_ref, core_ref, pair_ref, lowrank_ref, weights_ref, stats_ref, *refs):
    out_refs, numerators = refs[:-1], refs[-1]
    me, first = lax.axis_index("image"), stats_ref[0][2, 0].astype(jnp.int32)
    value = (mine_ref[0] + core_ref[0] + pair_ref[...] + lowrank_ref[...]).astype(jnp.bfloat16)
    weights = weights_ref[...]
    parts = [
        jnp.dot(weights, value[:, k * HEAD : (k + 1) * HEAD], preferred_element_type=jnp.float32)
        for k in range(KV_HEADS)
    ]
    result = select_rows(parts, weights.shape[0])
    rows = 8 * KV_HEADS
    for s in range(WINDOW):
        numerators[s, 0:rows, :] = result[s * rows : (s + 1) * rows]
        numerators[s, rows:MESSAGE, :] = stats_ref[s]
    match = [stats_ref[s][3, 0] for s in range(WINDOW)]
    line = lax.broadcasted_iota(jnp.int32, (MESSAGE, HEAD), 0)
    empty = jnp.where(line == rows, masked_score, 0.0)
    group = lax.rem(me, PLANE)
    for k, out_ref in enumerate(out_refs):
        core, x = lax.rem(group, CORES), group // CORES
        to = (x if k < CORES else 1 - x) * CORES + (core if k % CORES == 0 else 1 - core)
        for z in range(steps):
            s = z * PLANE + to - first
            inside = (s >= 0) & (s < WINDOW)
            s = jnp.clip(s, 0, WINDOW - 1)
            good = match[0] > 0.5
            for j in range(1, WINDOW):
                good = jnp.where(s == j, match[j], jnp.where(good, 1.0, 0.0)) > 0.5
            good = inside & good
            out_ref[z] = jnp.where(good, numerators[s], empty)


def merge(blocks):
    rows = 8 * KV_HEADS
    tops = [b[rows : rows + 1] for b in blocks]
    top = functools.reduce(jnp.maximum, tops)
    eye = lax.broadcasted_iota(jnp.int32, (rows, HEAD), 0) == lax.broadcasted_iota(jnp.int32, (rows, HEAD), 1)
    numerator, total = 0.0, 0.0
    for b, t in zip(blocks, tops):
        scale = jnp.exp(t - top)
        total = total + scale * b[rows + 1 : rows + 2]
        column = jnp.sum(jnp.where(eye, scale, 0.0), axis=1, keepdims=True)
        numerator = numerator + column * b[0:rows]
    return numerator, top, total, eye


def plane_kernel(steps, *refs):
    in_refs, out_refs, merged = refs[:PLANE], refs[PLANE : PLANE + steps], refs[-1]
    rows = 8 * KV_HEADS
    line = lax.broadcasted_iota(jnp.int32, (8, HEAD), 0)
    for z in range(steps):
        numerator, top, total, _ = merge([ref[z] for ref in in_refs])
        merged[z, 0:rows, :] = numerator
        merged[z, rows:MESSAGE, :] = jnp.where(line == 0, top, jnp.where(line == 1, total, 0.0))
    for d, out_ref in enumerate(out_refs):
        out_ref[...] = merged[lax.rem(lax.axis_index("image") // PLANE + d, steps)]


def final_kernel(*refs):
    out_ref = refs[-1]
    numerator, top, total, eye = merge([ref[...] for ref in refs[:-1]])
    column = jnp.sum(jnp.where(eye, total, 0.0), axis=1, keepdims=True)
    out = numerator / column
    for k in range(KV_HEADS):
        for r in range(8):
            at = (r * KV_HEADS + k) * HEAD
            out_ref[:, at : at + HEAD] = out[8 * k + r : 8 * k + r + 1].astype(out_ref.dtype)


def local(
    devices,
    vision,
    queries,
    text_request,
    key_weight,
    value_weight,
    key_gain,
    down_pages,
    up_pages,
    image_request,
    image_tiles,
    request_tenant,
    tenant_page,
):
    steps = devices // PLANE
    me = lax.axis_index("image").astype(jnp.int32)
    y = lax.axis_index("groups").astype(jnp.int32)
    z, x, core = me // PLANE, me // CORES % COLUMNS, me % CORES
    tokens = vision[0]
    rows, width = key_weight.shape
    half = rows // 2
    rank = up_pages.shape[1]
    everyone = range(devices)

    def across(value, bits):
        return lax.ppermute(value, "image", [(i, i ^ bits) for i in everyone])

    def along(value, d):
        return lax.ppermute(value, "image", [(i, (i - PLANE * d) % devices) for i in everyone])

    def swap(value, bits=0):
        pairs = [(g * devices + i, (1 - g) * devices + (i ^ bits)) for g in range(2) for i in everyone]
        return lax.ppermute(value, ("groups", "image"), pairs)

    def join(*arrays):
        return jnp.concatenate(arrays, axis=0)

    step = half + EXTRA
    sent = jax.ShapeDtypeStruct((tokens.shape[0], tokens.shape[1] // 4), tokens.dtype)
    key_half, value_half, to_pair, to_diagonal = pl.pallas_call(
        functools.partial(prepare_kernel, half),
        out_shape=[
            jax.ShapeDtypeStruct((step, width), key_weight.dtype),
            jax.ShapeDtypeStruct((half, width), value_weight.dtype),
            sent,
            sent,
        ],
        in_specs=whole(9, pl.ANY),
        out_specs=whole(4),
        scratch_shapes=[
            pltpu.SMEM(text_request.shape, jnp.int32),
            pltpu.SMEM(image_request.shape, jnp.int32),
            pltpu.SMEM(image_tiles.shape, jnp.int32),
            pltpu.SMEM(request_tenant.shape, jnp.int32),
            pltpu.SMEM(tenant_page.shape, jnp.int32),
            pltpu.VMEM(queries.shape, queries.dtype),
            pltpu.SemaphoreType.DMA((8,)),
            pltpu.SemaphoreType.DMA((2, sent.shape[1] // half)),
        ],
    )(
        text_request, image_request, image_tiles, request_tenant, tenant_page, queries, key_weight,
        value_weight, tokens,
    )

    (to_core,) = send_columns(tokens, half, ((True, False),))
    from_pair = swap(to_pair)
    from_diagonal = swap(to_diagonal, 1)
    from_core = across(to_core, 1)

    k1, k3 = along(key_half, 1), along(key_half, 3)
    k_own = across(key_half, CORES)
    k2 = along(after(key_half, k1, k3, k_own), 2)
    kx = across(after(join(k1, k3), k_own), CORES)
    v1, v3 = along(after(value_half, k2, kx, from_core), 1), along(after(value_half, k2, kx, from_core), 3)
    kx2 = across(after(join(k2, value_half), kx), CORES)
    v2 = along(after(value_half, v1, v3), 2)
    vx = across(after(join(v1, v3), kx2), CORES)

    spots = [(d, mirrored) for mirrored in (False, True) for d in (0, 1, 3, 2)]
    near = join(key_half[half:], k1[half:], k2[half:], k3[half:], k_own[half:], kx[half:step], kx2[half:step], kx[step + half :])
    images = [tokens, from_core, from_pair]
    arrays = [key_half, k_own, k1, k3, k2, kx, kx2]
    pieces = ((0, 0), (2, 0), (3, 0), (4, 0), (1, 0), (5, 0), (5, step), (6, 0))
    keys_part = project(images, 0, arrays, pieces, spots, half, steps)
    keys_core = across(keys_part[1], 1)
    late = project([from_diagonal], -1, [after(key_half, keys_part)] + arrays[1:], pieces, spots, half, steps)
    keys_sum = keys_part[2] + across(late[0], 1)
    vx2 = across(after(v2, keys_sum), CORES)
    keys_pair = [swap(keys_sum)]
    extras = join(near, across(after(near, keys_sum), 1))
    picked = call(
        functools.partial(pick_kernel, devices, steps, rank),
        jax.ShapeDtypeStruct((devices, rank, rows), down_pages.dtype),
        whole(2),
        scratch=[pltpu.VMEM(down_pages.shape[::-1], down_pages.dtype)],
    )(after(extras, keys_sum), down_pages)
    picked = picked.reshape(devices, 1, rank, rows)
    order = [0]
    pages = []
    while picked.shape[0] > 1:
        bit = picked.shape[0] // 2
        pages.append(across(picked[bit:], bit))
        picked = jnp.concatenate([picked[:bit], pages[-1]], axis=1)
        order = order + [k ^ bit for k in order]
    picked = picked.reshape(devices, rank, rows)
    lowrank = call(
        functools.partial(lowrank_kernel, tuple(order)),
        jax.ShapeDtypeStruct((tokens.shape[0], width), jnp.float32),
        whole(4),
        vmem=16,
        moved=tokens.size * 2,
    )(extras, tokens, picked, up_pages)

    pieces = ((0, 0), (2, 0), (3, 0), (4, 0), (1, step), (5, 0), (5, half), (6, 0))
    near_values = after(value_half, keys_sum, pages[0])
    images = images + [from_diagonal]
    values_part = project(images, 0, [near_values, kx2, v1, v3, v2, vx], pieces[:-1], spots, half, steps)
    values_part = project(images, 0, [after(vx2, keys_pair[0], pages[1])], ((0, 0),), spots[-1:], half, steps, values_part)
    values_core = across(jnp.stack([values_part[1], values_part[3]]), 1)
    values_sum = (values_part[2] + values_core[1]).astype(jnp.bfloat16)
    values_pair = swap(values_sum)

    heads = WINDOW * 8 * KV_HEADS
    weights, stats = call(
        functools.partial(score_kernel, devices, steps),
        [
            jax.ShapeDtypeStruct((heads, tokens.shape[0]), jnp.bfloat16),
            jax.ShapeDtypeStruct((WINDOW, 8, HEAD), jnp.float32),
        ],
        whole(5),
    )(keys_part, keys_core, *keys_pair, key_gain.reshape(1, HEAD), extras)

    message = jax.ShapeDtypeStruct((steps, MESSAGE, HEAD), jnp.float32)
    messages = call(
        functools.partial(value_kernel, steps),
        [message] * PLANE,
        whole(6),
        scratch=[pltpu.VMEM((WINDOW, MESSAGE, HEAD), jnp.float32)],
    )(values_part, values_core, values_pair, lowrank, weights, stats)
    arrived = [messages[0]] + [across(messages[k], k) for k in range(1, PLANE)]
    one = jax.ShapeDtypeStruct((MESSAGE, HEAD), jnp.float32)
    merged = call(
        functools.partial(plane_kernel, steps),
        [one] * steps,
        whole(PLANE),
        scratch=[pltpu.VMEM((steps, MESSAGE, HEAD), jnp.float32)],
    )(*arrived)
    arrived = [merged[0]] + [along(merged[d], steps - d) for d in range(1, steps)]
    out = call(
        final_kernel,
        jax.ShapeDtypeStruct(queries.shape, jnp.bfloat16),
        whole(steps),
    )(*arrived)
    return out


def fits(mesh, vision, queries, key_weight):
    devices = mesh.shape["image"]
    rows = key_weight.shape[0] // devices
    own = queries.shape[0] // (mesh.shape["groups"] * devices)
    one = vision.shape[0] == mesh.shape["groups"] * devices
    return rows % 256 == 0 and devices == 4 * PLANE and mesh.shape["groups"] == 2 and own == 1 and one


def solution(mesh):
    in_specs = (
        P(("groups", "image"), None, None),
        P(("groups", "image"), None),
        P(("groups", "image")),
        P("image", None),
        P("image", None),
        P(),
        P("image", None),
        P(),
        P(("groups", "image"), None),
        P(("groups", "image")),
        P("groups"),
        P(),
    )
    out_specs = P(("groups", "image"), None)

    def run(*args):
        if fits(mesh, args[0], args[1], args[3]):
            body = functools.partial(local, mesh.shape["image"])
        else:
            body = local_gathered
        return jax.shard_map(body, mesh=mesh, in_specs=in_specs, out_specs=out_specs, check_vma=False)(*args)

    return run
```

```python
import functools

import jax
import jax.numpy as jnp
from jax import lax
from jax.experimental import pallas as pl
from jax.experimental.pallas import tpu as pltpu
from jax.sharding import PartitionSpec as P

HEAD = 128
KV_HEADS = 4
TILES = 4


epsilon = 1e-05
masked_score = -1e30


def select_entry(table, position):
    matches = jnp.arange(table.shape[0], dtype=jnp.int32) == position
    return jnp.sum(jnp.where(matches, table, 0))


def local_gathered(
    vision,
    queries,
    text_request,
    key_weight,
    value_weight,
    key_gain,
    down_pages,
    up_pages,
    image_request,
    image_tiles,
    request_tenant,
    tenant_page,
):
    image_tokens = vision[0]
    key_count = image_tokens.shape[0]
    kv_width = key_weight.shape[1]
    low_rank = up_pages.shape[1]
    owner_id = image_request[0, 0]
    tenant_id = select_entry(request_tenant, owner_id)
    page_id = select_entry(tenant_page, tenant_id)

    def token_columns():
        return image_tokens

    pieces = (
        lax.all_gather(key_weight, "image", axis=0, tiled=True),
        lax.all_gather(value_weight, "image", axis=0, tiled=True),
    )
    columns = token_columns()
    key_raw = jnp.dot(columns, pieces[0], preferred_element_type=jnp.float32)
    value_raw = jnp.dot(columns, pieces[1], preferred_element_type=jnp.float32)
    columns = token_columns()
    lowrank_sum = jnp.dot(
        columns,
        lax.dynamic_slice_in_dim(
            lax.all_gather(down_pages, "image", axis=0, tiled=True), page_id * low_rank, low_rank, 1
        ),
        preferred_element_type=jnp.float32,
    )
    lowrank = lowrank_sum.astype(jnp.bfloat16)
    up_factor = lax.dynamic_index_in_dim(up_pages, page_id, 0, keepdims=False)
    value_block = (
        value_raw + jnp.dot(lowrank, up_factor, preferred_element_type=jnp.float32)
    ).astype(jnp.bfloat16)
    key_heads = key_raw.reshape(key_count, KV_HEADS, HEAD)
    inverse_rms = lax.rsqrt(jnp.mean(key_heads * key_heads, axis=-1, keepdims=True) + epsilon)
    key_block = (
        (key_heads * inverse_rms * key_gain).reshape(key_count, kv_width).astype(jnp.bfloat16)
    )
    every_query, every_request = (
        lax.all_gather(queries, "image", axis=0, tiled=True),
        lax.all_gather(text_request, "image", axis=0, tiled=True),
    )
    text_total = every_query.shape[0]
    own_count = queries.shape[0]
    window = min(4 * own_count, text_total)
    head_group = every_query.shape[1] // kv_width
    q_count = KV_HEADS * head_group
    first_token = jnp.sum((every_request < owner_id).astype(jnp.int32))
    first_token = jnp.minimum(first_token, text_total - window)
    window_query = lax.dynamic_slice_in_dim(every_query, first_token, window, 0)
    window_request = lax.dynamic_slice_in_dim(every_request, first_token, window, 0)
    query_heads = window_query.reshape(window, KV_HEADS, head_group, HEAD)
    positions = jnp.arange(key_count, dtype=jnp.int32)
    usable = (window_request[:, None] == owner_id) & (
        positions[None, :] < image_tiles[0] * (key_count // TILES)
    )
    scores = jnp.einsum(
        "tkgd,vkd->tkgv",
        query_heads,
        key_block.reshape(key_count, KV_HEADS, HEAD),
        preferred_element_type=jnp.float32,
    ) * HEAD ** (-0.5)
    scores = jnp.where(usable[:, None, None, :], scores, masked_score)
    window_max = jnp.max(scores, axis=-1).reshape(window, q_count)
    every_max = lax.dynamic_update_slice_in_dim(
        jnp.full((text_total, q_count), masked_score, jnp.float32), window_max, first_token, 0
    )
    top_score = lax.pmax(every_max, "image")
    window_top = lax.dynamic_slice_in_dim(top_score, first_token, window, 0).reshape(
        window, KV_HEADS, head_group
    )
    weights = jnp.where(
        usable[:, None, None, :], jnp.exp(scores - window_top[..., None]), 0.0
    ).astype(jnp.bfloat16)
    totals = jnp.sum(weights, axis=-1, dtype=jnp.float32).reshape(window, q_count)
    numerator = jnp.einsum(
        "tkgv,vkd->tkgd",
        weights,
        value_block.reshape(key_count, KV_HEADS, HEAD),
        preferred_element_type=jnp.float32,
    ).reshape(window, q_count * HEAD)
    my_first = lax.axis_index("image") * own_count
    own_tokens = my_first + jnp.arange(own_count, dtype=jnp.int32)
    window_slots = jnp.arange(window, dtype=jnp.int32)
    start_value = first_token.astype(jnp.float32).reshape(1)
    pieces = (
        lax.all_gather(numerator, "image", axis=0, tiled=True),
        lax.all_gather(totals, "image", axis=0, tiled=True),
        lax.all_gather(start_value, "image", axis=0, tiled=True),
    )
    piece_count = pieces[2].shape[0]
    starts = pieces[2].astype(jnp.int32)
    offsets = own_tokens[None, :] - starts[:, None]
    chooser = (window_slots[None, None, :] == offsets[:, :, None]).astype(jnp.float32)
    numer_piece = pieces[0].reshape(piece_count, window, -1)
    totals_piece = pieces[1].reshape(piece_count, window, -1)
    numer_own = jnp.einsum("jrw,jwc->rc", chooser, numer_piece, precision=lax.Precision.HIGHEST)
    totals_own = jnp.einsum("jrw,jwc->rc", chooser, totals_piece, precision=lax.Precision.HIGHEST)
    attended = numer_own.reshape(own_count, -1, HEAD) / totals_own[..., None]
    return attended.reshape(own_count, -1).astype(jnp.bfloat16)


CORES = 2
COLUMNS = 2
PLANE = CORES * COLUMNS
EXTRA = 16
WINDOW = 4
MESSAGE = 40
NARROW = 48
IMAGES = 4


def after(value, *others):
    return lax.optimization_barrier((value,) + others)[0]


def whole(count, space=pltpu.VMEM):
    return [pl.BlockSpec(memory_space=space)] * count


def call(kernel, out_shape, in_specs, scratch=(), vmem=16, flops=0, moved=0):
    outs = out_shape if isinstance(out_shape, (list, tuple)) else [out_shape]
    specs = [pl.BlockSpec(memory_space=pltpu.VMEM)] * len(outs)
    return pl.pallas_call(
        kernel,
        out_shape=out_shape,
        in_specs=in_specs,
        out_specs=specs if isinstance(out_shape, (list, tuple)) else specs[0],
        scratch_shapes=list(scratch),
        compiler_params=pltpu.CompilerParams(vmem_limit_bytes=vmem * 2**20),
        cost_estimate=pl.CostEstimate(flops=flops, bytes_accessed=moved, transcendentals=0),
    )


def column_copies(half, targets, vision_ref, out_refs, sems):
    y, core = lax.axis_index("groups"), lax.rem(lax.axis_index("image"), CORES)
    copies = []
    for t, (core_flip, half_flip) in enumerate(targets):
        at_core = 1 - core if core_flip else core
        at_half = 1 - y if half_flip else y
        for p in range(out_refs[t].shape[1] // half):
            at = pl.multiple_of(((p * CORES + at_core) * 2 + at_half) * half, half)
            copies.append(
                pltpu.make_async_copy(
                    vision_ref.at[:, pl.ds(at, half)],
                    out_refs[t].at[:, p * half : (p + 1) * half],
                    sems.at[t, p],
                )
            )
    return copies


def send_kernel(half, targets, vision_ref, *refs):
    copies = column_copies(half, targets, vision_ref, refs[:-1], refs[-1])
    for copy in copies:
        copy.start()
    for copy in copies:
        copy.wait()


def send_columns(vision, half, targets):
    keys, depth = vision.shape
    pairs = depth // half // (2 * CORES)
    one = jax.ShapeDtypeStruct((keys, pairs * half), vision.dtype)
    count = len(targets)
    return pl.pallas_call(
        functools.partial(send_kernel, half, targets),
        out_shape=[one] * count,
        in_specs=whole(1, pl.ANY),
        out_specs=whole(count),
        scratch_shapes=[pltpu.SemaphoreType.DMA((count, pairs))],
        cost_estimate=pl.CostEstimate(flops=0, bytes_accessed=count * keys * depth, transcendentals=0),
    )(vision)


def prepare_kernel(
    half, text_ref, image_ref, tiles_ref, tenant_ref, page_ref, queries_ref, key_ref, value_ref, vision_ref,
    key_out, value_out, pair_out, diagonal_out, text, image, tiles, tenant, pages, line, sems, column_sems,
):
    start = pl.multiple_of(lax.axis_index("groups") * half, half)
    copies = [
        pltpu.make_async_copy(*pair, sems.at[i])
        for i, pair in enumerate(
            (
                (text_ref, text), (image_ref, image), (tiles_ref, tiles), (tenant_ref, tenant),
                (page_ref, pages), (queries_ref, line),
                (key_ref.at[pl.ds(start, half), :], key_out.at[0:half, :]),
                (value_ref.at[pl.ds(start, half), :], value_out),
            )
        )
    ]
    columns = column_copies(
        half, ((False, True), (True, True)), vision_ref, (pair_out, diagonal_out), column_sems
    )
    for copy in copies + columns:
        copy.start()
    for copy in copies:
        copy.wait()
    width = key_ref.shape[1]
    owner = image[0, 0]
    page = pages[tenant[owner]]
    row = lax.broadcasted_iota(jnp.int32, (EXTRA, width), 0)
    lane = lax.broadcasted_iota(jnp.int32, (EXTRA, width), 1)
    block = jnp.zeros((EXTRA, width), jnp.float32)
    for r in range(queries_ref.shape[1] // width):
        piece = line[0:1, r * width : (r + 1) * width].astype(jnp.float32)
        block = jnp.where(row == r, piece, block)
    for at, number in enumerate((text[0], owner, page, tiles[0])):
        block = jnp.where((row == 8) & (lane == at), number.astype(jnp.float32), block)
    key_out[half : half + EXTRA, :] = block.astype(key_out.dtype)
    for copy in columns:
        copy.wait()


def project_kernel(pieces, spots, images, own, arrays, adds, half, steps, *refs):
    vision_refs = refs[:images]
    weight_refs = refs[images : images + arrays]
    before = refs[images + arrays : images + arrays + adds]
    out_ref, slots, weights, sems = refs[images + arrays + adds :]
    me, y = lax.axis_index("image"), lax.axis_index("groups")
    z, x, core = me // PLANE, me // CORES % COLUMNS, me % CORES
    count = len(pieces)
    weight_copies = []
    image_copies = [[] for _ in range(images)]
    for p, (which, row) in enumerate(pieces):
        weight_copies.append(
            pltpu.make_async_copy(
                weight_refs[which].at[row : row + half, :],
                weights.at[p * half : (p + 1) * half, :],
                sems.at[images, p],
            )
        )
    for i in range(images):
        for p in range(count):
            d, mirrored = spots[p]
            pair = lax.rem(z + d, steps) * COLUMNS + (1 - x if mirrored else x)
            at = pl.multiple_of(((pair * CORES + core) * 2 + y if i == own else pair) * half, half)
            image_copies[i].append(
                pltpu.make_async_copy(
                    vision_refs[i].at[:, pl.ds(at, half)],
                    slots.at[i, :, p * half : (p + 1) * half],
                    sems.at[i, p],
                )
            )
    order = [weight_copies] + image_copies
    for group in order:
        for copy in group:
            copy.start()
    for copy in weight_copies:
        copy.wait()
    for i in range(images):
        for copy in image_copies[i]:
            copy.wait()
        product = jnp.dot(slots[i], weights[...], preferred_element_type=jnp.float32)
        out_ref[i] = before[0][i] + product if adds else product


def project(images, own, arrays, pieces, spots, half, steps, *before):
    keys = images[-1].shape[0]
    width = arrays[0].shape[1]
    count = len(pieces)
    number = len(images)
    return call(
        functools.partial(project_kernel, pieces, spots, number, own, len(arrays), len(before), half, steps),
        jax.ShapeDtypeStruct((number, keys, width), jnp.float32),
        whole(number + len(arrays), pl.ANY) + whole(len(before)),
        scratch=[
            pltpu.VMEM((number, keys, count * half), images[0].dtype),
            pltpu.VMEM((count * half, width), arrays[0].dtype),
            pltpu.SemaphoreType.DMA((number + 1, count)),
        ],
        vmem=16,
        flops=2 * number * keys * half * width * count,
        moved=count * half * (number * keys + width) * 2,
    )(*images, *arrays, *before)


def slot_of(token, me, steps):
    z, x, core = token // PLANE, token // CORES % COLUMNS, token % CORES
    mz, mx, mcore = me // PLANE, me // CORES % COLUMNS, me % CORES
    d = lax.rem(z - mz + steps, steps)
    across = jnp.where(core == mcore, 0, 1) * COLUMNS + jnp.where(x == mx, 0, 1)
    return across * steps + d


def pick_kernel(total, steps, rank, extras_ref, down_ref, out_ref, flat):
    me = lax.axis_index("image")
    flat[...] = down_ref[...].T
    for k in range(total):
        at = pl.multiple_of(slot_of(jnp.bitwise_xor(me, k), me, steps) * EXTRA, EXTRA)
        tile = extras_ref[pl.ds(at, EXTRA), 0:HEAD].astype(jnp.float32)
        page = tile[8, 2].astype(jnp.int32)
        out_ref[k] = flat[pl.ds(pl.multiple_of(page * rank, rank), rank), :]


def own_fact(extras_ref, lane):
    return extras_ref[0:EXTRA, 0:HEAD].astype(jnp.float32)[8, lane].astype(jnp.int32)


def lowrank_kernel(order, extras_ref, vision_ref, down_ref, up_ref, out_ref):
    shards, rank, rows = down_ref.shape
    total = jnp.zeros((vision_ref.shape[0], rank), jnp.float32)
    for j in range(shards):
        shard = jnp.bitwise_xor(lax.axis_index("image"), order[j])
        total = total + lax.dot_general(
            vision_ref[:, pl.ds(pl.multiple_of(shard * rows, rows), rows)],
            down_ref[j],
            (((1,), (1,)), ((), ())),
            preferred_element_type=jnp.float32,
        )
    page = own_fact(extras_ref, 2)
    out_ref[...] = jnp.dot(
        total.astype(jnp.bfloat16), up_ref[page], preferred_element_type=jnp.float32
    )


def window_start(extras_ref, owner, text_total):
    ids = extras_ref[:, 0:HEAD].astype(jnp.float32)
    row = lax.broadcasted_iota(jnp.int32, ids.shape, 0)
    lane = lax.broadcasted_iota(jnp.int32, ids.shape, 1)
    smaller = (row % EXTRA == 8) & (lane == 0) & (ids < owner.astype(jnp.float32))
    first = jnp.sum(jnp.where(smaller, 1.0, 0.0)).astype(jnp.int32)
    return jnp.minimum(first, text_total - WINDOW)


def select_rows(parts, rows):
    head = lax.broadcasted_iota(jnp.int32, parts[0].shape, 0) % 8 // 2
    result = parts[0]
    for k in range(1, KV_HEADS):
        result = jnp.where(head == k, parts[k], result)
    return result


def score_kernel(
    total, steps, mine_ref, core_ref, pair_ref, gain_ref, extras_ref, weights_ref, stats_ref
):
    me, owner = lax.axis_index("image"), own_fact(extras_ref, 1)
    keys = mine_ref.shape[1]
    first = window_start(extras_ref, owner, total)
    tiles = []
    match = []
    for s in range(WINDOW):
        at = pl.multiple_of(slot_of(first + s, me, steps) * EXTRA, EXTRA)
        block = extras_ref[pl.ds(at, EXTRA), :].astype(jnp.float32)
        tiles += [block[0:8, k * HEAD : (k + 1) * HEAD] for k in range(KV_HEADS)]
        match.append(block[8, 0].astype(jnp.int32) == owner)
    query = jnp.concatenate(tiles, axis=0).astype(jnp.bfloat16)
    key_raw = mine_ref[0] + core_ref[...] + pair_ref[...]
    gain = gain_ref[...]
    parts = []
    for k in range(KV_HEADS):
        head = key_raw[:, k * HEAD : (k + 1) * HEAD]
        scale = lax.rsqrt(jnp.mean(head * head, axis=1, keepdims=True) + epsilon)
        block = (head * scale * gain).astype(jnp.bfloat16)
        parts.append(
            lax.dot_general(query, block, (((1,), (1,)), ((), ())), preferred_element_type=jnp.float32)
        )
    scores = select_rows(parts, query.shape[0]) * HEAD ** (-0.5)
    row = lax.broadcasted_iota(jnp.int32, scores.shape, 0) // (8 * KV_HEADS)
    lane = lax.broadcasted_iota(jnp.int32, scores.shape, 1)
    limit = jnp.zeros(scores.shape, jnp.int32)
    slots = own_fact(extras_ref, 3) * (keys // TILES)
    for s in range(WINDOW):
        limit = jnp.where(row == s, jnp.where(match[s], slots, 0), limit)
    usable = lane < limit
    scores = jnp.where(usable, scores, masked_score)
    top = jnp.max(scores, axis=1, keepdims=True)
    weights = jnp.where(usable, jnp.exp(scores - top), 0.0).astype(jnp.bfloat16)
    weights_ref[...] = weights
    sums = jnp.sum(weights.astype(jnp.float32), axis=1, keepdims=True)
    rows = 8 * KV_HEADS
    eye = lax.broadcasted_iota(jnp.int32, (rows, HEAD), 0) == lax.broadcasted_iota(jnp.int32, (rows, HEAD), 1)
    line = lax.broadcasted_iota(jnp.int32, (8, HEAD), 0)
    for s in range(WINDOW):
        own = slice(s * rows, (s + 1) * rows)
        top_row = jnp.sum(jnp.where(eye, top[own], 0.0), axis=0, keepdims=True)
        sum_row = jnp.sum(jnp.where(eye, sums[own], 0.0), axis=0, keepdims=True)
        block = jnp.where(line == 0, top_row, jnp.where(line == 1, sum_row, 0.0))
        block = jnp.where(line == 2, first.astype(jnp.float32), block)
        stats_ref[s] = jnp.where(line == 3, jnp.where(match[s], 1.0, 0.0), block)


def value_kernel(steps, mine_ref, core_ref, pair_ref, lowrank_ref, weights_ref, stats_ref, *refs):
    out_refs, numerators = refs[:-1], refs[-1]
    me, first = lax.axis_index("image"), stats_ref[0][2, 0].astype(jnp.int32)
    value = (mine_ref[0] + core_ref[0] + pair_ref[...] + lowrank_ref[...]).astype(jnp.bfloat16)
    weights = weights_ref[...]
    parts = [
        jnp.dot(weights, value[:, k * HEAD : (k + 1) * HEAD], preferred_element_type=jnp.float32)
        for k in range(KV_HEADS)
    ]
    result = select_rows(parts, weights.shape[0])
    rows = 8 * KV_HEADS
    for s in range(WINDOW):
        numerators[s, 0:rows, :] = result[s * rows : (s + 1) * rows]
        numerators[s, rows:MESSAGE, :] = stats_ref[s]
    match = [stats_ref[s][3, 0] for s in range(WINDOW)]
    line = lax.broadcasted_iota(jnp.int32, (MESSAGE, HEAD), 0)
    empty = jnp.where(line == rows, masked_score, 0.0)
    group = lax.rem(me, PLANE)
    for k, out_ref in enumerate(out_refs):
        core, x = lax.rem(group, CORES), group // CORES
        to = (x if k < CORES else 1 - x) * CORES + (core if k % CORES == 0 else 1 - core)
        for z in range(steps):
            s = z * PLANE + to - first
            inside = (s >= 0) & (s < WINDOW)
            s = jnp.clip(s, 0, WINDOW - 1)
            good = match[0] > 0.5
            for j in range(1, WINDOW):
                good = jnp.where(s == j, match[j], jnp.where(good, 1.0, 0.0)) > 0.5
            good = inside & good
            block = jnp.where(good, numerators[s], empty)
            if k == 0:
                out_ref[z] = block
                continue
            out_ref[z, 0:rows, :] = block[0:rows].astype(jnp.bfloat16)
            thirds = jnp.zeros((NARROW - rows, HEAD), jnp.float32)
            at = lax.broadcasted_iota(jnp.int32, thirds.shape, 0)
            for j in range(2):
                rest = block[rows + j : rows + j + 1]
                for i in range(3):
                    part = rest.astype(jnp.bfloat16).astype(jnp.float32)
                    thirds = jnp.where(at == 3 * j + i, part, thirds)
                    rest = rest - part
            out_ref[z, rows:NARROW, :] = thirds.astype(jnp.bfloat16)


def merge(blocks):
    rows = 8 * KV_HEADS
    tops = [b[rows : rows + 1] for b in blocks]
    top = functools.reduce(jnp.maximum, tops)
    eye = lax.broadcasted_iota(jnp.int32, (rows, HEAD), 0) == lax.broadcasted_iota(jnp.int32, (rows, HEAD), 1)
    numerator, total = 0.0, 0.0
    for b, t in zip(blocks, tops):
        scale = jnp.exp(t - top)
        total = total + scale * b[rows + 1 : rows + 2]
        column = jnp.sum(jnp.where(eye, scale, 0.0), axis=1, keepdims=True)
        numerator = numerator + column * b[0:rows]
    return numerator, top, total, eye


def widen(block):
    rows = 8 * KV_HEADS
    if block.shape[0] == MESSAGE:
        return block
    terms = block[rows:NARROW].astype(jnp.float32)
    line = lax.broadcasted_iota(jnp.int32, (8, HEAD), 0)
    top = terms[0:1] + terms[1:2] + terms[2:3]
    total = terms[3:4] + terms[4:5] + terms[5:6]
    stats = jnp.where(line == 0, top, jnp.where(line == 1, total, 0.0))
    return jnp.concatenate([block[0:rows].astype(jnp.float32), stats], axis=0)


def plane_kernel(steps, *refs):
    in_refs, out_refs, merged = refs[:PLANE], refs[PLANE : PLANE + steps], refs[-1]
    rows = 8 * KV_HEADS
    line = lax.broadcasted_iota(jnp.int32, (8, HEAD), 0)
    for z in range(steps):
        numerator, top, total, _ = merge([widen(ref[z]) for ref in in_refs])
        merged[z, 0:rows, :] = numerator
        merged[z, rows:MESSAGE, :] = jnp.where(line == 0, top, jnp.where(line == 1, total, 0.0))
    for d, out_ref in enumerate(out_refs):
        out_ref[...] = merged[lax.rem(lax.axis_index("image") // PLANE + d, steps)]


def final_kernel(*refs):
    out_ref = refs[-1]
    numerator, top, total, eye = merge([ref[...] for ref in refs[:-1]])
    column = jnp.sum(jnp.where(eye, total, 0.0), axis=1, keepdims=True)
    out = numerator / column
    for k in range(KV_HEADS):
        for r in range(8):
            at = (r * KV_HEADS + k) * HEAD
            out_ref[:, at : at + HEAD] = out[8 * k + r : 8 * k + r + 1].astype(out_ref.dtype)


def local(
    devices,
    vision,
    queries,
    text_request,
    key_weight,
    value_weight,
    key_gain,
    down_pages,
    up_pages,
    image_request,
    image_tiles,
    request_tenant,
    tenant_page,
):
    steps = devices // PLANE
    me = lax.axis_index("image").astype(jnp.int32)
    y = lax.axis_index("groups").astype(jnp.int32)
    z, x, core = me // PLANE, me // CORES % COLUMNS, me % CORES
    tokens = vision[0]
    rows, width = key_weight.shape
    half = rows // 2
    rank = up_pages.shape[1]
    everyone = range(devices)

    def across(value, bits):
        return lax.ppermute(value, "image", [(i, i ^ bits) for i in everyone])

    def along(value, d):
        return lax.ppermute(value, "image", [(i, (i - PLANE * d) % devices) for i in everyone])

    def swap(value, bits=0):
        pairs = [(g * devices + i, (1 - g) * devices + (i ^ bits)) for g in range(2) for i in everyone]
        return lax.ppermute(value, ("groups", "image"), pairs)

    def join(*arrays):
        return jnp.concatenate(arrays, axis=0)

    step = half + EXTRA
    sent = jax.ShapeDtypeStruct((tokens.shape[0], tokens.shape[1] // 4), tokens.dtype)
    key_half, value_half, to_pair, to_diagonal = pl.pallas_call(
        functools.partial(prepare_kernel, half),
        out_shape=[
            jax.ShapeDtypeStruct((step, width), key_weight.dtype),
            jax.ShapeDtypeStruct((half, width), value_weight.dtype),
            sent,
            sent,
        ],
        in_specs=whole(9, pl.ANY),
        out_specs=whole(4),
        scratch_shapes=[
            pltpu.SMEM(text_request.shape, jnp.int32),
            pltpu.SMEM(image_request.shape, jnp.int32),
            pltpu.SMEM(image_tiles.shape, jnp.int32),
            pltpu.SMEM(request_tenant.shape, jnp.int32),
            pltpu.SMEM(tenant_page.shape, jnp.int32),
            pltpu.VMEM(queries.shape, queries.dtype),
            pltpu.SemaphoreType.DMA((8,)),
            pltpu.SemaphoreType.DMA((2, sent.shape[1] // half)),
        ],
    )(
        text_request, image_request, image_tiles, request_tenant, tenant_page, queries, key_weight,
        value_weight, tokens,
    )

    (to_core,) = send_columns(tokens, half, ((True, False),))
    from_pair = swap(to_pair)
    from_diagonal = swap(to_diagonal, 1)
    from_core = across(to_core, 1)

    k1, k3 = along(key_half, 1), along(key_half, 3)
    k_own = across(key_half, CORES)
    k2 = along(after(key_half, k1, k3, k_own), 2)
    kx = across(after(join(k1, k3), k_own), CORES)
    v1, v3 = along(after(value_half, k2, kx, from_core), 1), along(after(value_half, k2, kx, from_core), 3)
    kx2 = across(after(join(k2, value_half), kx), CORES)
    v2 = along(after(value_half, v1, v3), 2)
    vx = across(after(join(v1, v3), kx2), CORES)

    spots = [(d, mirrored) for mirrored in (False, True) for d in (0, 1, 3, 2)]
    near = join(key_half[half:], k1[half:], k2[half:], k3[half:], k_own[half:], kx[half:step], kx2[half:step], kx[step + half :])
    images = [tokens, from_core, from_pair]
    arrays = [key_half, k_own, k1, k3, k2, kx, kx2]
    pieces = ((0, 0), (2, 0), (3, 0), (4, 0), (1, 0), (5, 0), (5, step), (6, 0))
    keys_part = project(images, 0, arrays, pieces, spots, half, steps)
    keys_core = across(keys_part[1], 1)
    late = project([from_diagonal], -1, [after(key_half, keys_part)] + arrays[1:], pieces, spots, half, steps)
    keys_sum = keys_part[2] + across(late[0], 1)
    vx2 = across(after(v2, keys_sum), CORES)
    keys_pair = [swap(keys_sum)]
    extras = join(near, across(after(near, keys_sum), 1))
    picked = call(
        functools.partial(pick_kernel, devices, steps, rank),
        jax.ShapeDtypeStruct((devices, rank, rows), down_pages.dtype),
        whole(2),
        scratch=[pltpu.VMEM(down_pages.shape[::-1], down_pages.dtype)],
    )(after(extras, keys_sum), down_pages)
    picked = picked.reshape(devices, 1, rank, rows)
    order = [0]
    pages = []
    while picked.shape[0] > 1:
        bit = picked.shape[0] // 2
        pages.append(across(picked[bit:], bit))
        picked = jnp.concatenate([picked[:bit], pages[-1]], axis=1)
        order = order + [k ^ bit for k in order]
    picked = picked.reshape(devices, rank, rows)
    lowrank = call(
        functools.partial(lowrank_kernel, tuple(order)),
        jax.ShapeDtypeStruct((tokens.shape[0], width), jnp.float32),
        whole(4),
        vmem=16,
        moved=tokens.size * 2,
    )(extras, tokens, picked, up_pages)

    pieces = ((0, 0), (2, 0), (3, 0), (4, 0), (1, step), (5, 0), (5, half), (6, 0))
    near_values = after(value_half, keys_sum, pages[0])
    images = images + [from_diagonal]
    values_part = project(images, 0, [near_values, kx2, v1, v3, v2, vx], pieces[:-1], spots, half, steps)
    values_part = project(images, 0, [after(vx2, keys_pair[0], pages[1])], ((0, 0),), spots[-1:], half, steps, values_part)
    values_core = across(jnp.stack([values_part[1], values_part[3]]), 1)
    values_sum = (values_part[2] + values_core[1]).astype(jnp.bfloat16)
    values_pair = swap(values_sum)

    heads = WINDOW * 8 * KV_HEADS
    weights, stats = call(
        functools.partial(score_kernel, devices, steps),
        [
            jax.ShapeDtypeStruct((heads, tokens.shape[0]), jnp.bfloat16),
            jax.ShapeDtypeStruct((WINDOW, 8, HEAD), jnp.float32),
        ],
        whole(5),
    )(keys_part, keys_core, *keys_pair, key_gain.reshape(1, HEAD), extras)

    message = jax.ShapeDtypeStruct((steps, MESSAGE, HEAD), jnp.float32)
    narrow = jax.ShapeDtypeStruct((steps, NARROW, HEAD), jnp.bfloat16)
    messages = call(
        functools.partial(value_kernel, steps),
        [message] + [narrow] * (PLANE - 1),
        whole(6),
        scratch=[pltpu.VMEM((WINDOW, MESSAGE, HEAD), jnp.float32)],
    )(values_part, values_core, values_pair, lowrank, weights, stats)
    arrived = [messages[0]] + [across(messages[k], k) for k in range(1, PLANE)]
    one = jax.ShapeDtypeStruct((MESSAGE, HEAD), jnp.float32)
    merged = call(
        functools.partial(plane_kernel, steps),
        [one] * steps,
        whole(PLANE),
        scratch=[pltpu.VMEM((steps, MESSAGE, HEAD), jnp.float32)],
    )(*arrived)
    arrived = [merged[0]] + [along(merged[d], steps - d) for d in range(1, steps)]
    out = call(
        final_kernel,
        jax.ShapeDtypeStruct(queries.shape, jnp.bfloat16),
        whole(steps),
    )(*arrived)
    return out


def fits(mesh, vision, queries, key_weight):
    devices = mesh.shape["image"]
    rows = key_weight.shape[0] // devices
    own = queries.shape[0] // (mesh.shape["groups"] * devices)
    one = vision.shape[0] == mesh.shape["groups"] * devices
    return rows % 256 == 0 and devices == 4 * PLANE and mesh.shape["groups"] == 2 and own == 1 and one


def solution(mesh):
    in_specs = (
        P(("groups", "image"), None, None),
        P(("groups", "image"), None),
        P(("groups", "image")),
        P("image", None),
        P("image", None),
        P(),
        P("image", None),
        P(),
        P(("groups", "image"), None),
        P(("groups", "image")),
        P("groups"),
        P(),
    )
    out_specs = P(("groups", "image"), None)

    def run(*args):
        if fits(mesh, args[0], args[1], args[3]):
            body = functools.partial(local, mesh.shape["image"])
        else:
            body = local_gathered
        return jax.shard_map(body, mesh=mesh, in_specs=in_specs, out_specs=out_specs, check_vma=False)(*args)

    return run
```

```python
import functools

import jax
import jax.numpy as jnp
from jax import lax
from jax.experimental import pallas as pl
from jax.experimental.pallas import tpu as pltpu
from jax.sharding import PartitionSpec as P

HEAD = 128
KV_HEADS = 4
TILES = 4


epsilon = 1e-05
masked_score = -1e30


def select_entry(table, position):
    matches = jnp.arange(table.shape[0], dtype=jnp.int32) == position
    return jnp.sum(jnp.where(matches, table, 0))


def local_gathered(
    vision,
    queries,
    text_request,
    key_weight,
    value_weight,
    key_gain,
    down_pages,
    up_pages,
    image_request,
    image_tiles,
    request_tenant,
    tenant_page,
):
    image_tokens = vision[0]
    key_count = image_tokens.shape[0]
    kv_width = key_weight.shape[1]
    low_rank = up_pages.shape[1]
    owner_id = image_request[0, 0]
    tenant_id = select_entry(request_tenant, owner_id)
    page_id = select_entry(tenant_page, tenant_id)

    def token_columns():
        return image_tokens

    pieces = (
        lax.all_gather(key_weight, "image", axis=0, tiled=True),
        lax.all_gather(value_weight, "image", axis=0, tiled=True),
    )
    columns = token_columns()
    key_raw = jnp.dot(columns, pieces[0], preferred_element_type=jnp.float32)
    value_raw = jnp.dot(columns, pieces[1], preferred_element_type=jnp.float32)
    columns = token_columns()
    lowrank_sum = jnp.dot(
        columns,
        lax.dynamic_slice_in_dim(
            lax.all_gather(down_pages, "image", axis=0, tiled=True), page_id * low_rank, low_rank, 1
        ),
        preferred_element_type=jnp.float32,
    )
    lowrank = lowrank_sum.astype(jnp.bfloat16)
    up_factor = lax.dynamic_index_in_dim(up_pages, page_id, 0, keepdims=False)
    value_block = (
        value_raw + jnp.dot(lowrank, up_factor, preferred_element_type=jnp.float32)
    ).astype(jnp.bfloat16)
    key_heads = key_raw.reshape(key_count, KV_HEADS, HEAD)
    inverse_rms = lax.rsqrt(jnp.mean(key_heads * key_heads, axis=-1, keepdims=True) + epsilon)
    key_block = (
        (key_heads * inverse_rms * key_gain).reshape(key_count, kv_width).astype(jnp.bfloat16)
    )
    every_query, every_request = (
        lax.all_gather(queries, "image", axis=0, tiled=True),
        lax.all_gather(text_request, "image", axis=0, tiled=True),
    )
    text_total = every_query.shape[0]
    own_count = queries.shape[0]
    window = min(4 * own_count, text_total)
    head_group = every_query.shape[1] // kv_width
    q_count = KV_HEADS * head_group
    first_token = jnp.sum((every_request < owner_id).astype(jnp.int32))
    first_token = jnp.minimum(first_token, text_total - window)
    window_query = lax.dynamic_slice_in_dim(every_query, first_token, window, 0)
    window_request = lax.dynamic_slice_in_dim(every_request, first_token, window, 0)
    query_heads = window_query.reshape(window, KV_HEADS, head_group, HEAD)
    positions = jnp.arange(key_count, dtype=jnp.int32)
    usable = (window_request[:, None] == owner_id) & (
        positions[None, :] < image_tiles[0] * (key_count // TILES)
    )
    scores = jnp.einsum(
        "tkgd,vkd->tkgv",
        query_heads,
        key_block.reshape(key_count, KV_HEADS, HEAD),
        preferred_element_type=jnp.float32,
    ) * HEAD ** (-0.5)
    scores = jnp.where(usable[:, None, None, :], scores, masked_score)
    window_max = jnp.max(scores, axis=-1).reshape(window, q_count)
    every_max = lax.dynamic_update_slice_in_dim(
        jnp.full((text_total, q_count), masked_score, jnp.float32), window_max, first_token, 0
    )
    top_score = lax.pmax(every_max, "image")
    window_top = lax.dynamic_slice_in_dim(top_score, first_token, window, 0).reshape(
        window, KV_HEADS, head_group
    )
    weights = jnp.where(
        usable[:, None, None, :], jnp.exp(scores - window_top[..., None]), 0.0
    ).astype(jnp.bfloat16)
    totals = jnp.sum(weights, axis=-1, dtype=jnp.float32).reshape(window, q_count)
    numerator = jnp.einsum(
        "tkgv,vkd->tkgd",
        weights,
        value_block.reshape(key_count, KV_HEADS, HEAD),
        preferred_element_type=jnp.float32,
    ).reshape(window, q_count * HEAD)
    my_first = lax.axis_index("image") * own_count
    own_tokens = my_first + jnp.arange(own_count, dtype=jnp.int32)
    window_slots = jnp.arange(window, dtype=jnp.int32)
    start_value = first_token.astype(jnp.float32).reshape(1)
    pieces = (
        lax.all_gather(numerator, "image", axis=0, tiled=True),
        lax.all_gather(totals, "image", axis=0, tiled=True),
        lax.all_gather(start_value, "image", axis=0, tiled=True),
    )
    piece_count = pieces[2].shape[0]
    starts = pieces[2].astype(jnp.int32)
    offsets = own_tokens[None, :] - starts[:, None]
    chooser = (window_slots[None, None, :] == offsets[:, :, None]).astype(jnp.float32)
    numer_piece = pieces[0].reshape(piece_count, window, -1)
    totals_piece = pieces[1].reshape(piece_count, window, -1)
    numer_own = jnp.einsum("jrw,jwc->rc", chooser, numer_piece, precision=lax.Precision.HIGHEST)
    totals_own = jnp.einsum("jrw,jwc->rc", chooser, totals_piece, precision=lax.Precision.HIGHEST)
    attended = numer_own.reshape(own_count, -1, HEAD) / totals_own[..., None]
    return attended.reshape(own_count, -1).astype(jnp.bfloat16)


CORES = 2
COLUMNS = 2
PLANE = CORES * COLUMNS
EXTRA = 16
WINDOW = 4
MESSAGE = 40
NARROW = 48
IMAGES = 4


def after(value, *others):
    return lax.optimization_barrier((value,) + others)[0]


def whole(count, space=pltpu.VMEM):
    return [pl.BlockSpec(memory_space=space)] * count


def call(kernel, out_shape, in_specs, scratch=(), vmem=16, flops=0, moved=0):
    outs = out_shape if isinstance(out_shape, (list, tuple)) else [out_shape]
    specs = [pl.BlockSpec(memory_space=pltpu.VMEM)] * len(outs)
    return pl.pallas_call(
        kernel,
        out_shape=out_shape,
        in_specs=in_specs,
        out_specs=specs if isinstance(out_shape, (list, tuple)) else specs[0],
        scratch_shapes=list(scratch),
        compiler_params=pltpu.CompilerParams(vmem_limit_bytes=vmem * 2**20),
        cost_estimate=pl.CostEstimate(flops=flops, bytes_accessed=moved, transcendentals=0),
    )


def column_copies(half, targets, vision_ref, out_refs, sems):
    y, core = lax.axis_index("groups"), lax.rem(lax.axis_index("image"), CORES)
    copies = []
    for t, (core_flip, half_flip) in enumerate(targets):
        at_core = 1 - core if core_flip else core
        at_half = 1 - y if half_flip else y
        for p in range(out_refs[t].shape[1] // half):
            at = pl.multiple_of(((p * CORES + at_core) * 2 + at_half) * half, half)
            copies.append(
                pltpu.make_async_copy(
                    vision_ref.at[:, pl.ds(at, half)],
                    out_refs[t].at[:, p * half : (p + 1) * half],
                    sems.at[t, p],
                )
            )
    return copies


def send_kernel(half, targets, vision_ref, *refs):
    copies = column_copies(half, targets, vision_ref, refs[:-1], refs[-1])
    for copy in copies:
        copy.start()
    for copy in copies:
        copy.wait()


def send_columns(vision, half, targets):
    keys, depth = vision.shape
    pairs = depth // half // (2 * CORES)
    one = jax.ShapeDtypeStruct((keys, pairs * half), vision.dtype)
    count = len(targets)
    return pl.pallas_call(
        functools.partial(send_kernel, half, targets),
        out_shape=[one] * count,
        in_specs=whole(1, pl.ANY),
        out_specs=whole(count),
        scratch_shapes=[pltpu.SemaphoreType.DMA((count, pairs))],
        cost_estimate=pl.CostEstimate(flops=0, bytes_accessed=count * keys * depth, transcendentals=0),
    )(vision)


def prepare_kernel(
    half, text_ref, image_ref, tiles_ref, tenant_ref, page_ref, queries_ref, key_ref, value_ref, vision_ref,
    key_out, value_out, pair_out, diagonal_out, text, image, tiles, tenant, pages, line, sems, column_sems,
):
    start = pl.multiple_of(lax.axis_index("groups") * half, half)
    copies = [
        pltpu.make_async_copy(*pair, sems.at[i])
        for i, pair in enumerate(
            (
                (text_ref, text), (image_ref, image), (tiles_ref, tiles), (tenant_ref, tenant),
                (page_ref, pages), (queries_ref, line),
                (key_ref.at[pl.ds(start, half), :], key_out.at[0:half, :]),
                (value_ref.at[pl.ds(start, half), :], value_out),
            )
        )
    ]
    columns = column_copies(
        half, ((False, True), (True, True)), vision_ref, (pair_out, diagonal_out), column_sems
    )
    for copy in copies + columns:
        copy.start()
    for copy in copies:
        copy.wait()
    width = key_ref.shape[1]
    owner = image[0, 0]
    page = pages[tenant[owner]]
    row = lax.broadcasted_iota(jnp.int32, (EXTRA, width), 0)
    lane = lax.broadcasted_iota(jnp.int32, (EXTRA, width), 1)
    block = jnp.zeros((EXTRA, width), jnp.float32)
    for r in range(queries_ref.shape[1] // width):
        piece = line[0:1, r * width : (r + 1) * width].astype(jnp.float32)
        block = jnp.where(row == r, piece, block)
    for at, number in enumerate((text[0], owner, page, tiles[0])):
        block = jnp.where((row == 8) & (lane == at), number.astype(jnp.float32), block)
    key_out[half : half + EXTRA, :] = block.astype(key_out.dtype)
    for copy in columns:
        copy.wait()


def project_kernel(pieces, spots, images, own, arrays, adds, half, steps, *refs):
    vision_refs = refs[:images]
    weight_refs = refs[images : images + arrays]
    before = refs[images + arrays : images + arrays + adds]
    out_ref, slots, weights, sems = refs[images + arrays + adds :]
    me, y = lax.axis_index("image"), lax.axis_index("groups")
    z, x, core = me // PLANE, me // CORES % COLUMNS, me % CORES
    count = len(pieces)
    weight_copies = []
    image_copies = [[] for _ in range(images)]
    for p, (which, row) in enumerate(pieces):
        weight_copies.append(
            pltpu.make_async_copy(
                weight_refs[which].at[row : row + half, :],
                weights.at[p * half : (p + 1) * half, :],
                sems.at[images, p],
            )
        )
    for i in range(images):
        for p in range(count):
            d, mirrored = spots[p]
            pair = lax.rem(z + d, steps) * COLUMNS + (1 - x if mirrored else x)
            at = pl.multiple_of(((pair * CORES + core) * 2 + y if i == own else pair) * half, half)
            image_copies[i].append(
                pltpu.make_async_copy(
                    vision_refs[i].at[:, pl.ds(at, half)],
                    slots.at[i, :, p * half : (p + 1) * half],
                    sems.at[i, p],
                )
            )
    order = [weight_copies] + image_copies
    for group in order:
        for copy in group:
            copy.start()
    for copy in weight_copies:
        copy.wait()
    for i in range(images):
        for copy in image_copies[i]:
            copy.wait()
        product = jnp.dot(slots[i], weights[...], preferred_element_type=jnp.float32)
        out_ref[i] = before[0][i] + product if adds else product


def project(images, own, arrays, pieces, spots, half, steps, *before):
    keys = images[-1].shape[0]
    width = arrays[0].shape[1]
    count = len(pieces)
    number = len(images)
    return call(
        functools.partial(project_kernel, pieces, spots, number, own, len(arrays), len(before), half, steps),
        jax.ShapeDtypeStruct((number, keys, width), jnp.float32),
        [pl.BlockSpec(memory_space=pltpu.HBM if i == own else pl.ANY) for i in range(number)]
        + whole(len(arrays), pl.ANY)
        + whole(len(before)),
        scratch=[
            pltpu.VMEM((number, keys, count * half), images[0].dtype),
            pltpu.VMEM((count * half, width), arrays[0].dtype),
            pltpu.SemaphoreType.DMA((number + 1, count)),
        ],
        vmem=16,
        flops=2 * number * keys * half * width * count,
        moved=count * half * (number * keys + width) * 2,
    )(*images, *arrays, *before)


def slot_of(token, me, steps):
    z, x, core = token // PLANE, token // CORES % COLUMNS, token % CORES
    mz, mx, mcore = me // PLANE, me // CORES % COLUMNS, me % CORES
    d = lax.rem(z - mz + steps, steps)
    across = jnp.where(core == mcore, 0, 1) * COLUMNS + jnp.where(x == mx, 0, 1)
    return across * steps + d


def pick_kernel(total, steps, rank, extras_ref, down_ref, out_ref, flat):
    me = lax.axis_index("image")
    flat[...] = down_ref[...].T
    for k in range(total):
        at = pl.multiple_of(slot_of(jnp.bitwise_xor(me, k), me, steps) * EXTRA, EXTRA)
        tile = extras_ref[pl.ds(at, EXTRA), 0:HEAD].astype(jnp.float32)
        page = tile[8, 2].astype(jnp.int32)
        out_ref[k] = flat[pl.ds(pl.multiple_of(page * rank, rank), rank), :]


def own_fact(extras_ref, lane):
    return extras_ref[0:EXTRA, 0:HEAD].astype(jnp.float32)[8, lane].astype(jnp.int32)


def lowrank_kernel(order, extras_ref, vision_ref, down_ref, up_ref, out_ref):
    shards, rank, rows = down_ref.shape
    total = jnp.zeros((vision_ref.shape[0], rank), jnp.float32)
    for j in range(shards):
        shard = jnp.bitwise_xor(lax.axis_index("image"), order[j])
        total = total + lax.dot_general(
            vision_ref[:, pl.ds(pl.multiple_of(shard * rows, rows), rows)],
            down_ref[j],
            (((1,), (1,)), ((), ())),
            preferred_element_type=jnp.float32,
        )
    page = own_fact(extras_ref, 2)
    out_ref[...] = jnp.dot(
        total.astype(jnp.bfloat16), up_ref[page], preferred_element_type=jnp.float32
    )


def window_start(extras_ref, owner, text_total):
    ids = extras_ref[:, 0:HEAD].astype(jnp.float32)
    row = lax.broadcasted_iota(jnp.int32, ids.shape, 0)
    lane = lax.broadcasted_iota(jnp.int32, ids.shape, 1)
    smaller = (row % EXTRA == 8) & (lane == 0) & (ids < owner.astype(jnp.float32))
    first = jnp.sum(jnp.where(smaller, 1.0, 0.0)).astype(jnp.int32)
    return jnp.minimum(first, text_total - WINDOW)


def select_rows(parts, rows):
    head = lax.broadcasted_iota(jnp.int32, parts[0].shape, 0) % 8 // 2
    result = parts[0]
    for k in range(1, KV_HEADS):
        result = jnp.where(head == k, parts[k], result)
    return result


def score_kernel(
    total, steps, mine_ref, core_ref, pair_ref, gain_ref, extras_ref, weights_ref, stats_ref
):
    me, owner = lax.axis_index("image"), own_fact(extras_ref, 1)
    keys = mine_ref.shape[1]
    first = window_start(extras_ref, owner, total)
    tiles = []
    match = []
    for s in range(WINDOW):
        at = pl.multiple_of(slot_of(first + s, me, steps) * EXTRA, EXTRA)
        block = extras_ref[pl.ds(at, EXTRA), :].astype(jnp.float32)
        tiles += [block[0:8, k * HEAD : (k + 1) * HEAD] for k in range(KV_HEADS)]
        match.append(block[8, 0].astype(jnp.int32) == owner)
    query = jnp.concatenate(tiles, axis=0).astype(jnp.bfloat16)
    key_raw = mine_ref[0] + core_ref[...] + pair_ref[...]
    gain = gain_ref[...]
    parts = []
    for k in range(KV_HEADS):
        head = key_raw[:, k * HEAD : (k + 1) * HEAD]
        scale = lax.rsqrt(jnp.mean(head * head, axis=1, keepdims=True) + epsilon)
        block = (head * scale * gain).astype(jnp.bfloat16)
        parts.append(
            lax.dot_general(query, block, (((1,), (1,)), ((), ())), preferred_element_type=jnp.float32)
        )
    scores = select_rows(parts, query.shape[0]) * HEAD ** (-0.5)
    row = lax.broadcasted_iota(jnp.int32, scores.shape, 0) // (8 * KV_HEADS)
    lane = lax.broadcasted_iota(jnp.int32, scores.shape, 1)
    limit = jnp.zeros(scores.shape, jnp.int32)
    slots = own_fact(extras_ref, 3) * (keys // TILES)
    for s in range(WINDOW):
        limit = jnp.where(row == s, jnp.where(match[s], slots, 0), limit)
    usable = lane < limit
    scores = jnp.where(usable, scores, masked_score)
    top = jnp.max(scores, axis=1, keepdims=True)
    weights = jnp.where(usable, jnp.exp(scores - top), 0.0).astype(jnp.bfloat16)
    weights_ref[...] = weights
    sums = jnp.sum(weights.astype(jnp.float32), axis=1, keepdims=True)
    rows = 8 * KV_HEADS
    eye = lax.broadcasted_iota(jnp.int32, (rows, HEAD), 0) == lax.broadcasted_iota(jnp.int32, (rows, HEAD), 1)
    line = lax.broadcasted_iota(jnp.int32, (8, HEAD), 0)
    for s in range(WINDOW):
        own = slice(s * rows, (s + 1) * rows)
        top_row = jnp.sum(jnp.where(eye, top[own], 0.0), axis=0, keepdims=True)
        sum_row = jnp.sum(jnp.where(eye, sums[own], 0.0), axis=0, keepdims=True)
        block = jnp.where(line == 0, top_row, jnp.where(line == 1, sum_row, 0.0))
        block = jnp.where(line == 2, first.astype(jnp.float32), block)
        stats_ref[s] = jnp.where(line == 3, jnp.where(match[s], 1.0, 0.0), block)


def value_kernel(steps, mine_ref, core_ref, pair_ref, lowrank_ref, weights_ref, stats_ref, *refs):
    out_refs, numerators = refs[:-1], refs[-1]
    me, first = lax.axis_index("image"), stats_ref[0][2, 0].astype(jnp.int32)
    value = (mine_ref[0] + core_ref[0] + pair_ref[...] + lowrank_ref[...]).astype(jnp.bfloat16)
    weights = weights_ref[...]
    parts = [
        jnp.dot(weights, value[:, k * HEAD : (k + 1) * HEAD], preferred_element_type=jnp.float32)
        for k in range(KV_HEADS)
    ]
    result = select_rows(parts, weights.shape[0])
    rows = 8 * KV_HEADS
    for s in range(WINDOW):
        numerators[s, 0:rows, :] = result[s * rows : (s + 1) * rows]
        numerators[s, rows:MESSAGE, :] = stats_ref[s]
    match = [stats_ref[s][3, 0] for s in range(WINDOW)]
    line = lax.broadcasted_iota(jnp.int32, (MESSAGE, HEAD), 0)
    empty = jnp.where(line == rows, masked_score, 0.0)
    group = lax.rem(me, PLANE)
    for k, out_ref in enumerate(out_refs):
        core, x = lax.rem(group, CORES), group // CORES
        to = (x if k < CORES else 1 - x) * CORES + (core if k % CORES == 0 else 1 - core)
        for z in range(steps):
            s = z * PLANE + to - first
            inside = (s >= 0) & (s < WINDOW)
            s = jnp.clip(s, 0, WINDOW - 1)
            good = match[0] > 0.5
            for j in range(1, WINDOW):
                good = jnp.where(s == j, match[j], jnp.where(good, 1.0, 0.0)) > 0.5
            good = inside & good
            block = jnp.where(good, numerators[s], empty)
            if k == 0:
                out_ref[z] = block
                continue
            out_ref[z, 0:rows, :] = block[0:rows].astype(jnp.bfloat16)
            thirds = jnp.zeros((NARROW - rows, HEAD), jnp.float32)
            at = lax.broadcasted_iota(jnp.int32, thirds.shape, 0)
            for j in range(2):
                rest = block[rows + j : rows + j + 1]
                for i in range(3):
                    part = rest.astype(jnp.bfloat16).astype(jnp.float32)
                    thirds = jnp.where(at == 3 * j + i, part, thirds)
                    rest = rest - part
            out_ref[z, rows:NARROW, :] = thirds.astype(jnp.bfloat16)


def merge(blocks):
    rows = 8 * KV_HEADS
    tops = [b[rows : rows + 1] for b in blocks]
    top = functools.reduce(jnp.maximum, tops)
    eye = lax.broadcasted_iota(jnp.int32, (rows, HEAD), 0) == lax.broadcasted_iota(jnp.int32, (rows, HEAD), 1)
    numerator, total = 0.0, 0.0
    for b, t in zip(blocks, tops):
        scale = jnp.exp(t - top)
        total = total + scale * b[rows + 1 : rows + 2]
        column = jnp.sum(jnp.where(eye, scale, 0.0), axis=1, keepdims=True)
        numerator = numerator + column * b[0:rows]
    return numerator, top, total, eye


def widen(block):
    rows = 8 * KV_HEADS
    if block.shape[0] == MESSAGE:
        return block
    terms = block[rows:NARROW].astype(jnp.float32)
    line = lax.broadcasted_iota(jnp.int32, (8, HEAD), 0)
    top = terms[0:1] + terms[1:2] + terms[2:3]
    total = terms[3:4] + terms[4:5] + terms[5:6]
    stats = jnp.where(line == 0, top, jnp.where(line == 1, total, 0.0))
    return jnp.concatenate([block[0:rows].astype(jnp.float32), stats], axis=0)


def plane_kernel(steps, *refs):
    in_refs, out_refs, merged = refs[:PLANE], refs[PLANE : PLANE + steps], refs[-1]
    rows = 8 * KV_HEADS
    line = lax.broadcasted_iota(jnp.int32, (8, HEAD), 0)
    for z in range(steps):
        numerator, top, total, _ = merge([widen(ref[z]) for ref in in_refs])
        merged[z, 0:rows, :] = numerator
        merged[z, rows:MESSAGE, :] = jnp.where(line == 0, top, jnp.where(line == 1, total, 0.0))
    for d, out_ref in enumerate(out_refs):
        out_ref[...] = merged[lax.rem(lax.axis_index("image") // PLANE + d, steps)]


def final_kernel(*refs):
    out_ref = refs[-1]
    numerator, top, total, eye = merge([ref[...] for ref in refs[:-1]])
    column = jnp.sum(jnp.where(eye, total, 0.0), axis=1, keepdims=True)
    out = numerator / column
    for k in range(KV_HEADS):
        for r in range(8):
            at = (r * KV_HEADS + k) * HEAD
            out_ref[:, at : at + HEAD] = out[8 * k + r : 8 * k + r + 1].astype(out_ref.dtype)


def local(
    devices,
    vision,
    queries,
    text_request,
    key_weight,
    value_weight,
    key_gain,
    down_pages,
    up_pages,
    image_request,
    image_tiles,
    request_tenant,
    tenant_page,
):
    steps = devices // PLANE
    me = lax.axis_index("image").astype(jnp.int32)
    y = lax.axis_index("groups").astype(jnp.int32)
    z, x, core = me // PLANE, me // CORES % COLUMNS, me % CORES
    tokens = vision[0]
    rows, width = key_weight.shape
    half = rows // 2
    rank = up_pages.shape[1]
    everyone = range(devices)

    def across(value, bits):
        return lax.ppermute(value, "image", [(i, i ^ bits) for i in everyone])

    def along(value, d):
        return lax.ppermute(value, "image", [(i, (i - PLANE * d) % devices) for i in everyone])

    def swap(value, bits=0):
        pairs = [(g * devices + i, (1 - g) * devices + (i ^ bits)) for g in range(2) for i in everyone]
        return lax.ppermute(value, ("groups", "image"), pairs)

    def join(*arrays):
        return jnp.concatenate(arrays, axis=0)

    step = half + EXTRA
    sent = jax.ShapeDtypeStruct((tokens.shape[0], tokens.shape[1] // 4), tokens.dtype)
    key_half, value_half, to_pair, to_diagonal = pl.pallas_call(
        functools.partial(prepare_kernel, half),
        out_shape=[
            jax.ShapeDtypeStruct((step, width), key_weight.dtype),
            jax.ShapeDtypeStruct((half, width), value_weight.dtype),
            sent,
            sent,
        ],
        in_specs=whole(9, pl.ANY),
        out_specs=whole(4),
        scratch_shapes=[
            pltpu.SMEM(text_request.shape, jnp.int32),
            pltpu.SMEM(image_request.shape, jnp.int32),
            pltpu.SMEM(image_tiles.shape, jnp.int32),
            pltpu.SMEM(request_tenant.shape, jnp.int32),
            pltpu.SMEM(tenant_page.shape, jnp.int32),
            pltpu.VMEM(queries.shape, queries.dtype),
            pltpu.SemaphoreType.DMA((8,)),
            pltpu.SemaphoreType.DMA((2, sent.shape[1] // half)),
        ],
    )(
        text_request, image_request, image_tiles, request_tenant, tenant_page, queries, key_weight,
        value_weight, tokens,
    )

    (to_core,) = send_columns(tokens, half, ((True, False),))
    from_pair = swap(to_pair)
    from_diagonal = swap(to_diagonal, 1)
    from_core = across(to_core, 1)

    k1, k3 = along(key_half, 1), along(key_half, 3)
    k_own = across(key_half, CORES)
    k2 = along(after(key_half, k1, k3, k_own), 2)
    kx = across(after(join(k1, k3), k_own), CORES)
    v1, v3 = along(after(value_half, k2, kx, from_core), 1), along(after(value_half, k2, kx, from_core), 3)
    kx2 = across(after(join(k2, value_half), kx), CORES)
    v2 = along(after(value_half, v1, v3), 2)
    vx = across(after(join(v1, v3), kx2), CORES)

    spots = [(d, mirrored) for mirrored in (False, True) for d in (0, 1, 3, 2)]
    near = join(key_half[half:], k1[half:], k2[half:], k3[half:], k_own[half:], kx[half:step], kx2[half:step], kx[step + half :])
    images = [tokens, from_core, from_pair]
    arrays = [key_half, k_own, k1, k3, k2, kx, kx2]
    pieces = ((0, 0), (2, 0), (3, 0), (4, 0), (1, 0), (5, 0), (5, step), (6, 0))
    keys_part = project(images, 0, arrays, pieces, spots, half, steps)
    keys_core = across(keys_part[1], 1)
    late = project([from_diagonal], -1, [after(key_half, keys_part)] + arrays[1:], pieces, spots, half, steps)
    keys_sum = keys_part[2] + across(late[0], 1)
    vx2 = across(after(v2, keys_sum), CORES)
    keys_pair = [swap(keys_sum)]
    extras = join(near, across(after(near, keys_sum), 1))
    picked = call(
        functools.partial(pick_kernel, devices, steps, rank),
        jax.ShapeDtypeStruct((devices, rank, rows), down_pages.dtype),
        whole(2),
        scratch=[pltpu.VMEM(down_pages.shape[::-1], down_pages.dtype)],
    )(after(extras, keys_sum), down_pages)
    picked = picked.reshape(devices, 1, rank, rows)
    order = [0]
    pages = []
    while picked.shape[0] > 1:
        bit = picked.shape[0] // 2
        pages.append(across(picked[bit:], bit))
        picked = jnp.concatenate([picked[:bit], pages[-1]], axis=1)
        order = order + [k ^ bit for k in order]
    picked = picked.reshape(devices, rank, rows)
    lowrank = call(
        functools.partial(lowrank_kernel, tuple(order)),
        jax.ShapeDtypeStruct((tokens.shape[0], width), jnp.float32),
        whole(4),
        vmem=16,
        moved=tokens.size * 2,
    )(extras, tokens, picked, up_pages)

    pieces = ((0, 0), (2, 0), (3, 0), (4, 0), (1, step), (5, 0), (5, half), (6, 0))
    near_values = after(value_half, keys_sum, pages[0])
    images = images + [from_diagonal]
    values_part = project(images, 0, [near_values, kx2, v1, v3, v2, vx], pieces[:-1], spots, half, steps)
    values_part = project(images, 0, [after(vx2, keys_pair[0], pages[1])], ((0, 0),), spots[-1:], half, steps, values_part)
    values_core = across(jnp.stack([values_part[1], values_part[3]]), 1)
    values_sum = (values_part[2] + values_core[1]).astype(jnp.bfloat16)
    values_pair = swap(values_sum)

    heads = WINDOW * 8 * KV_HEADS
    weights, stats = call(
        functools.partial(score_kernel, devices, steps),
        [
            jax.ShapeDtypeStruct((heads, tokens.shape[0]), jnp.bfloat16),
            jax.ShapeDtypeStruct((WINDOW, 8, HEAD), jnp.float32),
        ],
        whole(5),
    )(keys_part, keys_core, *keys_pair, key_gain.reshape(1, HEAD), extras)

    message = jax.ShapeDtypeStruct((steps, MESSAGE, HEAD), jnp.float32)
    narrow = jax.ShapeDtypeStruct((steps, NARROW, HEAD), jnp.bfloat16)
    messages = call(
        functools.partial(value_kernel, steps),
        [message] + [narrow] * (PLANE - 1),
        whole(6),
        scratch=[pltpu.VMEM((WINDOW, MESSAGE, HEAD), jnp.float32)],
    )(values_part, values_core, values_pair, lowrank, weights, stats)
    arrived = [messages[0]] + [across(messages[k], k) for k in range(1, PLANE)]
    one = jax.ShapeDtypeStruct((MESSAGE, HEAD), jnp.float32)
    merged = call(
        functools.partial(plane_kernel, steps),
        [one] * steps,
        whole(PLANE),
        scratch=[pltpu.VMEM((steps, MESSAGE, HEAD), jnp.float32)],
    )(*arrived)
    arrived = [merged[0]] + [along(merged[d], steps - d) for d in range(1, steps)]
    out = call(
        final_kernel,
        jax.ShapeDtypeStruct(queries.shape, jnp.bfloat16),
        whole(steps),
    )(*arrived)
    return out


def fits(mesh, vision, queries, key_weight):
    devices = mesh.shape["image"]
    rows = key_weight.shape[0] // devices
    own = queries.shape[0] // (mesh.shape["groups"] * devices)
    one = vision.shape[0] == mesh.shape["groups"] * devices
    return rows % 256 == 0 and devices == 4 * PLANE and mesh.shape["groups"] == 2 and own == 1 and one


def solution(mesh):
    in_specs = (
        P(("groups", "image"), None, None),
        P(("groups", "image"), None),
        P(("groups", "image")),
        P("image", None),
        P("image", None),
        P(),
        P("image", None),
        P(),
        P(("groups", "image"), None),
        P(("groups", "image")),
        P("groups"),
        P(),
    )
    out_specs = P(("groups", "image"), None)

    def run(*args):
        if fits(mesh, args[0], args[1], args[3]):
            body = functools.partial(local, mesh.shape["image"])
        else:
            body = local_gathered
        return jax.shard_map(body, mesh=mesh, in_specs=in_specs, out_specs=out_specs, check_vma=False)(*args)

    return run
```
